32 devices in a mesh: dp: 8 (over y, x, core), space: 4 (over z).
Axes of the slice: x: 2, y: 2, z: 4, core: 2. Of those that a mesh axis runs over, the one named last changes fastest.
Arguments:
- clip_maps: bfloat16 [384, 8, 8, 2048], P('dp', 'space'), may hold values from -6 to 6
- next_frame: int32 [384], P('dp'), may hold values from 1 to 383, as said below
- valid_rows: int32 [384, 8], P('dp', 'space'), may hold values from 0 to 1, as said below
- proj_in: bfloat16 [2, 2048, 512], replicated, may hold values from -0.125 to 0.125
- conv_mid: bfloat16 [2, 4608, 512], replicated, may hold values from -0.09375 to 0.09375
- proj_out: bfloat16 [2, 512, 2048], replicated, may hold values from -0.25 to 0.25
- gate_reduce: bfloat16 [2, 2048, 128], replicated, may hold values from -0.125 to 0.125
- gate_convs: bfloat16 [2, 3, 1152, 128], replicated, may hold values from -0.1875 to 0.1875
- gate_expand: bfloat16 [2, 128, 2048], replicated, may hold values from -0.5 to 0.5
- norm_gain: float32 [2, 3072], replicated, may hold values from 0.5 to 1.5
- norm_bias: float32 [2, 3072], replicated, may hold values from -1.5 to 1.5
- out_grad: bfloat16 [384, 8, 8, 2048], P('dp', 'space'), may hold values from -6 to 6
Outputs:
- out_maps: bfloat16 [384, 8, 8, 2048], P('dp', 'space')
- grad_maps: bfloat16 [384, 8, 8, 2048], P('dp', 'space')
- grad_proj_in: float32 [2, 2048, 512], P(None, 'dp')
- grad_conv_mid: float32 [2, 4608, 512], P(None, 'dp')
- grad_proj_out: float32 [2, 512, 2048], P(None, 'dp')
- grad_gate_reduce: float32 [2, 2048, 128], P(None, 'dp')
- grad_gate_convs: float32 [2, 3, 1152, 128], replicated
- grad_gate_expand: float32 [2, 128, 2048], replicated
- grad_norm_gain: float32 [2, 3072], replicated
- grad_norm_bias: float32 [2, 3072], replicated
The draws below stay inside these ranges and needn't reach their ends.
Inputs may be any that keep to these rules, and one draw needn't show every extreme that they name: `next_frame`: for each frame, the index of the next segment's frame of its clip, or its own index for a clip's last segment. Clips are runs of 8 or 16 consecutive frames starting at a multiple of their length and lie inside one block of 48 frames. `valid_rows`: 1 on the first rows of a frame and 0 below; the frames of one clip share the same count of such rows, 4 to 8; in every block of 48 frames some clip has all 8 rows.
All inputs are finite; a program needn't handle non-finite values.
Results may differ from the reference program's by a relative error of at most 0.023.
Values may be sent and summed in bfloat16 or wider, within the bound.
No kernel may reach another device: no remote copies, remote signals or barrier semaphores. Data moves between devices by JAX's collectives and lax.ppermute only.
A program may use at most 320 MiB of HBM per device.

```python
import jax
import jax.numpy as jnp
from jax import lax

C = 2048
MID = 512
RED = 128
HGT = 8
WID = 8
FR_DEV = 48
FRAMES = 384


def clip_shape(key):
    pair_count = FRAMES // 16
    long_pairs = jax.random.randint(key, (pair_count,), 0, 2)
    frame_ids = jnp.arange(FRAMES, dtype=jnp.int32)
    in_pair = frame_ids % 16
    long_frame = jnp.repeat(long_pairs, 16)
    clip_size = jnp.where(long_frame == 1, 16, 8)
    position = jnp.where(long_frame == 1, in_pair, in_pair % 8)
    return (frame_ids, clip_size, position)


def draw_next_frame(key, part):
    frame_ids, clip_size, position = clip_shape(key)
    return jnp.where(position == clip_size - 1, frame_ids, frame_ids + 1).astype(jnp.int32)


def draw_valid_rows(key, part):
    frame_ids, clip_size, position = clip_shape(key)
    key = jax.random.fold_in(key, 5)
    height_key, pick_key = jax.random.split(key)
    clip_first = frame_ids - position
    heights = jax.random.randint(height_key, (FRAMES,), HGT // 2, HGT + 1)
    clip_height = heights[clip_first]
    block_count = FRAMES // FR_DEV
    picks = jax.random.randint(pick_key, (block_count,), 0, FR_DEV) + jnp.arange(block_count, dtype=jnp.int32) * FR_DEV
    chosen_first = picks - position[picks]
    block_of = frame_ids // FR_DEV
    full_clip = clip_first == chosen_first[block_of]
    clip_height = jnp.where(full_clip, HGT, clip_height)
    row_ids = jnp.arange(HGT, dtype=jnp.int32)
    return (row_ids[None, :] < clip_height[:, None]).astype(jnp.int32)


def block_scale(own_key, dims, cuts, least, largest):
    def one(axis_at, blocks):
        steps = jax.random.uniform(jax.random.fold_in(jax.random.fold_in(own_key, 6), axis_at), (blocks,), jnp.float32, least / len(cuts), largest / len(cuts))
        return jnp.repeat(jnp.exp(steps), dims[axis_at] // blocks).reshape((-1,) + (1,) * (len(dims) - axis_at - 1))

    level = one(*cuts[0])
    for cut in cuts[1:]:
        level = level * one(*cut)
    return level


def centred(stream_key, shape, deviation, bound, cuts=(), kind=jnp.bfloat16):
    entries = jax.random.normal(stream_key, shape, jnp.float32) * deviation
    if len(cuts) > 0:
        entries = block_scale(stream_key, shape, cuts, -0.22, 0.18) * entries
    return jnp.clip(entries, min=-bound, max=bound).astype(kind)


def setup_inputs(seed: int = 0) -> dict:
    key_list = jax.random.split(jax.random.key(seed), 13)
    return {
        "clip_maps": centred(key_list[0], (FRAMES, HGT, WID, C), 1.0, 6.0, ((0, 8), (1, 4))),
        "next_frame": draw_next_frame(jax.random.fold_in(key_list[12], 71), 0),
        "valid_rows": draw_valid_rows(jax.random.fold_in(key_list[12], 71), 0),
        "proj_in": centred(key_list[3], (2, C, MID), C ** -0.5, 0.125),
        "conv_mid": centred(key_list[4], (2, 9 * MID, MID), (9 * MID) ** -0.5, 0.09375),
        "proj_out": centred(key_list[5], (2, MID, C), MID ** -0.5, 0.25),
        "gate_reduce": centred(key_list[6], (2, C, RED), C ** -0.5, 0.125),
        "gate_convs": centred(key_list[7], (2, 3, 9 * RED, RED), (9 * RED) ** -0.5, 0.1875),
        "gate_expand": centred(key_list[8], (2, RED, C), RED ** -0.5, 0.5),
        "norm_gain": jnp.clip(1.0 + 0.1 * jax.random.normal(key_list[9], (2, 2 * MID + C), jnp.float32), 0.5, 1.5),
        "norm_bias": centred(key_list[10], (2, 2 * MID + C), 0.3, 1.5, (), jnp.float32),
        "out_grad": centred(key_list[11], (FRAMES, HGT, WID, C), 1.0, 6.0, ((0, 8), (1, 4))),
    }


norm_eps = 1e-05
highest = lax.Precision.HIGHEST

@jax.custom_vjp
def low(v):
    return lax.optimization_barrier(v.astype(jnp.bfloat16)).astype(jnp.float32)

@jax.custom_vjp
def low_back(v):
    return v

def low_keep(v):
    return (low(v), None)

def low_pass(kept, grad):
    return (grad,)

def back_keep(v):
    return (v, None)

def back_low(kept, grad):
    return (low(grad),)
low.defvjp(low_keep, low_pass)
low_back.defvjp(back_keep, back_low)

def channel_product(values, weight):
    return jnp.einsum('fhwc,cd->fhwd', values, weight, precision=highest)

def conv_three(values, weight):
    channels_in = values.shape[3]
    height = values.shape[1]
    map_width = values.shape[2]
    padded = jnp.pad(values, ((0, 0), (1, 1), (1, 1), (0, 0)))
    running = jnp.zeros(values.shape[:3] + (weight.shape[1],), jnp.float32)
    for tap_row in range(3):
        for tap_col in range(3):
            tap_index = tap_row * 3 + tap_col
            window = padded[:, tap_row:tap_row + height, tap_col:tap_col + map_width, :]
            running = running + channel_product(window, weight[tap_index * channels_in:(tap_index + 1) * channels_in])
    return running

def pool_map(values, factor):
    frames, height, map_width, channels = values.shape
    shaped = values.reshape(frames, height // factor, factor, map_width // factor, factor, channels)
    return lax.optimization_barrier(jnp.mean(shaped, axis=(2, 4)))

def expand_map(values, factor):
    return jnp.repeat(jnp.repeat(values, factor, axis=1), factor, axis=2)

def normalize_then_activate(values, mask_maps, gain_part, bias_part, apply_activation):
    pixel_total = jnp.sum(mask_maps) * values.shape[2]
    masked = values * mask_maps
    mean_value = lax.optimization_barrier(jnp.sum(masked, axis=(0, 1, 2))) / pixel_total
    mean_square = lax.optimization_barrier(jnp.sum(masked * values, axis=(0, 1, 2))) / pixel_total
    variance = mean_square - mean_value * mean_value
    normed = (values - mean_value) * lax.rsqrt(variance + norm_eps) * gain_part + bias_part
    if apply_activation:
        return jax.nn.silu(normed) * mask_maps
    return normed

def block(maps, w_in, w_mid, w_out, w_reduce, w_convs, w_expand, gains, biases, mask_maps, next_frame):
    middle = w_in.shape[1]
    low_in = low(maps)
    first = low_back(channel_product(low_in, w_in))
    hidden_one = low(normalize_then_activate(first, mask_maps, gains[:middle], biases[:middle], True))
    second = low_back(conv_three(hidden_one, w_mid))
    hidden_two = low(normalize_then_activate(second, mask_maps, gains[middle:2 * middle], biases[middle:2 * middle], True))
    third = low_back(channel_product(hidden_two, w_out))
    branch = normalize_then_activate(third, mask_maps, gains[2 * middle:], biases[2 * middle:], False)
    reduce_rows = low(low_back(channel_product(low_in, w_reduce))) * mask_maps
    shifted = jnp.take(reduce_rows, next_frame, axis=0)
    difference = low_back(conv_three(shifted, w_convs[0])) - reduce_rows
    coarse_two = low(pool_map(difference, 2))
    coarse_four = low(pool_map(difference, 4))
    conv_two = low_back(conv_three(coarse_two, w_convs[1]))
    conv_four = low_back(conv_three(coarse_four, w_convs[2]))
    summed = difference + expand_map(conv_two, 2) + expand_map(conv_four, 4)
    gate_pre = low_back(channel_product(low(summed), w_expand))
    return jax.nn.silu(maps + branch * jax.nn.sigmoid(gate_pre)) * mask_maps

def reference(clip_maps, next_frame, valid_rows, proj_in, conv_mid, proj_out, gate_reduce, gate_convs, gate_expand, norm_gain, norm_bias, out_grad):
    mask_maps = valid_rows.astype(jnp.float32)[:, :, None, None]

    def layer_step(maps, w_in, w_mid, w_out, w_reduce, w_convs, w_expand, gains, biases):
        return block(maps, w_in, w_mid, w_out, w_reduce, w_convs, w_expand, gains, biases, mask_maps, next_frame)
    checked = jax.checkpoint(layer_step)

    def forward(maps, w_in, w_mid, w_out, w_reduce, w_convs, w_expand, gains, biases):
        current = maps * mask_maps
        for layer_index in range(2):
            current = checked(current, w_in[layer_index], w_mid[layer_index], w_out[layer_index], w_reduce[layer_index], w_convs[layer_index], w_expand[layer_index], gains[layer_index], biases[layer_index])
        return current
    result, pullback = jax.vjp(forward, clip_maps.astype(jnp.float32), proj_in.astype(jnp.float32), conv_mid.astype(jnp.float32), proj_out.astype(jnp.float32), gate_reduce.astype(jnp.float32), gate_convs.astype(jnp.float32), gate_expand.astype(jnp.float32), norm_gain.astype(jnp.float32), norm_bias.astype(jnp.float32))
    gradients = pullback(out_grad.astype(jnp.float32))
    return (result.astype(jnp.bfloat16), gradients[0].astype(jnp.bfloat16), gradients[1], gradients[2], gradients[3], gradients[4], gradients[5], gradients[6], gradients[7], gradients[8])
```

```python
import jax
import jax.numpy as jnp
from jax import lax
from jax.sharding import PartitionSpec as P

norm_eps = 1e-05
both = ("dp", "space")
f32 = jnp.float32
bf16 = jnp.bfloat16


def mm(left, right):
    return jnp.dot(left, right, preferred_element_type=f32)


def mm_inner(left, right):
    return lax.dot_general(left, right, (((0,), (0,)), ((), ())), preferred_element_type=f32)


def mm_back(left, right):
    return lax.dot_general(left, right, (((1,), (1,)), ((), ())), preferred_element_type=f32)


def all_sum(block):
    count = lax.axis_size("dp") * lax.axis_size("space")
    spread = jnp.broadcast_to(block[None], (count,) + block.shape)
    return jnp.sum(lax.all_to_all(spread, both, 0, 0), axis=0)


def sum_pair(first, second):
    width = first.shape[0]
    packed = all_sum(jnp.concatenate([first, second]).reshape(-1, 128)).reshape(2, width)
    return packed[0], packed[1]


def halo_rows(block):
    count = lax.axis_size("space")
    forward = [(i, i + 1) for i in range(count - 1)]
    backward = [(i + 1, i) for i in range(count - 1)]
    rows = block.shape[1]
    low = lax.ppermute(block[:, rows - 1 : rows], "space", forward)
    high = lax.ppermute(block[:, :1], "space", backward)
    return low, high


def tap_stack(padded, num_rows, num_cols, flipped):
    windows = []
    for tap_row in range(3):
        for tap_col in range(3):
            first_row = 2 - tap_row if flipped else tap_row
            first_col = 2 - tap_col if flipped else tap_col
            windows.append(
                padded[:, first_row : first_row + num_rows, first_col : first_col + num_cols, :]
            )
    stacked = jnp.concatenate(windows, axis=-1)
    return stacked.reshape(-1, stacked.shape[-1])


def pad_columns(values):
    return jnp.pad(values, ((0, 0), (0, 0), (1, 1), (0, 0)))


def full_taps(values, flipped):
    padded = jnp.pad(values, ((0, 0), (1, 1), (1, 1), (0, 0)))
    return tap_stack(padded, values.shape[1], values.shape[2], flipped)


def flip_weight(weight, channels_in):
    tap_blocks = weight.reshape(9, channels_in, -1)
    return jnp.swapaxes(tap_blocks, 1, 2).reshape(-1, channels_in)


def pool_map(values, factor):
    frames, height, map_width, channels = values.shape
    shaped = values.reshape(frames, height // factor, factor, map_width // factor, factor, channels)
    return jnp.mean(shaped, axis=(2, 4))


def expand_map(values, factor):
    return jnp.repeat(jnp.repeat(values, factor, axis=1), factor, axis=2)


def norm_scale(sum_values, sum_squares, total, gain, bias):
    mean = sum_values / total
    variance = sum_squares / total - mean * mean
    inverse = lax.rsqrt(variance + norm_eps)
    scale = inverse * gain
    return mean, inverse, scale, bias - mean * scale


def back_terms(sums, total, mean, inverse, scale):
    sum_bias, sum_gain = sums
    factor = -scale / total
    return factor * (sum_bias - inverse * sum_gain * mean), factor * inverse * sum_gain


def silu_slope(value):
    sig = jax.nn.sigmoid(value)
    return sig * (1.0 + value * (1.0 - sig))


group_size = 16


def to_frames(own_rows):
    space = lax.axis_size("space")
    frames, rows, cols, channels = own_rows.shape
    padded = jnp.pad(own_rows, ((0, space * group_size - frames), (0, 0), (0, 0), (0, 0))) if space * group_size > frames else own_rows
    return lax.all_to_all(padded, "space", 0, 1, tiled=True)


def to_rows(full_rows, frames):
    return lax.all_to_all(full_rows, "space", 1, 0, tiled=True)[:frames]


def gate_forward(reduce_rows, next_group, convs_layer):
    reduced = reduce_rows.shape[3]
    shifted = jnp.take(reduce_rows, next_group, axis=0)
    diff_taps = full_taps(shifted, False)
    difference = mm(diff_taps, convs_layer[0]).reshape(reduce_rows.shape) - reduce_rows.astype(f32)
    coarse_two = pool_map(difference, 2).astype(bf16)
    coarse_four = pool_map(difference, 4).astype(bf16)
    two_taps = full_taps(coarse_two, False)
    four_taps = full_taps(coarse_four, False)
    conv_two = mm(two_taps, convs_layer[1]).reshape(coarse_two.shape)
    conv_four = mm(four_taps, convs_layer[2]).reshape(coarse_four.shape)
    summed = difference + expand_map(conv_two, 2) + expand_map(conv_four, 4)
    return summed.astype(bf16), (diff_taps, two_taps, four_taps)


def gate_backward(grad_low, gate_kept, convs_layer, next_group):
    diff_taps, two_taps, four_taps = gate_kept
    reduced = grad_low.shape[3]
    grad_summed = grad_low.astype(f32)
    grad_two = (pool_map(grad_summed, 2) * 4.0).astype(bf16)
    grad_four = (pool_map(grad_summed, 4) * 16.0).astype(bf16)
    weight_two = mm_inner(two_taps, grad_two.reshape(-1, reduced))
    weight_four = mm_inner(four_taps, grad_four.reshape(-1, reduced))
    back_two = mm(full_taps(grad_two, True), flip_weight(convs_layer[1], reduced)).reshape(
        grad_two.shape
    )
    back_four = mm(full_taps(grad_four, True), flip_weight(convs_layer[2], reduced)).reshape(
        grad_four.shape
    )
    grad_diff = grad_summed + expand_map(back_two, 2) / 4.0 + expand_map(back_four, 4) / 16.0
    grad_diff_low = grad_diff.astype(bf16)
    weight_diff = mm_inner(diff_taps, grad_diff_low.reshape(-1, reduced))
    back_shift = mm(full_taps(grad_diff_low, True), flip_weight(convs_layer[0], reduced)).reshape(
        grad_low.shape
    )
    chosen = (next_group[None, :] == jnp.arange(group_size)[:, None]).astype(f32)
    grad_rows = jnp.einsum("ef,fhwc->ehwc", chosen, back_shift) - grad_diff
    return grad_rows.astype(bf16), jnp.stack([weight_diff, weight_two, weight_four], axis=0)


def halve(parts, axis_name, bit):
    index = lax.axis_index(axis_name)
    count = lax.axis_size(axis_name)
    mine = (index // bit) % 2
    kept = lax.dynamic_index_in_dim(parts, mine, 0, keepdims=False)
    sent = lax.dynamic_index_in_dim(parts, 1 - mine, 0, keepdims=False)
    got = lax.ppermute(sent, axis_name, [(i, i ^ bit) for i in range(count)])
    return (kept.astype(f32) + got.astype(f32)).astype(bf16)


def chain_sum(own):
    count = lax.axis_size("space")
    index = lax.axis_index("space")
    low = jnp.zeros_like(own)
    high = jnp.zeros_like(own)
    total_low = own
    total_high = own
    for step in range(1, count):
        got_low = lax.ppermute(total_low, "space", [(step - 1, step)])
        got_high = lax.ppermute(total_high, "space", [(count - step, count - step - 1)])
        low = low + got_low
        high = high + got_high
        total_low = (own.astype(f32) + low.astype(f32)).astype(bf16)
        total_high = (own.astype(f32) + high.astype(f32)).astype(bf16)
    return own.astype(f32) + low.astype(f32) + high.astype(f32)


def reduce_fast(grad):
    count = lax.axis_size("dp")
    bits = []
    bit = 2
    while bit < count:
        bits.append(bit)
        bit *= 2
    rows, cols = grad.shape[1:]
    order = [1] + bits
    view = grad.reshape((2,) * len(order) + (rows, cols))

    def along(parts, current, chosen):
        at = len(current) - 1 - current.index(chosen)
        return jnp.moveaxis(parts, at, 0), [b for b in current if b != chosen]

    parts, current = along(view, order, 1)
    parts = halve(parts, "dp", 1)
    outs = []
    half = len(bits) // 2
    for which, sequence in enumerate((bits, bits[half:] + bits[:half])):
        piece = parts[..., which * (rows // 2) : (which + 1) * (rows // 2), :]
        left = current
        for chosen in sequence:
            piece, left = along(piece, left, chosen)
            piece = halve(piece, "dp", chosen)
        outs.append(chain_sum(piece))
    return jnp.concatenate(outs, axis=0)


def reduce_slow(grad):
    part = lax.psum_scatter(grad, "dp", scatter_dimension=0, tiled=False)
    return lax.psum(part, "space").astype(f32)


def chunks(grad):
    count = lax.axis_size("dp")
    return grad.astype(bf16).reshape(count, -1, 512)


def body(
    clip_maps,
    next_frame,
    valid_rows,
    proj_in,
    conv_mid,
    proj_out,
    gate_reduce,
    gate_convs,
    gate_expand,
    norm_gain,
    norm_bias,
    out_grad,
):
    frames, rows_dev, map_width, channels = clip_maps.shape
    middle = proj_in.shape[2]
    reduced = gate_reduce.shape[2]
    mask_maps = valid_rows.astype(f32)[:, :, None, None]
    mask_rows = jnp.broadcast_to(mask_maps, (frames, rows_dev, map_width, 1)).reshape(-1, 1)
    mask_low, mask_high = halo_rows(mask_maps)
    group_base = lax.axis_index("dp") * frames + lax.axis_index("space") * group_size
    padded_next = jnp.pad(next_frame, (0, lax.axis_size("space") * group_size - frames))
    own_next = lax.dynamic_slice_in_dim(
        padded_next, lax.axis_index("space") * group_size, group_size
    )
    next_group = jnp.clip(own_next - group_base, 0, group_size - 1)
    flat = (-1, middle)
    maps4 = (frames, rows_dev, map_width, middle)

    def forward(layer, values, low_in, total):
        gains, biases = norm_gain[layer], norm_bias[layer]
        first = mm(low_in, proj_in[layer])
        reduce_rows = mm(low_in, gate_reduce[layer]).astype(bf16).reshape(
            frames, rows_dev, map_width, reduced
        ) * mask_maps.astype(bf16)
        first_low, first_high = halo_rows(first.astype(bf16).reshape(maps4))
        own_sum, own_square = jnp.sum(first, axis=0), jnp.sum(first * first, axis=0)
        if total is None:
            packed = jnp.concatenate(
                [own_sum, own_square, jnp.full((128,), jnp.sum(mask_rows))]
            ).reshape(-1, 128)
            packed = all_sum(packed).reshape(-1)
            sums_one = packed[:middle], packed[middle : 2 * middle]
            total = packed[2 * middle]
        else:
            sums_one = sum_pair(own_sum, own_square)
        full_rows = to_frames(reduce_rows)
        gate_full, gate_kept = gate_forward(full_rows, next_group, gate_convs[layer])
        gate_own = to_rows(gate_full, frames).reshape(-1, reduced)
        norm_one = norm_scale(*sums_one, total, gains[:middle], biases[:middle])

        def activate(block, scales, mask):
            return (jax.nn.silu(block * scales[2] + scales[3]) * mask).astype(bf16)

        hidden_one = jnp.concatenate(
            [
                activate(first_low.astype(f32), norm_one, mask_low),
                activate(first.reshape(maps4), norm_one, mask_maps),
                activate(first_high.astype(f32), norm_one, mask_high),
            ],
            axis=1,
        )
        mid_taps = tap_stack(pad_columns(hidden_one), rows_dev, map_width, False)
        second = mm(mid_taps, conv_mid[layer])
        masked = second * mask_rows
        sums_two = sum_pair(jnp.sum(masked, axis=0), jnp.sum(masked * second, axis=0))
        norm_two = norm_scale(
            *sums_two, total, gains[middle : 2 * middle], biases[middle : 2 * middle]
        )
        hidden_two = activate(second, norm_two, mask_rows)
        third = mm(hidden_two, proj_out[layer])
        sums_three = sum_pair(jnp.sum(third, axis=0), jnp.sum(third * third, axis=0))
        norm_three = norm_scale(*sums_three, total, gains[2 * middle :], biases[2 * middle :])
        second_halo = halo_rows(second.astype(bf16).reshape(maps4))
        branch = third * norm_three[2] + norm_three[3]
        gate_sig = jax.nn.sigmoid(mm(gate_own, gate_expand[layer]))
        summed = values + branch * gate_sig
        out = jax.nn.silu(summed) * mask_rows
        kept = (
            low_in,
            first,
            norm_one,
            mid_taps,
            second,
            second_halo,
            norm_two,
            hidden_two,
            third,
            norm_three,
            gate_own,
            gate_kept,
            summed,
            branch,
            gate_sig,
        )
        return out, kept, total

    def backward(layer, kept, grad_out, total):
        (
            low_in,
            first,
            norm_one,
            mid_taps,
            second,
            second_halo,
            norm_two,
            hidden_two,
            third,
            norm_three,
            gate_own,
            gate_kept,
            summed,
            branch,
            gate_sig,
        ) = kept
        grad_in = grad_out * mask_rows * silu_slope(summed)
        grad_branch = grad_in * gate_sig
        grad_pre = (grad_branch * branch * (1.0 - gate_sig)).astype(bf16)
        sums_three = sum_pair(
            jnp.sum(grad_branch, axis=0),
            jnp.sum(grad_branch * ((third - norm_three[0]) * norm_three[1]), axis=0),
        )
        grad_gate = to_frames(
            mm_back(grad_pre, gate_expand[layer])
            .astype(bf16)
            .reshape(frames, rows_dev, map_width, reduced)
        )
        grad_rows, grad_convs = gate_backward(grad_gate, gate_kept, gate_convs[layer], next_group)
        grad_rows = (to_rows(grad_rows, frames) * mask_maps.astype(bf16)).reshape(-1, reduced)
        grad_expand = mm_inner(gate_own, grad_pre)
        grad_reduce = mm_inner(low_in, grad_rows)

        def spread(grad, values, scales, terms, mask):
            return (grad + mask * (terms[0] + terms[1] * values)).astype(bf16)

        terms = back_terms(sums_three, total, *norm_three[:3])
        grad_third = spread(grad_branch * norm_three[2], third, norm_three, terms, mask_rows)
        grad_out_w = mm_inner(hidden_two, grad_third)
        grad_norm = mm_back(grad_third, proj_out[layer]) * (
            silu_slope(second * norm_two[2] + norm_two[3]) * mask_rows
        )
        part_two = grad_norm * norm_two[2]
        part_low, part_high = halo_rows(part_two.astype(bf16).reshape(maps4))
        sums_two = sum_pair(
            jnp.sum(grad_norm, axis=0),
            jnp.sum(grad_norm * ((second - norm_two[0]) * norm_two[1]), axis=0),
        )
        terms = back_terms(sums_two, total, *norm_two[:3])
        grad_second = spread(part_two, second, norm_two, terms, mask_rows)
        grad_ext = jnp.concatenate(
            [
                spread(part_low.astype(f32), second_halo[0].astype(f32), norm_two, terms, mask_low),
                grad_second.reshape(maps4),
                spread(
                    part_high.astype(f32), second_halo[1].astype(f32), norm_two, terms, mask_high
                ),
            ],
            axis=1,
        )
        grad_norm = mm(
            tap_stack(pad_columns(grad_ext), rows_dev, map_width, True),
            flip_weight(conv_mid[layer], middle),
        ) * (silu_slope(first * norm_one[2] + norm_one[3]) * mask_rows)
        sums_one = sum_pair(
            jnp.sum(grad_norm, axis=0),
            jnp.sum(grad_norm * ((first - norm_one[0]) * norm_one[1]), axis=0),
        )
        grad_conv = mm_inner(mid_taps, grad_second)
        terms = back_terms(sums_one, total, *norm_one[:3])
        grad_first = spread(grad_norm * norm_one[2], first, norm_one, terms, mask_rows)
        grad_proj = mm_inner(low_in, grad_first)
        grad_in = (
            grad_in
            + mm_back(grad_first, proj_in[layer])
            + mm_back(grad_rows, gate_reduce[layer])
        )
        large = (grad_proj, grad_conv, grad_out_w, grad_reduce)
        small = (
            grad_convs,
            grad_expand,
            jnp.concatenate([sums_one[1], sums_two[1], sums_three[1]]),
            jnp.concatenate([sums_one[0], sums_two[0], sums_three[0]]),
        )
        return grad_in, large, small

    start = clip_maps.astype(f32).reshape(-1, channels) * mask_rows
    mid_out, kept_zero, total_rows = forward(0, start, start.astype(bf16), None)
    total = total_rows * 1.0
    final, kept_one, total = forward(1, mid_out, mid_out.astype(bf16), total)
    final_maps = final.astype(bf16).reshape(clip_maps.shape)
    grad = out_grad.astype(f32).reshape(-1, channels)
    grad, large_one, small_one = backward(1, kept_one, grad, total)
    sum_one = reduce_slow(jnp.concatenate([chunks(g) for g in large_one], axis=1))
    grad, large_zero, small_zero = backward(0, kept_zero, grad, total)
    sum_zero = jnp.concatenate(
        [
            reduce_fast(jnp.concatenate([chunks(g) for g in large_zero[:2]], axis=1)),
            reduce_slow(jnp.concatenate([chunks(g) for g in large_zero[2:]], axis=1)),
        ],
        axis=0,
    )
    grad_maps = (grad * mask_rows).astype(bf16).reshape(clip_maps.shape)

    def unpack(position):
        pieces = []
        for summed, large in ((sum_zero, large_zero), (sum_one, large_one)):
            offset = 0
            for at in range(position):
                offset += large[at].size // (lax.axis_size("dp") * 512)
            size = large[position].size // (lax.axis_size("dp") * 512)
            pieces.append(summed[offset : offset + size].reshape(-1, large[position].shape[1]))
        return jnp.stack(pieces)

    convs, expand = lax.psum(
        (
            jnp.stack([small_zero[0], small_one[0]]).astype(bf16),
            jnp.stack([small_zero[1], small_one[1]]).astype(bf16),
        ),
        both,
    )
    return (
        final_maps,
        grad_maps,
        unpack(0),
        unpack(1),
        unpack(2),
        unpack(3),
        convs.astype(f32),
        expand.astype(f32),
        jnp.stack([small_zero[2], small_one[2]]),
        jnp.stack([small_zero[3], small_one[3]]),
    )


def solution(mesh):
    maps = P("dp", "space", None, None)
    in_specs = (maps, P("dp"), P("dp", "space")) + (P(),) * 8 + (maps,)
    out_specs = (maps, maps) + (P(None, "dp", None),) * 4 + (P(),) * 4
    return jax.shard_map(body, mesh=mesh, in_specs=in_specs, out_specs=out_specs, check_vma=False)
```

```python
import functools

import jax
import jax.numpy as jnp
from jax import lax
from jax.experimental import pallas as pl
from jax.experimental.pallas import tpu as pltpu
from jax.sharding import PartitionSpec as P

norm_eps = 1e-05
both = ("dp", "space")
f32 = jnp.float32
bf16 = jnp.bfloat16
group = 16
part = 512
chunk = 16
absent = -1e30
MB = 1024 * 1024


def dot(left, right):
    return jnp.dot(left, right, preferred_element_type=f32)


def dot_back(left, right):
    return lax.dot_general(left, right, (((1,), (1,)), ((), ())), preferred_element_type=f32)


def dot_inner(left, right):
    return lax.dot_general(left, right, (((0,), (0,)), ((), ())), preferred_element_type=f32)


def sigmoid(value):
    return 0.5 * jnp.tanh(0.5 * value) + 0.5


def silu(value):
    return value * sigmoid(value)


def silu_slope(value):
    sig = sigmoid(value)
    return sig * (1.0 + value * (1.0 - sig))


def lanes(rows):
    return jnp.concatenate([rows[i : i + 1] for i in range(rows.shape[0])], axis=1)


def unlanes(vector):
    return jnp.concatenate(
        [vector[:, 128 * i : 128 * (i + 1)] for i in range(vector.shape[1] // 128)], axis=0
    )


def pair_sum(ref):
    total = jnp.sum(ref[...], axis=0)
    return lanes(total[0:4]), lanes(total[4:8])


def norm_scale(sums, inv_count, gain, bias):
    mean = sums[0] * inv_count
    variance = sums[1] * inv_count - mean * mean
    inverse = lax.rsqrt(variance + norm_eps)
    scale = inverse * gain
    return mean, inverse, scale, bias - mean * scale


def store_pair(ref, first, second):
    rows = jnp.concatenate([unlanes(first), unlanes(second)], axis=0)
    ref[...] = jnp.broadcast_to(rows[None], (ref.shape[0], 8, 128))


def fold(value):
    return jnp.sum(value.reshape(-1, 8, value.shape[-1]), axis=0)


def squash(value):
    return jnp.sum(value, axis=0, keepdims=True)


def loop(count, body, init):
    return lax.fori_loop(0, count, body, init, unroll=True)


def at(index):
    return pl.ds(pl.multiple_of(index * chunk, chunk), chunk)


def columns(shape):
    return lax.broadcasted_iota(jnp.int32, shape, 0) % 8


def shift_columns(value, step):
    if step == 0:
        return value
    size = value.shape[0]
    col = columns(value.shape)
    moved = pltpu.roll(value, (-step) % size, 0)
    keep = (col + step >= 0) & (col + step < 8)
    return jnp.where(keep, moved, 0.0)


def params():
    return pltpu.CompilerParams(vmem_limit_bytes=60 * MB, dimension_semantics=("arbitrary",))


def whole(array):
    zeros = (0,) * array.ndim
    return pl.BlockSpec(array.shape, lambda *_: zeros)


def full(shape):
    zeros = (0,) * len(shape)
    return pl.BlockSpec(shape, lambda *_: zeros)


def gate_conv_rows(owners):
    return -(-7 * 128 // (owners * 16)) * 16


def wide_rows(owners, channels):
    return 9 * part // owners, channels // owners, channels // 4 // owners, gate_conv_rows(owners)


def shape_of(shape, kind):
    return jax.ShapeDtypeStruct(shape, kind)


def in_hbm(array):
    return pltpu.with_memory_space_constraint(array, pltpu.HBM)


def hbm_shape(shape, kind):
    return pltpu.HBM(shape, kind)


def cost(flops, moved, special=0):
    return pl.CostEstimate(flops=flops // 4, bytes_accessed=moved // 4, transcendentals=special)


def store_halo(low_ref, high_ref, value_of, mask_ref, sums, rows, size):
    mean = (sums * (1.0 / (rows * size))).astype(bf16)
    centre = mean.astype(f32)
    for ref, row in ((low_ref, 0), (high_ref, rows - 1)):

        def piece(i, _, ref=ref, row=row):
            value = value_of(row, i) - centre
            ref[at(i), :] = jnp.where(mask_ref[row, at(i), :] > 0.0, value, absent).astype(bf16)
            return 0

        loop(size // chunk, piece, 0)
        ref[pl.ds(size, 16), :] = jnp.broadcast_to(mean.astype(f32), (16, mean.shape[1])).astype(
            bf16
        )


def store_reduce(ref, acc, mask_ref, rows, size):
    space = ref.shape[0]
    for g in range(space):
        for r in range(rows):
            if g * group * 8 < size:
                lo = g * group * 8
                value = acc[r, lo : lo + group * 8, :].astype(bf16).astype(f32)
                ref[g, r] = (value * mask_ref[r, lo : lo + group * 8, :]).astype(bf16)
            else:
                ref[g, r] = jnp.zeros((group * 8, ref.shape[3]), bf16)


def finish_first(acc, acc_red, mask_ref, first, red, pay, low, high, rows, size):
    def piece(i, carry):
        s, q = carry
        for r in range(rows):
            value = acc[r, at(i), :] * mask_ref[r, at(i), :]
            first[r, at(i), :] = value
            s = s + fold(value)
            q = q + fold(value * value)
        return s, q

    zero = jnp.zeros((8, part), f32)
    s, q = loop(size // chunk, piece, (zero, zero))
    s, q = squash(s), squash(q)
    store_pair(pay, s, q)
    store_halo(low, high, lambda r, i: first[r, at(i), :], mask_ref, s, rows, size)
    store_reduce(red, acc_red, mask_ref, rows, size)


def first_kernel(rows, size, steps, x, w, w_red, mask, first, red, pay, low, high, acc, acc_red):
    step = pl.program_id(0)
    for r in range(rows):
        value = x[:, r].reshape(size, part)
        new, new_red = dot(value, w[...]), dot(value, w_red[...])

        @pl.when(step == 0)
        def _():
            acc[r] = new
            acc_red[r] = new_red

        @pl.when(step > 0)
        def _():
            acc[r] += new
            acc_red[r] += new_red

    @pl.when(step == steps - 1)
    def _():
        finish_first(acc, acc_red, mask, first, red, pay, low, high, rows, size)


def first_outputs(rows, size, devices, space, reduced):
    shapes = (
        shape_of((rows, size, part), f32),
        shape_of((space, rows, group * 8, reduced), bf16),
        shape_of((devices, 8, 128), f32),
        shape_of((size + 16, part), bf16),
        shape_of((size + 16, part), bf16),
    )
    return shapes, tuple(full(s.shape) for s in shapes)


def run_first(maps, layer, w, w_red, mask, devices, space):
    frames, rows, cols, channels = maps.shape
    size = frames * cols
    steps = channels // part
    reduced = w_red.shape[2]
    shapes, specs = first_outputs(rows, size, devices, space, reduced)
    return pl.pallas_call(
        functools.partial(first_kernel, rows, size, steps),
        grid=(steps,),
        in_specs=[
            pl.BlockSpec((frames, rows, cols, part), lambda k: (0, 0, 0, k)),
            pl.BlockSpec((None, part, part), lambda k: (layer, k, 0)),
            pl.BlockSpec((None, part, reduced), lambda k: (layer, k, 0)),
            whole(mask),
        ],
        out_specs=specs,
        out_shape=shapes,
        scratch_shapes=[pltpu.VMEM((rows, size, part), f32), pltpu.VMEM((rows, size, reduced), f32)],
        compiler_params=params(),
        cost_estimate=cost(2 * rows * size * channels * 640, 8 * MB),
        name="first",
    )(in_hbm(maps), in_hbm(w), in_hbm(w_red), mask)


def conv_kernel(rows, size, first, sums, inv, gain, bias, mask, w, hidden, out, shifted):
    step = pl.program_id(0)

    @pl.when(step == 0)
    def _():
        mean, inverse, scale, offset = norm_scale(
            pair_sum(sums), inv[0:1, 0:1], gain[...], bias[...]
        )

        def own(i, _):
            for r in range(rows):
                value = silu(first[r, at(i), :] * scale + offset) * mask[r, at(i), :]
                hidden[r, at(i), :] = value.astype(bf16)
                for j in range(3):
                    shifted[j, r, at(i), :] = shift_columns(value, j - 1).astype(bf16)
            return 0

        loop(size // chunk, own, 0)

    def taps(lo, hi, source):
        new = None
        for j in range(3):
            left = shifted[j, source : source + hi - lo].reshape((hi - lo) * size, part)
            term = dot(left, w[j * part : (j + 1) * part, :])
            new = term if new is None else new + term
        return new.reshape(hi - lo, size, part)

    own_taps(rows, step, out, taps)


def own_taps(rows, step, out, taps):
    @pl.when(step == 0)
    def _():
        out[...] = taps(0, rows, 0)

    if rows > 1:

        @pl.when(step == 1)
        def _():
            out[1:rows] += taps(1, rows, 0)

        @pl.when(step == 2)
        def _():
            out[0 : rows - 1] += taps(0, rows - 1, 1)


smem = pl.BlockSpec(memory_space=pltpu.SMEM)


def tap_order(step):
    return lax.rem(step + 1, 3)


def run_conv(first, sums, inv, gain, bias, mask, layer, w):
    rows, size = first.shape[:2]
    shapes = (shape_of((rows, size, part), bf16), shape_of((rows, size, part), f32))
    return pl.pallas_call(
        functools.partial(conv_kernel, rows, size),
        grid=(3 if rows > 1 else 1,),
        in_specs=[whole(first), whole(sums), whole(inv), whole(gain), whole(bias), whole(mask),
                  pl.BlockSpec((None, 3 * part, part), lambda i: (layer, jnp.where(i == 0, 1, jnp.where(i == 1, 0, 2)), 0))],
        out_specs=tuple(full(s.shape) for s in shapes),
        out_shape=shapes,
        scratch_shapes=[pltpu.VMEM((3, rows, size, part), bf16)],
        compiler_params=params(),
        cost_estimate=cost(2 * rows * size * 6 * part * part, 8 * MB),
        name="conv",
    )(first, sums, inv, gain, bias, mask, in_hbm(w))


def conv_edge_kernel(rows, size, before, low, high, edge, sums, inv, gain, bias, mask, w,
                     second, hidden, pay, send_low, send_high, shifted):
    step = pl.program_id(0)
    mean, inverse, scale, offset = norm_scale(pair_sum(sums), inv[0:1, 0:1], gain[...], bias[...])

    @pl.when(step == 0)
    def _():
        second[...] = before[...]

    for which, ref, row in ((0, low, 0), (1, high, rows - 1)):

        @pl.when(step == which)
        def _():
            centre = ref[pl.ds(size, 16), :].astype(f32)[0:1]
            here = edge[which] > 0

            def piece(i, _):
                got = ref[at(i), :].astype(f32)
                value = silu((got + centre) * scale + offset)
                value = jnp.where((got > 0.5 * absent) & here, value, 0.0)
                hidden[which, at(i), :] = value.astype(bf16)
                for j in range(3):
                    shifted[j, at(i), :] = shift_columns(value, j - 1).astype(bf16)
                return 0

            loop(size // chunk, piece, 0)
            new = None
            for j in range(3):
                term = dot(shifted[j], w[j * part : (j + 1) * part, :])
                new = term if new is None else new + term
            second[row] += new

    @pl.when(step == 1)
    def _():
        def piece(i, carry):
            s, q = carry
            for r in range(rows):
                value = second[r, at(i), :]
                masked = value * mask[r, at(i), :]
                s = s + fold(masked)
                q = q + fold(masked * value)
            return s, q

        zero = jnp.zeros((8, part), f32)
        s, q = loop(size // chunk, piece, (zero, zero))
        s, q = squash(s), squash(q)
        store_pair(pay, s, q)
        store_halo(send_low, send_high, lambda r, i: second[r, at(i), :], mask, s, rows, size)


def run_conv_edge(before, low, high, edge, sums, inv, gain, bias, mask, layer, w):
    rows, size = before.shape[:2]
    devices = sums.shape[0]
    shapes = (
        shape_of((rows, size, part), f32),
        shape_of((2, size, part), bf16),
        shape_of((devices, 8, 128), f32),
        shape_of((size + 16, part), bf16),
        shape_of((size + 16, part), bf16),
    )
    return pl.pallas_call(
        functools.partial(conv_edge_kernel, rows, size),
        grid=(2,),
        in_specs=[whole(before), whole(low), whole(high), smem, whole(sums), whole(inv), whole(gain),
                  whole(bias), whole(mask),
                  pl.BlockSpec((None, 3 * part, part), lambda i: (layer, 2 * i, 0))],
        out_specs=tuple(full(s.shape) for s in shapes),
        out_shape=shapes,
        scratch_shapes=[pltpu.VMEM((3, size, part), bf16)],
        compiler_params=params(),
        cost_estimate=cost(2 * size * 6 * part * part, 8 * MB),
        name="conv_edge",
    )(before, low, high, edge, sums, inv, gain, bias, mask, in_hbm(w))


def third_kernel(rows, size, second, sums, inv, gain, bias, mask, w, hidden, pay, prod):
    @pl.when(pl.program_id(0) == 0)
    def _():
        mean, inverse, scale, offset = norm_scale(
            pair_sum(sums), inv[0:1, 0:1], gain[...], bias[...]
        )

        def own(i, _):
            for r in range(rows):
                value = silu(second[r, at(i), :] * scale + offset) * mask[r, at(i), :]
                hidden[r, at(i), :] = value.astype(bf16)
            return 0

        loop(size // chunk, own, 0)

    prod[...] = dot(hidden[...].reshape(rows * size, part), w[...])

    def piece(i, carry):
        value = prod[at(i), :]
        return carry[0] + fold(value), carry[1] + fold(value * value)

    zero = jnp.zeros((8, part), f32)
    s, q = loop(rows * size // chunk, piece, (zero, zero))
    store_pair(pay, squash(s), squash(q))


def run_third(second, sums, inv, gain, bias, mask, layer, w):
    rows, size = second.shape[:2]
    devices = sums.shape[0]
    channels = w.shape[2]
    steps = channels // part
    return pl.pallas_call(
        functools.partial(third_kernel, rows, size),
        grid=(steps,),
        in_specs=[whole(second), whole(sums), whole(inv), whole(gain), whole(bias), whole(mask),
                  pl.BlockSpec((None, part, part), lambda k: (layer, 0, k))],
        out_specs=(full((rows, size, part)), pl.BlockSpec((devices, 8, 128), lambda k: (0, k, 0))),
        out_shape=(shape_of((rows, size, part), bf16), shape_of((devices, 8 * steps, 128), f32)),
        scratch_shapes=[pltpu.VMEM((rows * size, part), f32)],
        compiler_params=params(),
        cost_estimate=cost(2 * rows * size * channels * part, 5 * MB),
        name="third",
    )(second, sums, inv, gain, bias, mask, in_hbm(w))


def flat_gate(gate, rows, size):
    pieces = []
    for r in range(rows):
        for g in range(size // (group * 8)):
            pieces.append(gate[g, r])
    return jnp.concatenate(pieces, axis=0)


def mid_kernel(rows, size, steps, hidden, w_out, sums, inv, gain, bias, x, gate, w_exp, mask,
               w_next, red_next,
               out, branch, sig_out, slope, first, red, pay, low, high,
               prod, pre, acc, acc_red):
    step = pl.program_id(0)
    prod[...] = dot(hidden[...].reshape(rows * size, part), w_out[...]).reshape(rows, size, part)
    pre[...] = dot(flat_gate(gate, rows, size), w_exp[...]).reshape(rows, size, part)
    mean, inverse, scale, offset = norm_scale(pair_sum(sums), inv[0:1, 0:1], gain[...], bias[...])
    frames = chunk // 8

    def piece(i, _):
        for r in range(rows):
            b = prod[r, at(i), :] * scale + offset
            sig = sigmoid(pre[r, at(i), :])
            z = x[pl.ds(i * frames, frames), r].astype(f32).reshape(chunk, part) + b * sig
            zs = sigmoid(z)
            m = mask[r, at(i), :]
            out[r, at(i), :] = (z * zs * m).astype(bf16)
            slope[r, at(i), :] = (zs * (1.0 + z * (1.0 - zs)) * m).astype(bf16)
            branch[r, at(i), :] = b.astype(bf16)
            sig_out[r, at(i), :] = sig.astype(bf16)
        return 0

    loop(size // chunk, piece, 0)
    value = out[...].reshape(rows * size, part)
    new = dot(value, w_next[...]).reshape(rows, size, part)
    new_red = dot(value, red_next[...]).reshape(rows, size, acc_red.shape[2])

    @pl.when(step == 0)
    def _():
        acc[...] = new
        acc_red[...] = new_red

    @pl.when(step > 0)
    def _():
        acc[...] += new
        acc_red[...] += new_red

    @pl.when(step == steps - 1)
    def _():
        finish_first(acc, acc_red, mask, first, red, pay, low, high, rows, size)


def run_mid(layer, hidden, w_out, sums, inv, gain, bias, maps, gate, w_exp, mask, w_next, red_next):
    frames, rows, cols, channels = maps.shape
    size = frames * cols
    steps = channels // part
    devices, space = sums.shape[0], gate.shape[0]
    reduced = w_exp.shape[1]
    more, more_specs = first_outputs(rows, size, devices, space, reduced)
    wide = hbm_shape((rows, size, channels), bf16)
    slab = pl.BlockSpec((rows, size, part), lambda k: (0, 0, k))
    return pl.pallas_call(
        functools.partial(mid_kernel, rows, size, steps),
        grid=(steps,),
        in_specs=[
            whole(hidden),
            pl.BlockSpec((None, part, part), lambda k: (layer, 0, k)),
            pl.BlockSpec((devices, 8, 128), lambda k: (0, k, 0)),
            whole(inv),
            pl.BlockSpec((1, part), lambda k: (0, k)),
            pl.BlockSpec((1, part), lambda k: (0, k)),
            pl.BlockSpec((frames, rows, cols, part), lambda k: (0, 0, 0, k)),
            whole(gate),
            pl.BlockSpec((None, reduced, part), lambda k: (layer, 0, k)),
            whole(mask),
            pl.BlockSpec((None, part, part), lambda k: (layer + 1, k, 0)),
            pl.BlockSpec((None, part, reduced), lambda k: (layer + 1, k, 0)),
        ],
        out_specs=(slab,) * 4 + more_specs,
        out_shape=(wide,) * 4 + more,
        scratch_shapes=[pltpu.VMEM((rows, size, part), f32)] * 3
        + [pltpu.VMEM((rows, size, reduced), f32)],
        compiler_params=params(),
        cost_estimate=cost(2 * rows * size * channels * (part + part + 256), 20 * MB),
        name="mid",
    )(hidden, in_hbm(w_out), sums, inv, gain, bias, in_hbm(maps), gate, in_hbm(w_exp), mask,
      in_hbm(w_next), in_hbm(red_next))


def place(owner, owners, me):
    if me is None:
        return owner
    other = jnp.bitwise_xor(owner, me[0])
    return lax.rem(other, 2) * (owners // 2) + other // 2


def put_rows(ref, me, begin, per, value):
    done = 0
    while done < value.shape[0]:
        owner, offset = (begin + done) // per, (begin + done) % per
        length = min(value.shape[0] - done, per - offset)
        ref[place(owner, ref.shape[0], me), offset : offset + length, :] = value[done : done + length]
        done += length


def gate_grads(step, steps, rows, size, me, pre_grad, gate, w_exp, grad_exp, grad_gate, acc):
    left = flat_gate(gate, rows, size)
    right = pre_grad[...].reshape(rows * size, part)
    value = dot_inner(left, right).astype(bf16)
    owners, per = grad_exp.shape[:2]
    for i in range(steps):

        @pl.when(step == i)
        def _():
            put_rows(grad_exp, me, i * value.shape[0], per, value)

    new = dot_back(right, w_exp[...]).reshape(rows, size, acc.shape[2])

    @pl.when(step == 0)
    def _():
        acc[...] = new

    @pl.when(step > 0)
    def _():
        acc[...] += new

    @pl.when(step == steps - 1)
    def _():
        for g in range(grad_gate.shape[0]):
            for r in range(rows):
                lo = g * group * 8
                if lo < size:
                    grad_gate[g, r] = acc[r, lo : lo + group * 8, :].astype(bf16)
                else:
                    grad_gate[g, r] = jnp.zeros((group * 8, acc.shape[2]), bf16)


def last_kernel(rows, size, steps, hidden, w_out, sums, inv, gain, bias, x, gate, w_exp, mask,
                grad_out,
                out, branch, grad_branch, grad_in, grad_exp, grad_gate, pay,
                prod, pre, pre_grad, acc):
    step = pl.program_id(0)
    prod[...] = dot(hidden[...].reshape(rows * size, part), w_out[...]).reshape(rows, size, part)
    pre[...] = dot(flat_gate(gate, rows, size), w_exp[...]).reshape(rows, size, part)
    mean, inverse, scale, offset = norm_scale(pair_sum(sums), inv[0:1, 0:1], gain[...], bias[...])
    frames = chunk // 8

    def piece(i, carry):
        s, q = carry
        for r in range(rows):
            n = (prod[r, at(i), :] - mean) * inverse
            b = n * gain[...] + bias[...]
            sig = sigmoid(pre[r, at(i), :])
            z = x[r, at(i), :].astype(f32) + b * sig
            zs = sigmoid(z)
            m = mask[r, at(i), :]
            out[pl.ds(i * frames, frames), r] = (z * zs * m).reshape(frames, 8, part).astype(bf16)
            dz = grad_out[pl.ds(i * frames, frames), r].astype(f32).reshape(chunk, part)
            dz = dz * m * (zs * (1.0 + z * (1.0 - zs)))
            db = dz * sig
            s = s + fold(db)
            q = q + fold(db * n)
            branch[r, at(i), :] = b.astype(bf16)
            grad_branch[r, at(i), :] = db.astype(bf16)
            grad_in[r, at(i), :] = dz.astype(bf16)
            pre_grad[r, at(i), :] = (db * b * (1.0 - sig)).astype(bf16)
        return s, q

    zero = jnp.zeros((8, part), f32)
    s, q = loop(size // chunk, piece, (zero, zero))
    store_pair(pay, squash(s), squash(q))
    gate_grads(step, steps, rows, size, None, pre_grad, gate, w_exp, grad_exp, grad_gate, acc)


def expand_spec(owners, channels):
    rows = wide_rows(owners, channels)
    return pl.BlockSpec((owners, rows[2], part), lambda *_: (0, (rows[0] + rows[1]) // rows[2], 0))


def run_last(owners, layer, hidden, w_out, sums, inv, gain, bias, maps, gate, w_exp, mask, grad_out):
    frames, rows, cols, channels = grad_out.shape
    size = frames * cols
    steps = channels // part
    devices, space = sums.shape[0], gate.shape[0]
    reduced = w_exp.shape[1]
    wide = hbm_shape((rows, size, channels), bf16)
    slab = pl.BlockSpec((rows, size, part), lambda k: (0, 0, k))
    outside = pl.BlockSpec((frames, rows, cols, part), lambda k: (0, 0, 0, k))
    pays = pl.BlockSpec((devices, 8, 128), lambda k: (0, k, 0))
    row = pl.BlockSpec((1, part), lambda k: (0, k))
    return pl.pallas_call(
        functools.partial(last_kernel, rows, size, steps),
        grid=(steps,),
        in_specs=[
            whole(hidden), pl.BlockSpec((None, part, part), lambda k: (layer, 0, k)), pays, whole(inv),
            row, row, slab, whole(gate), pl.BlockSpec((None, reduced, part), lambda k: (layer, 0, k)),
            whole(mask), outside,
        ],
        out_specs=(outside, slab, slab, slab, expand_spec(owners, channels), full(gate.shape), pays),
        out_shape=(hbm_shape(grad_out.shape, bf16), wide, wide, wide,
                   hbm_shape((owners, sum(wide_rows(owners, channels)), part), bf16),
                   shape_of(gate.shape, bf16), shape_of(sums.shape, f32)),
        scratch_shapes=[pltpu.VMEM((rows, size, part), f32)] * 2
        + [pltpu.VMEM((rows, size, part), bf16), pltpu.VMEM((rows, size, reduced), f32)],
        compiler_params=params(),
        cost_estimate=cost(2 * rows * size * channels * (part + 512), 20 * MB),
        name="last",
    )(hidden, in_hbm(w_out), sums, inv, gain, bias, in_hbm(maps), gate, in_hbm(w_exp), mask,
      in_hbm(grad_out))


def third_back_kernel(rows, size, steps, fixed, me, buffer, grad_branch, branch, back_sums, sums, inv, gain, bias, mask,
                      hidden, w_out, second, sums_two, gain_two, bias_two,
                      grad_w, part_two, pay, low, high, third_grad, hidden_t, acc):
    step = pl.program_id(0)

    @pl.when(step == 0)
    def _():
        hidden_t[...] = hidden[...].reshape(rows * size, part).T

    inv_count = inv[0:1, 0:1]
    mean, inverse, scale, offset = norm_scale(pair_sum(sums), inv_count, gain[...], bias[...])
    sum_bias, sum_gain = pair_sum(back_sums)
    inv_gain = 1.0 / gain[...]
    slope = -scale * inv_count * sum_gain * inv_gain
    const = -scale * inv_count * sum_bias - slope * bias[...]

    def piece(i, _):
        for r in range(rows):
            db = grad_branch[r, at(i), :].astype(f32)
            b = branch[r, at(i), :].astype(f32)
            value = scale * db + mask[r, at(i), :] * (const + slope * b)
            third_grad[r, at(i), :] = value.astype(bf16)
        return 0

    loop(size // chunk, piece, 0)
    right = third_grad[...].reshape(rows * size, part)
    new = dot_back(right, w_out[...]).reshape(rows, size, part)

    @pl.when(step == 0)
    def _():
        acc[...] = new

    @pl.when(step > 0)
    def _():
        acc[...] += new

    put_rows(grad_w, None if fixed else me, 0, grad_w.shape[1], dot(hidden_t[...], right).astype(bf16))

    @pl.when(step == steps - 1)
    def _():
        finish_back(rows, size, acc, second, sums_two, inv, gain_two, bias_two, mask,
                    part_two, pay, low, high)


def finish_back(rows, size, acc, value_ref, sums, inv, gain, bias, mask, part_ref, pay, low, high):
    mean, inverse, scale, offset = norm_scale(pair_sum(sums), inv[0:1, 0:1], gain[...], bias[...])

    def piece(i, carry):
        s, q = carry
        for r in range(rows):
            n = (value_ref[r, at(i), :] - mean) * inverse
            grad = acc[r, at(i), :] * silu_slope(n * gain[...] + bias[...]) * mask[r, at(i), :]
            s = s + fold(grad)
            q = q + fold(grad * n)
            part_ref[r, at(i), :] = grad * scale
        return s, q

    zero = jnp.zeros((8, part), f32)
    s, q = loop(size // chunk, piece, (zero, zero))
    s, q = squash(s), squash(q)
    store_pair(pay, s, q)
    if low is not None:
        store_halo(low, high, lambda r, i: part_ref[r, at(i), :], mask, s * scale, rows, size)


def run_third_back(me, fixed, buffer, layer, grad_branch, branch, back_sums, sums, inv, gain, bias, mask,
                   hidden, w_out, second, sums_two, gain_two, bias_two):
    rows, size, channels = branch.shape
    steps = channels // part
    devices = sums.shape[0]
    owners = buffer.shape[0]
    slab = pl.BlockSpec((rows, size, part), lambda k: (0, 0, k))
    pays = pl.BlockSpec((devices, 8, 128), lambda k: (0, k, 0))
    row = pl.BlockSpec((1, part), lambda k: (0, k))
    return pl.pallas_call(
        functools.partial(third_back_kernel, rows, size, steps, fixed),
        grid=(steps,),
        in_specs=[smem, pl.BlockSpec(memory_space=pl.ANY), slab, slab, pays, pays, whole(inv), row, row, whole(mask), whole(hidden),
                  pl.BlockSpec((None, part, part), lambda k: (layer, 0, k)), whole(second), whole(sums_two),
                  whole(gain_two), whole(bias_two)],
        out_specs=(pl.BlockSpec((owners, part // owners, part), lambda k: (0, 9 + k, 0)),
                   full((rows, size, part)),
                   full((devices, 8, 128)), full((size + 16, part)), full((size + 16, part))),
        out_shape=(hbm_shape(buffer.shape, bf16), shape_of((rows, size, part), f32),
                   shape_of((devices, 8, 128), f32), shape_of((size + 16, part), bf16),
                   shape_of((size + 16, part), bf16)),
        scratch_shapes=[pltpu.VMEM((rows, size, part), bf16), pltpu.VMEM((part, rows * size), bf16),
                        pltpu.VMEM((rows, size, part), f32)],
        compiler_params=params(),
        cost_estimate=cost(4 * rows * size * channels * part, 12 * MB),
        input_output_aliases={1: 0},
        name="third_back",
    )(me, in_hbm(buffer), in_hbm(grad_branch), in_hbm(branch), back_sums, sums, inv, gain, bias, mask, hidden,
      in_hbm(w_out), second, sums_two, gain_two, bias_two)


def conv_back_kernel(rows, size, part_two, second, back_sums, sums_two, gain_two, bias_two, inv, mask,
                     w, grad_second, out, shifted):
    step = pl.program_id(0)

    @pl.when(step == 0)
    def _():
        inv_count = inv[0:1, 0:1]
        mean, inverse, scale, offset = norm_scale(
            pair_sum(sums_two), inv_count, gain_two[...], bias_two[...]
        )
        sum_bias, sum_gain = pair_sum(back_sums)
        slope = -scale * inv_count * sum_gain * inverse
        const = -scale * inv_count * sum_bias

        def own(i, _):
            for r in range(rows):
                centred = second[r, at(i), :] - mean
                value = part_two[r, at(i), :] + mask[r, at(i), :] * (const + slope * centred)
                grad_second[r, at(i), :] = value.astype(bf16)
                for j in range(3):
                    shifted[j, r, at(i), :] = shift_columns(value, 1 - j).astype(bf16)
            return 0

        loop(size // chunk, own, 0)

    def taps(lo, hi, source):
        new = None
        for j in range(3):
            left = shifted[j, source : source + hi - lo].reshape((hi - lo) * size, part)
            term = dot_back(left, w[j * part : (j + 1) * part, :])
            new = term if new is None else new + term
        return new.reshape(hi - lo, size, part)

    own_taps(rows, step, out, taps)


def run_conv_back(part_two, second, back_sums, sums_two, gain_two, bias_two, inv, mask, layer, w):
    rows, size = second.shape[:2]
    args = (part_two, second, back_sums, sums_two, gain_two, bias_two, inv, mask)
    shapes = (shape_of((rows, size, part), bf16), shape_of((rows, size, part), f32))
    return pl.pallas_call(
        functools.partial(conv_back_kernel, rows, size),
        grid=(3 if rows > 1 else 1,),
        in_specs=[whole(a) for a in args]
        + [pl.BlockSpec((None, 3 * part, part), lambda i: (layer, jnp.where(i == 0, 1, jnp.where(i == 1, 2, 0)), 0))],
        out_specs=tuple(full(s.shape) for s in shapes),
        out_shape=shapes,
        scratch_shapes=[pltpu.VMEM((3, rows, size, part), bf16)],
        compiler_params=params(),
        cost_estimate=cost(2 * rows * size * 6 * part * part, 8 * MB),
        name="conv_back",
    )(*args, in_hbm(w))


def conv_back_edge_kernel(rows, size, before, part_low, part_high, second_low, second_high, edge,
                          back_sums, sums_two, gain_two, bias_two, inv, mask, w,
                          first, sums_one, gain_one, bias_one, part_one, pay, shifted, acc):
    step = pl.program_id(0)
    inv_count = inv[0:1, 0:1]
    mean, inverse, scale, offset = norm_scale(
        pair_sum(sums_two), inv_count, gain_two[...], bias_two[...]
    )
    sum_bias, sum_gain = pair_sum(back_sums)
    slope = -scale * inv_count * sum_gain * inverse
    const = -scale * inv_count * sum_bias

    @pl.when(step == 0)
    def _():
        acc[...] = before[...]

    for which, ref, val, row, side in (
        (0, part_high, second_high, rows - 1, 1), (1, part_low, second_low, 0, 0)
    ):

        @pl.when(step == which)
        def _():
            middle = val[pl.ds(size, 16), :].astype(f32)[0:1] - mean
            base = ref[pl.ds(size, 16), :].astype(f32)[0:1] + const + slope * middle
            here = edge[side] > 0

            def piece(i, _):
                got = ref[at(i), :].astype(f32)
                value = got + base + slope * val[at(i), :].astype(f32)
                value = jnp.where((got > 0.5 * absent) & here, value, 0.0)
                for j in range(3):
                    shifted[j, at(i), :] = shift_columns(value, 1 - j).astype(bf16)
                return 0

            loop(size // chunk, piece, 0)
            new = None
            for j in range(3):
                term = dot_back(shifted[j], w[j * part : (j + 1) * part, :])
                new = term if new is None else new + term
            acc[row] += new

    @pl.when(step == 1)
    def _():
        finish_back(rows, size, acc, first, sums_one, inv, gain_one, bias_one, mask,
                    part_one, pay, None, None)


def run_conv_back_edge(before, part_low, part_high, second_low, second_high, edge, back_sums, sums_two,
                       gain_two, bias_two, inv, mask, layer, w, first, sums_one, gain_one, bias_one):
    rows, size = before.shape[:2]
    devices = sums_two.shape[0]
    args = (before, part_low, part_high, second_low, second_high, edge, back_sums, sums_two,
            gain_two, bias_two, inv, mask, w, first, sums_one, gain_one, bias_one)
    specs = [None if a is w else whole(a) for a in args]
    specs[5] = smem
    specs[12] = pl.BlockSpec((None, 3 * part, part), lambda i: (layer, 2 * i, 0))
    shapes = (shape_of((rows, size, part), f32), shape_of((devices, 8, 128), f32))
    return pl.pallas_call(
        functools.partial(conv_back_edge_kernel, rows, size),
        grid=(2,),
        in_specs=specs,
        out_specs=tuple(full(s.shape) for s in shapes),
        out_shape=shapes,
        scratch_shapes=[pltpu.VMEM((3, size, part), bf16), pltpu.VMEM((rows, size, part), f32)],
        compiler_params=params(),
        cost_estimate=cost(2 * size * 6 * part * part, 8 * MB),
        name="conv_back_edge",
    )(*[in_hbm(a) if a is w else a for a in args])


def conv_weight_kernel(rows, size, fixed, me, hidden, hidden_edge, grad_second, buffer, out, hidden_t, shifted):
    step = pl.program_id(0)
    owners, per = out.shape[:2]

    @pl.when(step == 0)
    def _():
        hidden_t[:, 0:size] = hidden_edge[0].T
        for r in range(rows):
            hidden_t[:, (r + 1) * size : (r + 2) * size] = hidden[r].T
        hidden_t[:, (rows + 1) * size : (rows + 2) * size] = hidden_edge[1].T

        def piece(i, _):
            for r in range(rows):
                value = grad_second[r, at(i), :].astype(f32)
                for j in range(3):
                    shifted[j, r, at(i), :] = shift_columns(value, 1 - j).astype(bf16)
            return 0

        loop(size // chunk, piece, 0)

    for i in range(3):

        @pl.when(step == i)
        def _():
            left = hidden_t[:, i * size : (i + rows) * size]
            for j in range(3):
                right = shifted[j].reshape(rows * size, part)
                value = dot(left, right).astype(bf16)
                put_rows(out, None if fixed else me, (3 * i + j) * part, per, value)


def run_conv_weight(me, fixed, hidden, hidden_edge, grad_second, buffer):
    rows, size = grad_second.shape[:2]
    owners = buffer.shape[0]
    return pl.pallas_call(
        functools.partial(conv_weight_kernel, rows, size, fixed),
        grid=(3,),
        in_specs=[smem, whole(hidden), whole(hidden_edge), whole(grad_second),
                  pl.BlockSpec(memory_space=pl.ANY)],
        out_specs=full((owners, 9 * part // owners, part)),
        out_shape=hbm_shape(buffer.shape, bf16),
        scratch_shapes=[pltpu.VMEM((part, (rows + 2) * size), bf16), pltpu.VMEM((3, rows, size, part), bf16)],
        input_output_aliases={4: 0},
        compiler_params=params(),
        cost_estimate=cost(2 * rows * size * 9 * part * part, 8 * MB),
        name="conv_weight",
    )(me, hidden, hidden_edge, grad_second, in_hbm(buffer))


def first_grad(rows, size, part_one, first, back_sums, sums_one, inv, gain, bias, mask, out):
    inv_count = inv[0:1, 0:1]
    mean, inverse, scale, offset = norm_scale(pair_sum(sums_one), inv_count, gain[...], bias[...])
    sum_bias, sum_gain = pair_sum(back_sums)
    slope = -scale * inv_count * sum_gain * inverse
    const = -scale * inv_count * sum_bias

    def own(i, _):
        for r in range(rows):
            centred = first[r, at(i), :] - mean
            value = part_one[r, at(i), :] + mask[r, at(i), :] * (const + slope * centred)
            out[r, at(i), :] = value.astype(bf16)
        return 0

    loop(size // chunk, own, 0)


def mask_gate(grad_rows, mask, out, rows, size):
    for r in range(rows):
        for g in range(size // (group * 8)):
            lo = g * group * 8
            value = grad_rows[g, r].astype(f32) * mask[r, lo : lo + group * 8, :]
            out[r, lo : lo + group * 8, :] = value.astype(bf16)


def between_kernel(rows, size, steps, part_one, first, back_sums, sums_one, inv, gain, bias, mask,
                   grad_rows, w_in, w_red, grad_above, slope, sig, branch, gain_three, bias_three,
                   gate, w_exp, me,
                   first_out, rows_out, grad_in, grad_branch, grad_exp, grad_gate, pay,
                   prod, pre_grad, acc):
    step = pl.program_id(0)

    @pl.when(step == 0)
    def _():
        first_grad(rows, size, part_one, first, back_sums, sums_one, inv, gain, bias, mask, first_out)
        mask_gate(grad_rows, mask, rows_out, rows, size)

    prod[...] = (
        dot_back(first_out[...].reshape(rows * size, part), w_in[...])
        + dot_back(rows_out[...].reshape(rows * size, rows_out.shape[2]), w_red[...])
    ).reshape(rows, size, part)
    inv_gain = 1.0 / gain_three[...]
    offset = bias_three[...] * inv_gain

    def piece(i, carry):
        s, q = carry
        for r in range(rows):
            dy = grad_above[r, at(i), :].astype(f32) + prod[r, at(i), :]
            dz = dy * slope[r, at(i), :].astype(f32)
            sg = sig[r, at(i), :].astype(f32)
            b = branch[r, at(i), :].astype(f32)
            db = dz * sg
            s = s + fold(db)
            q = q + fold(db * (b * inv_gain - offset))
            grad_branch[r, at(i), :] = db.astype(bf16)
            grad_in[r, at(i), :] = dz.astype(bf16)
            pre_grad[r, at(i), :] = (db * b * (1.0 - sg)).astype(bf16)
        return s, q

    zero = jnp.zeros((8, part), f32)
    s, q = loop(size // chunk, piece, (zero, zero))
    store_pair(pay, squash(s), squash(q))
    gate_grads(step, steps, rows, size, me, pre_grad, gate, w_exp, grad_exp, grad_gate, acc)


def run_between(me, owners, layer, part_one, first, back_sums, sums_one, inv, gain, bias, mask, grad_rows, w_in, w_red,
                grad_above, slope, sig, branch, gain_three, bias_three, gate, w_exp):
    rows, size, channels = branch.shape
    steps = channels // part
    devices = sums_one.shape[0]
    reduced = w_exp.shape[1]
    slab = pl.BlockSpec((rows, size, part), lambda k: (0, 0, k))
    pays = pl.BlockSpec((devices, 8, 128), lambda k: (0, k, 0))
    row = pl.BlockSpec((1, part), lambda k: (0, k))
    wide = hbm_shape(branch.shape, bf16)
    return pl.pallas_call(
        functools.partial(between_kernel, rows, size, steps),
        grid=(steps,),
        in_specs=[whole(part_one), whole(first), whole(back_sums), whole(sums_one), whole(inv),
                  whole(gain), whole(bias), whole(mask), whole(grad_rows),
                  pl.BlockSpec((None, part, part), lambda k: (layer, k, 0)),
                  pl.BlockSpec((None, part, reduced), lambda k: (layer, k, 0)),
                  slab, slab, slab, slab, row, row, whole(gate),
                  pl.BlockSpec((None, reduced, part), lambda k: (layer - 1, 0, k)), smem],
        out_specs=(full((rows, size, part)), full((rows, size, reduced)), slab, slab,
                   expand_spec(owners, channels), full(gate.shape), pays),
        out_shape=(shape_of((rows, size, part), bf16), shape_of((rows, size, reduced), bf16), wide, wide,
                   hbm_shape((owners, sum(wide_rows(owners, channels)), part), bf16),
                   shape_of(gate.shape, bf16), shape_of((devices, 8 * steps, 128), f32)),
        scratch_shapes=[pltpu.VMEM((rows, size, part), f32), pltpu.VMEM((rows, size, part), bf16),
                        pltpu.VMEM((rows, size, reduced), f32)],
        compiler_params=params(),
        cost_estimate=cost(2 * rows * size * channels * (part + 512), 20 * MB),
        name="between",
    )(part_one, first, back_sums, sums_one, inv, gain, bias, mask, grad_rows, in_hbm(w_in),
      in_hbm(w_red), in_hbm(grad_above), in_hbm(slope), in_hbm(sig), in_hbm(branch), gain_three,
      bias_three, gate, in_hbm(w_exp), me)


def first_back_kernel(rows, size, part_one, first, back_sums, sums_one, inv, gain, bias, mask, grad_rows,
                      first_out, rows_out):
    first_grad(rows, size, part_one, first, back_sums, sums_one, inv, gain, bias, mask, first_out)
    mask_gate(grad_rows, mask, rows_out, rows, size)


def run_first_back(part_one, first, back_sums, sums_one, inv, gain, bias, mask, grad_rows):
    rows, size = first.shape[:2]
    reduced = grad_rows.shape[3]
    args = (part_one, first, back_sums, sums_one, inv, gain, bias, mask, grad_rows)
    return pl.pallas_call(
        functools.partial(first_back_kernel, rows, size),
        grid=(1,),
        in_specs=[whole(a) for a in args],
        out_specs=(full((rows, size, part)), full((rows, size, reduced))),
        out_shape=(shape_of((rows, size, part), bf16), shape_of((rows, size, reduced), bf16)),
        compiler_params=params(),
        cost_estimate=cost(rows * size * part * 8, 5 * MB),
        name="first_back",
    )(*args)


def input_kernel(rows, size, first_out, rows_out, w_in, w_red, grad_above, mask, out, prod):
    prod[...] = (
        dot_back(first_out[...].reshape(rows * size, part), w_in[...])
        + dot_back(rows_out[...].reshape(rows * size, rows_out.shape[2]), w_red[...])
    ).reshape(rows, size, part)
    frames = chunk // 8

    def piece(i, _):
        for r in range(rows):
            value = grad_above[r, at(i), :].astype(f32) + prod[r, at(i), :] * mask[r, at(i), :]
            out[pl.ds(i * frames, frames), r] = value.reshape(frames, 8, part).astype(bf16)
        return 0

    loop(size // chunk, piece, 0)


def run_input(layer, first_out, rows_out, w_in, w_red, grad_above, mask, frames):
    rows, size, channels = grad_above.shape
    steps = channels // part
    reduced = w_red.shape[2]
    return pl.pallas_call(
        functools.partial(input_kernel, rows, size),
        grid=(steps,),
        in_specs=[whole(first_out), whole(rows_out),
                  pl.BlockSpec((None, part, part), lambda k: (layer, k, 0)),
                  pl.BlockSpec((None, part, reduced), lambda k: (layer, k, 0)),
                  pl.BlockSpec((rows, size, part), lambda k: (0, 0, k)), whole(mask)],
        out_specs=pl.BlockSpec((frames, rows, 8, part), lambda k: (0, 0, 0, k)),
        out_shape=hbm_shape((frames, rows, 8, channels), bf16),
        scratch_shapes=[pltpu.VMEM((rows, size, part), f32)],
        compiler_params=params(),
        cost_estimate=cost(2 * rows * size * channels * 640, 10 * MB),
        name="input",
    )(first_out, rows_out, in_hbm(w_in), in_hbm(w_red), in_hbm(grad_above), mask)


def weight_kernel(rows, size, steps, outside, fixed, me, x, first_out, rows_out, out):
    step = pl.program_id(0)
    for r in range(rows):
        value = x[:, r].reshape(size, part) if outside else x[r]
        turned = value.T
        new, new_red = dot(turned, first_out[r]), dot(turned, rows_out[r])
        total = new if r == 0 else total + new
        total_red = new_red if r == 0 else total_red + new_red
    owners = out.shape[0]
    here = owners // steps
    per = part // here
    quarter = per // 4
    for i in range(steps):

        @pl.when(step == i)
        def _():
            for d in range(here):
                where = place(i * here + d, owners, None if fixed else me)
                out[where, 0:per, :] = total[d * per : (d + 1) * per].astype(bf16)
                piece = total_red[d * per : (d + 1) * per]
                wide = [piece[j * quarter : (j + 1) * quarter] for j in range(4)]
                out[where, per : per + quarter, :] = jnp.concatenate(wide, axis=1).astype(bf16)


def run_weight(me, fixed, owners, x, first_out, rows_out):
    rows, size = first_out.shape[:2]
    channels = x.shape[-1]
    steps = channels // part
    per = channels // owners
    outside = x.ndim == 4
    if outside:
        x_spec = pl.BlockSpec((x.shape[0], rows, 8, part), lambda k: (0, 0, 0, k))
    else:
        x_spec = pl.BlockSpec((rows, size, part), lambda k: (0, 0, k))
    return pl.pallas_call(
        functools.partial(weight_kernel, rows, size, steps, outside, fixed),
        grid=(steps,),
        in_specs=[smem, x_spec, whole(first_out), whole(rows_out)],
        out_specs=full((owners, per + per // 4, part)),
        out_shape=hbm_shape((owners, per + per // 4, part), bf16),
        compiler_params=params(),
        cost_estimate=cost(2 * rows * size * channels * 640, 8 * MB),
        name="weight",
    )(me, in_hbm(x), first_out, rows_out)


def three_shifts(value, step, sign):
    height, size, channels = value.shape
    flat = value.reshape(height * size, channels)
    wide = jnp.concatenate(
        [shift_columns(flat, sign * (j - 1) * step).astype(bf16) for j in range(3)], axis=1
    ).reshape(height, size, 3 * channels)
    blank = jnp.zeros((1, size, 3 * channels), bf16)
    return jnp.concatenate([blank, wide, blank], axis=0)


def small_conv(taps, w):
    height, size = taps.shape[0] - 2, taps.shape[1]
    depth = taps.shape[2]
    total = None
    for i in range(3):
        new = dot(taps[i : i + height].reshape(height * size, depth), w[i * depth : (i + 1) * depth])
        total = new if total is None else total + new
    return total.reshape(height, size, -1)


def small_conv_back(taps, w):
    height, size = taps.shape[0] - 2, taps.shape[1]
    channels = taps.shape[2] // 3
    total = None
    for i in range(3):
        left = taps[2 - i : 2 - i + height].reshape(height * size, 3 * channels)
        for j in range(3):
            tap = (3 * i + j) * channels
            new = dot_back(left[:, j * channels : (j + 1) * channels], w[tap : tap + channels])
            total = new if total is None else total + new
    return total.reshape(height, size, channels)


def small_weight(taps, grad, out, me, which, factor):
    height, size = taps.shape[0] - 2, taps.shape[1]
    depth = taps.shape[2]
    right = grad.reshape(height * size, -1)
    for i in range(3):
        left = taps[i : i + height].reshape(height * size, depth)
        value = (dot_inner(left, right) * factor).astype(bf16)
        for j in range(3):
            block = 9 * which + 3 * i + j
            lane = block % 4 * 128
            put_rows(out.at[:, :, lane : lane + 128], me, block // 4 * 128, out.shape[1],
                     value[j * 128 : (j + 1) * 128])


def add_rows(value):
    height, size, channels = value.shape
    pairs = value.reshape(height // 2, 2, size, channels)
    return pairs[:, 0] + pairs[:, 1]


def add_columns(value, step):
    height, size, channels = value.shape
    flat = value.reshape(height * size, channels)
    count = height * size
    lower = columns(flat.shape) % (2 * step) < step
    moved = jnp.where(lower, pltpu.roll(flat, count - step, 0), pltpu.roll(flat, step, 0))
    return (flat + moved).reshape(height, size, channels)


def spread_rows(value, factor):
    height, size, channels = value.shape
    wide = jnp.broadcast_to(value[:, None], (height, factor, size, channels))
    return wide.reshape(height * factor, size, channels)


def take_frames(dest, source, index):
    height = dest.shape[0]
    for f in range(group):
        dest[:, f] = source[:, index[f]]


def gate_kernel(reduce_ref, index, w, out, coarse_two, coarse_four, plain, moved):
    height, size, channels = reduce_ref.shape
    plain[...] = reduce_ref[...].astype(f32).reshape(height, group, 8, channels)
    take_frames(moved, plain, index)
    diff = small_conv(three_shifts(moved[...].reshape(height, size, channels), 1, 1), w[0])
    diff = diff - plain[...].reshape(height, size, channels)
    sum_two = add_columns(add_rows(diff), 1)
    sum_four = add_columns(add_rows(sum_two), 2)
    two = (sum_two * 0.25).astype(bf16)
    four = (sum_four * 0.0625).astype(bf16)
    coarse_two[...] = two
    coarse_four[...] = four
    conv_two = small_conv(three_shifts(two.astype(f32), 2, 1), w[1])
    conv_four = small_conv(three_shifts(four.astype(f32), 4, 1), w[2])
    out[...] = (diff + spread_rows(conv_two, 2) + spread_rows(conv_four, 4)).astype(bf16)


def run_gate(layer, reduce_full, index, w):
    height, size, channels = reduce_full.shape
    shapes = (
        shape_of((height, size, channels), bf16),
        shape_of((height // 2, size, channels), bf16),
        shape_of((height // 4, size, channels), bf16),
    )
    return pl.pallas_call(
        gate_kernel,
        grid=(1,),
        in_specs=[whole(reduce_full), smem, pl.BlockSpec((None,) + w.shape[1:], lambda k: (layer, 0, 0, 0))],
        out_specs=tuple(full(s.shape) for s in shapes),
        out_shape=shapes,
        scratch_shapes=[pltpu.VMEM((height, group, 8, channels), f32)] * 2,
        compiler_params=params(),
        cost_estimate=cost(2 * height * size * 9 * channels * channels * 2, 2 * MB),
        name="gate",
    )(reduce_full, index, in_hbm(w))


def gate_back_kernel(fixed, me, buffer, grad, reduce_ref, index, w, coarse_two, coarse_four, out, grad_w,
                     plain, moved, total, back):
    height, size, channels = reduce_ref.shape
    me = None if fixed else me
    plain[...] = reduce_ref[...].astype(f32).reshape(height, group, 8, channels)
    take_frames(moved, plain, index)
    g = grad[...].astype(f32)
    sum_two = add_columns(add_rows(g), 1)
    sum_four = add_columns(add_rows(sum_two), 2)
    two = sum_two.astype(bf16)
    four = sum_four.astype(bf16)
    small_weight(three_shifts(coarse_two[...].astype(f32), 2, 1), two, grad_w, me, 1, 0.5)
    small_weight(three_shifts(coarse_four[...].astype(f32), 4, 1), four, grad_w, me, 2, 0.25)
    back_two = small_conv_back(three_shifts(two.astype(f32), 2, -1), w.at[1])
    back_four = small_conv_back(three_shifts(four.astype(f32), 4, -1), w.at[2])
    diff = g + spread_rows(back_two * 0.25, 2) + spread_rows(back_four * 0.0625, 4)
    low = diff.astype(bf16)
    small_weight(three_shifts(moved[...].reshape(height, size, channels), 1, 1), low, grad_w, me, 0, 1.0)
    back[...] = small_conv_back(three_shifts(low.astype(f32), 1, -1), w.at[0]).reshape(
        height, group, 8, channels
    )
    total[...] = -diff.reshape(height, group, 8, channels)
    for f in range(group):
        total[:, index[f]] += back[:, f]
    out[...] = total[...].reshape(height, size, channels).astype(bf16)


def run_gate_back(me, fixed, buffer, layer, grad, reduce_full, index, w, coarse_two, coarse_four):
    height, size, channels = reduce_full.shape
    owners, total = buffer.shape[:2]
    per = gate_conv_rows(owners)
    return pl.pallas_call(
        functools.partial(gate_back_kernel, fixed),
        grid=(1,),
        in_specs=[smem, pl.BlockSpec(memory_space=pl.ANY), whole(grad), whole(reduce_full), smem,
                  pl.BlockSpec((None,) + w.shape[1:], lambda k: (layer, 0, 0, 0)),
                  whole(coarse_two), whole(coarse_four)],
        out_specs=(full((height, size, channels)),
                   pl.BlockSpec((owners, per, part), lambda k: (0, (total - per) // per, 0))),
        out_shape=(shape_of((height, size, channels), bf16), hbm_shape(buffer.shape, bf16)),
        scratch_shapes=[pltpu.VMEM((height, group, 8, channels), f32)] * 4,
        compiler_params=params(),
        cost_estimate=cost(2 * height * size * 9 * channels * channels * 4, 3 * MB),
        input_output_aliases={1: 1},
        name="gate_back",
    )(me, in_hbm(buffer), grad, reduce_full, index, in_hbm(w), coarse_two, coarse_four)


def small_kernel(counts, owners, channels, places, first, second, convs, expand):
    wide, per = counts[2], counts[3]
    for layer, ref in ((0, first), (1, second)):
        for owner in range(owners):
            where = places[layer, owner]
            value = ref[where].astype(f32)
            done = 0
            while done < wide:
                row = owner * wide + done
                length = min(wide - done, 128 - row % 128)
                lane = row // 128 * part
                expand[layer, row % 128 : row % 128 + length, lane : lane + part] = value[done : done + length]
                done += length
            done = 0
            while done < per and owner * per + done < 7 * 128:
                row = owner * per + done
                length = min(per - done, 128 - row % 128)
                for j in range(4):
                    block = row // 128 * 4 + j
                    if block < 27:
                        top = block % 9 * 128 + row % 128
                        convs[layer, block // 9, top : top + length, :] = value[
                            wide + done : wide + done + length, j * 128 : (j + 1) * 128
                        ]
                done += length


def run_small(halves, places, counts, owners, channels):
    shapes = (shape_of((2, 3, 9 * 128, 128), f32), shape_of((2, 128, channels), f32))
    return pl.pallas_call(
        functools.partial(small_kernel, counts, owners, channels),
        grid=(1,),
        in_specs=[smem, whole(halves[0]), whole(halves[1])],
        out_specs=tuple(full(s.shape) for s in shapes),
        out_shape=shapes,
        compiler_params=params(),
        cost_estimate=cost(0, 8 * MB),
        name="small",
    )(places, *halves)


def large_kernel(counts, owners, channels, wide0, wide1, proj0, proj1, proj, conv, out, red):
    for layer, (wide, first) in enumerate(((wide0, proj0), (wide1, proj1))):
        rows = channels // owners
        proj[layer] = first[0:rows, :].astype(f32)
        quarter = rows // 4
        for j in range(4):
            red[layer, j * quarter : (j + 1) * quarter, :] = first[
                rows : rows + quarter, j * 128 : (j + 1) * 128
            ].astype(f32)
        conv[layer] = wide[0 : counts[0], :].astype(f32)
        per = part // owners
        for k in range(channels // part):
            at_row = counts[0] + k * per
            out[layer, :, k * part : (k + 1) * part] = wide[at_row : at_row + per, :].astype(f32)


def run_large(wide, proj, counts, owners, channels):
    rows = channels // owners
    shapes = (
        shape_of((2, rows, part), f32),
        shape_of((2, counts[0], part), f32),
        shape_of((2, part // owners, channels), f32),
        shape_of((2, rows, 128), f32),
    )
    args = (*wide, *proj)
    return pl.pallas_call(
        functools.partial(large_kernel, counts, owners, channels),
        grid=(1,),
        in_specs=[whole(a) for a in args],
        out_specs=tuple(full(s.shape) for s in shapes),
        out_shape=shapes,
        compiler_params=params(),
        cost_estimate=cost(0, 8 * MB),
        name="large",
    )(*args)


def exchange(block):
    return lax.all_to_all(block, both, 0, 0, tiled=True)


def to_frames(own):
    space, rows, size, channels = own.shape
    return lax.all_to_all(own, "space", 0, 0, tiled=True).reshape(space * rows, size, channels)


def to_rows(all_rows, rows):
    height, size, channels = all_rows.shape
    return lax.all_to_all(all_rows.reshape(height // rows, rows, size, channels), "space", 0, 0, tiled=True)


def neighbours(low, high):
    count = lax.axis_size("space")
    from_low = lax.ppermute(high, "space", [(i, i + 1) for i in range(count - 1)])
    from_high = lax.ppermute(low, "space", [(i + 1, i) for i in range(count - 1)])
    return from_low, from_high


def add(left, right):
    return (left.astype(f32) + right.astype(f32)).astype(bf16)


def swap(block, bit):
    count = lax.axis_size("dp")
    return lax.ppermute(block, "dp", [(i, i ^ bit) for i in range(count)])


def core_sum(grad):
    half = grad.shape[0] // 2
    return grad[:half], swap(grad[half:], 1)


def gather_owners(own):
    count = lax.axis_size("dp")
    bits = chip_bits()
    half = len(bits) // 2
    mine = lax.axis_index("dp")
    rows = own.shape[0] // 2
    sequences = (bits + [1], bits[half:] + bits[:half] + [1])
    got = [own[None, which * rows : (which + 1) * rows] for which in range(2)]
    for stage in range(len(sequences[0])):
        got = together(*got)
        new = [swap(g, sequence[stage]) for g, sequence in zip(got, sequences)]
        got = [jnp.concatenate(pair, axis=0) for pair in zip(got, new)]
    places = []
    for sequence in sequences:
        row = []
        for owner in range(count):
            other = jnp.bitwise_xor(mine, owner)
            row.append(sum(jnp.where(other & bit, 1 << i, 0) for i, bit in enumerate(sequence)))
        places.append(jnp.stack(row))
    return got, jnp.stack(places).astype(jnp.int32)


def chip_bits():
    count = lax.axis_size("dp")
    bits = []
    bit = 2
    while bit < count:
        bits.append(bit)
        bit *= 2
    return bits


def reduce_start(kept, got):
    bits = chip_bits()
    rows, cols = kept.shape[1:]
    half = len(bits) // 2
    state = []
    for which, sequence in enumerate((bits, bits[half:] + bits[:half])):
        span = slice(which * (rows // 2), (which + 1) * (rows // 2))
        shape = (2,) * len(bits) + (rows // 2, cols)
        state.append((kept[:, span].reshape(shape), got[:, span].reshape(shape), bits, sequence))
    return reduce_step(state)


def reduce_step(state):
    stays, goes = [], []
    for keep, new, left, sequence in state:
        where = len(left) - 1 - left.index(sequence[0])
        stay, go = [
            add(
                lax.index_in_dim(keep, side, where, keepdims=False),
                lax.index_in_dim(new, side, where, keepdims=False),
            )
            for side in (0, 1)
        ]
        stays.append(stay)
        goes.append(go)
    goes = together(*goes)
    return [
        (stay, swap(go, sequence[0]), [b for b in left if b != sequence[0]], sequence[1:])
        for stay, go, (_, _, left, sequence) in zip(stays, goes, state)
    ]


def reduce_finish(state):
    while state[0][3]:
        state = reduce_step(state)
    return jnp.concatenate([add(keep, new) for keep, new, _, _ in state], axis=0)


def space_sum(value):
    count = lax.axis_size("space")
    rows, cols = value.shape
    parts = lax.all_to_all(value.reshape(count, rows // count, cols), "space", 0, 0, tiled=True)
    own = jnp.sum(parts.astype(f32), axis=0).astype(bf16)
    spread = jnp.broadcast_to(own[None], (count,) + own.shape)
    return lax.all_to_all(spread, "space", 0, 0, tiled=True).reshape(rows, cols)


def together(*values):
    return lax.optimization_barrier(values)


def body(
    clip_maps,
    next_frame,
    valid_rows,
    proj_in,
    conv_mid,
    proj_out,
    gate_reduce,
    gate_convs,
    gate_expand,
    norm_gain,
    norm_bias,
    out_grad,
):
    frames, rows, cols, channels = clip_maps.shape
    size = frames * cols
    space, here = lax.axis_size("space"), lax.axis_index("space")
    devices = lax.axis_size("dp") * space
    valid = valid_rows.astype(f32)
    mask = jnp.broadcast_to(valid.T[:, :, None], (rows, frames, cols)).reshape(rows, size, 1)
    edge = jnp.stack([(here > 0).astype(jnp.int32), (here < space - 1).astype(jnp.int32)])
    padded = jnp.pad(next_frame, (0, space * group - frames))
    own_next = lax.dynamic_slice_in_dim(padded, here * group, group)
    base = lax.axis_index("dp") * frames + here * group
    index = jnp.clip(own_next - base, 0, group - 1)
    count = exchange(jnp.full((devices, 1, 128), jnp.sum(valid) * cols))
    inv = 1.0 / jnp.sum(count, axis=0)

    def vectors(layer):
        out = []
        for source in (norm_gain, norm_bias):
            row = source[layer][None]
            out.append((row[:, :part], row[:, part : 2 * part], row[:, 2 * part :]))
        return out

    gains, biases = zip(vectors(0), vectors(1))
    owners = lax.axis_size("dp")
    firsts = [run_first(clip_maps, 0, proj_in, gate_reduce, mask, devices, space), None]
    sums_one, sums_two, sums_three = [None, None], [None, None], [None, None]
    seconds, hidden_twos, gates, reduces = [None, None], [None, None], [None, None], [None, None]
    gate_kept, halos, hidden_ones = [None, None], [None, None], [None, None]
    firsts[0] = list(firsts[0])
    for layer in range(2):
        gain, bias = gains[layer], biases[layer]
        first, red, pay, low, high = firsts[layer]
        sums_one[layer] = exchange(pay)
        halo = neighbours(low, high)
        reduces[layer] = to_frames(red)
        hidden_own, before = run_conv(
            first, sums_one[layer], inv, gain[0], bias[0], mask, layer, conv_mid
        )
        second, hidden_edge, pay, low, high = run_conv_edge(
            before, *halo, edge, sums_one[layer], inv, gain[0], bias[0], mask, layer, conv_mid
        )
        hidden_ones[layer] = hidden_own, hidden_edge
        seconds[layer] = second
        sums_two[layer] = exchange(pay)
        gate_full, *gate_kept[layer] = run_gate(layer, reduces[layer], index, gate_convs)
        sums_two[layer], gate_full = together(sums_two[layer], gate_full)
        gates[layer] = to_rows(gate_full, rows)
        hidden_twos[layer], pay = run_third(
            second, sums_two[layer], inv, gain[1], bias[1], mask, layer, proj_out
        )
        sums_three[layer] = exchange(pay)
        low, high = together(sums_three[layer], low, high)[1:]
        halos[layer] = neighbours(low, high)
        if layer == 0:
            mid, branch_zero, sig_zero, slope_zero, *firsts[1] = run_mid(
                0, hidden_twos[0], proj_out, sums_three[0], inv, gain[2], bias[2], clip_maps,
                gates[0], gate_expand, mask, proj_in, gate_reduce,
            )
            firsts[1][2], *halos[0] = together(firsts[1][2], *halos[0])
    out_maps, branch_one, grad_branch, grad_in, buffer, grad_gate, pay = run_last(
        owners, 1, hidden_twos[1], proj_out, sums_three[1], inv, gains[1][2], biases[1][2], mid,
        gates[1], gate_expand, mask, out_grad,
    )
    pay, *halos[1] = together(pay, *halos[1])
    branches = [branch_zero, branch_one]
    me = lax.axis_index("dp").astype(jnp.int32)[None]
    results = [None, None]
    vectors_of = [None, None]

    def scatter(grad):
        return lax.psum_scatter(grad, "dp", scatter_dimension=0, tiled=False)

    for layer in (1, 0):
        fixed = layer == 1
        gain, bias = gains[layer], biases[layer]
        first, second = firsts[layer][0], seconds[layer]
        back_three = exchange(pay)
        grad_full = to_frames(grad_gate)
        if layer == 0:
            grad_proj = run_weight(me, True, owners, mid, first_out, rows_out)
            back_three, grad_proj = together(back_three, grad_proj)
            results[1] = results[1] + (scatter(grad_proj),)
        buffer, part_two, pay, low, high = run_third_back(
            me, fixed, buffer, layer, grad_branch, branches[layer], back_three, sums_three[layer], inv,
            gain[2], bias[2], mask, hidden_twos[layer], proj_out, second, sums_two[layer],
            gain[1], bias[1],
        )
        back_two = exchange(pay)
        halo = neighbours(low, high)
        rows_full, buffer = run_gate_back(
            me, fixed, buffer, layer, grad_full, reduces[layer], index, gate_convs, *gate_kept[layer]
        )
        back_two, rows_full = together(back_two, rows_full)
        grad_second, before = run_conv_back(
            part_two, second, back_two, sums_two[layer], gain[1], bias[1], inv, mask, layer, conv_mid
        )
        grad_rows = to_rows(rows_full, rows)
        if layer == 0:
            before, scattered = together(before, results[1][0])
            results[1] = (scattered,) + results[1][1:]
        part_one, pay = run_conv_back_edge(
            before, *halo, *halos[layer], edge, back_two, sums_two[layer], gain[1], bias[1], inv, mask,
            layer, conv_mid, first, sums_one[layer], gain[0], bias[0],
        )
        pay, grad_second, grad_rows = together(pay, grad_second, grad_rows)
        back_one = exchange(pay)
        buffer = run_conv_weight(me, fixed, *hidden_ones[layer], grad_second, buffer)
        if layer == 0:
            back_one, buffer, scattered = together(back_one, buffer, results[1][1])
            results[1] = (results[1][0], scattered)
        else:
            back_one, buffer = together(back_one, buffer)
        common = (part_one, first, back_one, sums_one[layer], inv, gain[0], bias[0], mask, grad_rows)
        if layer == 1:
            results[1] = (scatter(buffer),)
            first_out, rows_out, grad_in, grad_branch, buffer, grad_gate, pay = run_between(
                me, owners, 1, *common, proj_in, gate_reduce, grad_in, slope_zero, sig_zero,
                branch_zero, gains[0][2], biases[0][2], gates[0], gate_expand,
            )
        else:
            wide_sum = core_sum(buffer)
            first_out, rows_out = run_first_back(*common)
            grad_proj = run_weight(me, False, owners, clip_maps, first_out, rows_out)
            wide_state = reduce_start(*wide_sum)
            grad_proj, *arrived = together(grad_proj, *[half[1] for half in wide_state])
            wide_state = [(half[0], new) + half[2:] for half, new in zip(wide_state, arrived)]
            results[0] = reduce_finish(wide_state), reduce_finish(reduce_start(*core_sum(grad_proj)))
            grad_maps = run_input(0, first_out, rows_out, proj_in, gate_reduce, grad_in, mask, frames)
        vecs = [jnp.sum(back, axis=0) for back in (back_one, back_two, back_three)]

        def pick(which):
            return jnp.concatenate(
                [v.reshape(-1, 2, 4, 128)[:, which].reshape(-1) for v in vecs]
            )

        vectors_of[layer] = pick(1), pick(0)

    counts = wide_rows(owners, channels)
    ends = [sum(counts[: i + 1]) for i in range(4)]
    wide, proj = results[0]
    wide, *later = together(wide, *lax.psum(results[1], "space"))
    wide = space_sum(wide)
    proj = space_sum(proj)
    halves, places = gather_owners(jnp.concatenate([v[ends[1] :] for v in (wide, later[0])], axis=0))
    convs, expand = run_small(halves, places, counts, owners, channels)
    large = run_large([wide, later[0]], [proj, later[1]], counts, owners, channels)
    little = [jnp.stack(pair) for pair in zip(*vectors_of)]
    return (out_maps, grad_maps, *large, convs, expand, *little)


def solution(mesh):
    maps = P("dp", "space", None, None)
    in_specs = (maps, P("dp"), P("dp", "space")) + (P(),) * 8 + (maps,)
    out_specs = (maps, maps) + (P(None, "dp", None),) * 4 + (P(),) * 4
    return jax.shard_map(body, mesh=mesh, in_specs=in_specs, out_specs=out_specs, check_vma=False)
```

```python
import functools

import jax
import jax.numpy as jnp
from jax import lax
from jax.experimental import pallas as pl
from jax.experimental.pallas import tpu as pltpu
from jax.sharding import PartitionSpec as P

norm_eps = 1e-05
both = ("dp", "space")
f32 = jnp.float32
bf16 = jnp.bfloat16
group = 16
part = 512
chunk = 16
absent = -1e30
MB = 1024 * 1024


def dot(left, right):
    return jnp.dot(left, right, preferred_element_type=f32)


def dot_back(left, right):
    return lax.dot_general(left, right, (((1,), (1,)), ((), ())), preferred_element_type=f32)


def dot_inner(left, right):
    return lax.dot_general(left, right, (((0,), (0,)), ((), ())), preferred_element_type=f32)


def sigmoid(value):
    return 0.5 * jnp.tanh(0.5 * value) + 0.5


def silu(value):
    return value * sigmoid(value)


def silu_slope(value):
    sig = sigmoid(value)
    return sig * (1.0 + value * (1.0 - sig))


def lanes(rows):
    return jnp.concatenate([rows[i : i + 1] for i in range(rows.shape[0])], axis=1)


def unlanes(vector):
    return jnp.concatenate(
        [vector[:, 128 * i : 128 * (i + 1)] for i in range(vector.shape[1] // 128)], axis=0
    )


def pair_sum(ref):
    total = jnp.sum(ref[...], axis=0)
    return lanes(total[0:4]), lanes(total[4:8])


def norm_scale(sums, inv_count, gain, bias):
    mean = sums[0] * inv_count
    variance = sums[1] * inv_count - mean * mean
    inverse = lax.rsqrt(variance + norm_eps)
    scale = inverse * gain
    return mean, inverse, scale, bias - mean * scale


def store_pair(ref, first, second):
    rows = jnp.concatenate([unlanes(first), unlanes(second)], axis=0)
    ref[:, 0:8, :] = jnp.broadcast_to(rows[None], (ref.shape[0], 8, 128))


def fold(value):
    return jnp.sum(value.reshape(-1, 8, value.shape[-1]), axis=0)


def squash(value):
    return jnp.sum(value, axis=0, keepdims=True)


def loop(count, body, init):
    return lax.fori_loop(0, count, body, init, unroll=True)


def at(index):
    return pl.ds(pl.multiple_of(index * chunk, chunk), chunk)


def columns(shape):
    return lax.broadcasted_iota(jnp.int32, shape, 0) % 8


def shift_columns(value, step):
    if step == 0:
        return value
    size = value.shape[0]
    col = columns(value.shape)
    moved = pltpu.roll(value, (-step) % size, 0)
    keep = (col + step >= 0) & (col + step < 8)
    return jnp.where(keep, moved, 0.0)


def params():
    return pltpu.CompilerParams(vmem_limit_bytes=60 * MB, dimension_semantics=("arbitrary",))


def whole(array):
    zeros = (0,) * array.ndim
    return pl.BlockSpec(array.shape, lambda *_: zeros)


def full(shape):
    zeros = (0,) * len(shape)
    return pl.BlockSpec(shape, lambda *_: zeros)


def gate_conv_rows(owners):
    return -(-7 * 128 // (owners * 16)) * 16


def wide_rows(owners, channels):
    return 9 * part // owners, channels // owners, channels // 4 // owners, gate_conv_rows(owners)


def shape_of(shape, kind):
    return jax.ShapeDtypeStruct(shape, kind)


def in_hbm(array):
    return pltpu.with_memory_space_constraint(array, pltpu.HBM)


def hbm_shape(shape, kind):
    return pltpu.HBM(shape, kind)


def cost(flops, moved, special=0):
    return pl.CostEstimate(flops=flops // 4, bytes_accessed=moved // 4, transcendentals=special)


def store_halo(low_ref, high_ref, value_of, mask_ref, sums, rows, size):
    mean = (sums * (1.0 / (rows * size))).astype(bf16)
    centre = mean.astype(f32)
    for ref, row in ((low_ref, 0), (high_ref, rows - 1)):

        def piece(i, _, ref=ref, row=row):
            value = value_of(row, i) - centre
            ref[at(i), :] = jnp.where(mask_ref[row, at(i), :] > 0.0, value, absent).astype(bf16)
            return 0

        loop(size // chunk, piece, 0)
        ref[pl.ds(size, 16), :] = jnp.broadcast_to(mean.astype(f32), (16, mean.shape[1])).astype(
            bf16
        )


def store_reduce(ref, acc, mask_ref, rows, size):
    space = ref.shape[0]
    for g in range(space):
        for r in range(rows):
            if g * group * 8 < size:
                lo = g * group * 8
                value = acc[r, lo : lo + group * 8, :].astype(bf16).astype(f32)
                ref[g, r] = (value * mask_ref[r, lo : lo + group * 8, :]).astype(bf16)
            else:
                ref[g, r] = jnp.zeros((group * 8, ref.shape[3]), bf16)


def finish_first(acc, acc_red, mask_ref, first, red, pay, low, high, rows, size):
    def piece(i, carry):
        s, q = carry
        for r in range(rows):
            value = acc[r, at(i), :] * mask_ref[r, at(i), :]
            first[r, at(i), :] = value
            s = s + fold(value)
            q = q + fold(value * value)
        return s, q

    zero = jnp.zeros((8, part), f32)
    s, q = loop(size // chunk, piece, (zero, zero))
    s, q = squash(s), squash(q)
    store_pair(pay, s, q)
    if pay.shape[1] > 8:
        total = mask_ref[0]
        for r in range(1, rows):
            total = total + mask_ref[r]
        total = jnp.broadcast_to(jnp.sum(total, axis=0, keepdims=True), (1, 128))
        pay[:, 8:9, :] = jnp.broadcast_to(total[None], (pay.shape[0], 1, 128))
    store_halo(low, high, lambda r, i: first[r, at(i), :], mask_ref, s, rows, size)
    store_reduce(red, acc_red, mask_ref, rows, size)


def first_kernel(rows, size, steps, x, w, w_red, mask, first, red, pay, low, high, acc, acc_red):
    step = pl.program_id(0)
    for r in range(rows):
        value = x[:, r].reshape(size, part)
        new, new_red = dot(value, w[...]), dot(value, w_red[...])

        @pl.when(step == 0)
        def _():
            acc[r] = new
            acc_red[r] = new_red

        @pl.when(step > 0)
        def _():
            acc[r] += new
            acc_red[r] += new_red

    @pl.when(step == steps - 1)
    def _():
        finish_first(acc, acc_red, mask, first, red, pay, low, high, rows, size)


def first_outputs(rows, size, devices, space, reduced, pay_rows=8):
    shapes = (
        shape_of((rows, size, part), f32),
        shape_of((space, rows, group * 8, reduced), bf16),
        shape_of((devices, pay_rows, 128), f32),
        shape_of((size + 16, part), bf16),
        shape_of((size + 16, part), bf16),
    )
    return shapes, tuple(full(s.shape) for s in shapes)


def run_first(maps, layer, w, w_red, mask, devices, space):
    frames, rows, cols, channels = maps.shape
    size = frames * cols
    steps = channels // part
    reduced = w_red.shape[2]
    shapes, specs = first_outputs(rows, size, devices, space, reduced, 9)
    return pl.pallas_call(
        functools.partial(first_kernel, rows, size, steps),
        grid=(steps,),
        in_specs=[
            pl.BlockSpec((frames, rows, cols, part), lambda k: (0, 0, 0, k)),
            pl.BlockSpec((None, part, part), lambda k: (layer, k, 0)),
            pl.BlockSpec((None, part, reduced), lambda k: (layer, k, 0)),
            whole(mask),
        ],
        out_specs=specs,
        out_shape=shapes,
        scratch_shapes=[pltpu.VMEM((rows, size, part), f32), pltpu.VMEM((rows, size, reduced), f32)],
        compiler_params=params(),
        cost_estimate=cost(2 * rows * size * channels * 640, 8 * MB),
        name="first",
    )(in_hbm(maps), in_hbm(w), in_hbm(w_red), mask)


def conv_kernel(rows, size, first, sums, inv, gain, bias, mask, w, hidden, out, shifted):
    step = pl.program_id(0)

    @pl.when(step == 0)
    def _():
        mean, inverse, scale, offset = norm_scale(
            pair_sum(sums), inv[0:1, 0:1], gain[...], bias[...]
        )

        def own(i, _):
            for r in range(rows):
                value = silu(first[r, at(i), :] * scale + offset) * mask[r, at(i), :]
                hidden[r, at(i), :] = value.astype(bf16)
                for j in range(3):
                    shifted[j, r, at(i), :] = shift_columns(value, j - 1).astype(bf16)
            return 0

        loop(size // chunk, own, 0)

    def taps(lo, hi, source):
        new = None
        for j in range(3):
            left = shifted[j, source : source + hi - lo].reshape((hi - lo) * size, part)
            term = dot(left, w[j * part : (j + 1) * part, :])
            new = term if new is None else new + term
        return new.reshape(hi - lo, size, part)

    own_taps(rows, step, out, taps)


def own_taps(rows, step, out, taps):
    @pl.when(step == 0)
    def _():
        out[...] = taps(0, rows, 0)

    if rows > 1:

        @pl.when(step == 1)
        def _():
            out[1:rows] += taps(1, rows, 0)

        @pl.when(step == 2)
        def _():
            out[0 : rows - 1] += taps(0, rows - 1, 1)


smem = pl.BlockSpec(memory_space=pltpu.SMEM)


def tap_order(step):
    return lax.rem(step + 1, 3)


def run_conv(first, sums, inv, gain, bias, mask, layer, w):
    rows, size = first.shape[:2]
    shapes = (shape_of((rows, size, part), bf16), shape_of((rows, size, part), f32))
    return pl.pallas_call(
        functools.partial(conv_kernel, rows, size),
        grid=(3 if rows > 1 else 1,),
        in_specs=[whole(first), whole(sums), whole(inv), whole(gain), whole(bias), whole(mask),
                  pl.BlockSpec((None, 3 * part, part), lambda i: (layer, jnp.where(i == 0, 1, jnp.where(i == 1, 0, 2)), 0))],
        out_specs=tuple(full(s.shape) for s in shapes),
        out_shape=shapes,
        scratch_shapes=[pltpu.VMEM((3, rows, size, part), bf16)],
        compiler_params=params(),
        cost_estimate=cost(2 * rows * size * 6 * part * part, 8 * MB),
        name="conv",
    )(first, sums, inv, gain, bias, mask, in_hbm(w))


def conv_edge_kernel(rows, size, before, low, high, edge, sums, inv, gain, bias, mask, w,
                     second, hidden, pay, send_low, send_high, shifted):
    step = pl.program_id(0)
    mean, inverse, scale, offset = norm_scale(pair_sum(sums), inv[0:1, 0:1], gain[...], bias[...])

    @pl.when(step == 0)
    def _():
        second[...] = before[...]

    for which, ref, row in ((0, low, 0), (1, high, rows - 1)):

        @pl.when(step == which)
        def _():
            centre = ref[pl.ds(size, 16), :].astype(f32)[0:1]
            here = edge[which] > 0

            def piece(i, _):
                got = ref[at(i), :].astype(f32)
                value = silu((got + centre) * scale + offset)
                value = jnp.where((got > 0.5 * absent) & here, value, 0.0)
                hidden[which, at(i), :] = value.astype(bf16)
                for j in range(3):
                    shifted[j, at(i), :] = shift_columns(value, j - 1).astype(bf16)
                return 0

            loop(size // chunk, piece, 0)
            new = None
            for j in range(3):
                term = dot(shifted[j], w[j * part : (j + 1) * part, :])
                new = term if new is None else new + term
            second[row] += new

    @pl.when(step == 1)
    def _():
        def piece(i, carry):
            s, q = carry
            for r in range(rows):
                value = second[r, at(i), :]
                masked = value * mask[r, at(i), :]
                s = s + fold(masked)
                q = q + fold(masked * value)
            return s, q

        zero = jnp.zeros((8, part), f32)
        s, q = loop(size // chunk, piece, (zero, zero))
        s, q = squash(s), squash(q)
        store_pair(pay, s, q)
        store_halo(send_low, send_high, lambda r, i: second[r, at(i), :], mask, s, rows, size)


def run_conv_edge(before, low, high, edge, sums, inv, gain, bias, mask, layer, w):
    rows, size = before.shape[:2]
    devices = sums.shape[0]
    shapes = (
        shape_of((rows, size, part), f32),
        shape_of((2, size, part), bf16),
        shape_of((devices, 8, 128), f32),
        shape_of((size + 16, part), bf16),
        shape_of((size + 16, part), bf16),
    )
    return pl.pallas_call(
        functools.partial(conv_edge_kernel, rows, size),
        grid=(2,),
        in_specs=[whole(before), whole(low), whole(high), smem, whole(sums), whole(inv), whole(gain),
                  whole(bias), whole(mask),
                  pl.BlockSpec((None, 3 * part, part), lambda i: (layer, 2 * i, 0))],
        out_specs=tuple(full(s.shape) for s in shapes),
        out_shape=shapes,
        scratch_shapes=[pltpu.VMEM((3, size, part), bf16)],
        compiler_params=params(),
        cost_estimate=cost(2 * size * 6 * part * part, 8 * MB),
        name="conv_edge",
    )(before, low, high, edge, sums, inv, gain, bias, mask, in_hbm(w))


def third_kernel(rows, size, second, sums, inv, gain, bias, mask, w, hidden, pay, prod):
    @pl.when(pl.program_id(0) == 0)
    def _():
        mean, inverse, scale, offset = norm_scale(
            pair_sum(sums), inv[0:1, 0:1], gain[...], bias[...]
        )

        def own(i, _):
            for r in range(rows):
                value = silu(second[r, at(i), :] * scale + offset) * mask[r, at(i), :]
                hidden[r, at(i), :] = value.astype(bf16)
            return 0

        loop(size // chunk, own, 0)

    prod[...] = dot(hidden[...].reshape(rows * size, part), w[...])

    def piece(i, carry):
        value = prod[at(i), :]
        return carry[0] + fold(value), carry[1] + fold(value * value)

    zero = jnp.zeros((8, part), f32)
    s, q = loop(rows * size // chunk, piece, (zero, zero))
    store_pair(pay, squash(s), squash(q))


def run_third(second, sums, inv, gain, bias, mask, layer, w):
    rows, size = second.shape[:2]
    devices = sums.shape[0]
    channels = w.shape[2]
    steps = channels // part
    return pl.pallas_call(
        functools.partial(third_kernel, rows, size),
        grid=(steps,),
        in_specs=[whole(second), whole(sums), whole(inv), whole(gain), whole(bias), whole(mask),
                  pl.BlockSpec((None, part, part), lambda k: (layer, 0, k))],
        out_specs=(full((rows, size, part)), pl.BlockSpec((devices, 8, 128), lambda k: (0, k, 0))),
        out_shape=(shape_of((rows, size, part), bf16), shape_of((devices, 8 * steps, 128), f32)),
        scratch_shapes=[pltpu.VMEM((rows * size, part), f32)],
        compiler_params=params(),
        cost_estimate=cost(2 * rows * size * channels * part, 5 * MB),
        name="third",
    )(second, sums, inv, gain, bias, mask, in_hbm(w))


def flat_gate(gate, rows, size):
    pieces = []
    for r in range(rows):
        for g in range(size // (group * 8)):
            pieces.append(gate[g, r])
    return jnp.concatenate(pieces, axis=0)


def mid_kernel(rows, size, steps, hidden, w_out, sums, inv, gain, bias, x, gate, w_exp, mask,
               w_next, red_next,
               out, branch, sig_out, slope, first, red, pay, low, high,
               prod, pre, acc, acc_red):
    step = pl.program_id(0)
    prod[...] = dot(hidden[...].reshape(rows * size, part), w_out[...]).reshape(rows, size, part)
    pre[...] = dot(flat_gate(gate, rows, size), w_exp[...]).reshape(rows, size, part)
    mean, inverse, scale, offset = norm_scale(pair_sum(sums), inv[0:1, 0:1], gain[...], bias[...])
    frames = chunk // 8

    def piece(i, _):
        for r in range(rows):
            b = prod[r, at(i), :] * scale + offset
            sig = sigmoid(pre[r, at(i), :])
            z = x[pl.ds(i * frames, frames), r].astype(f32).reshape(chunk, part) + b * sig
            zs = sigmoid(z)
            m = mask[r, at(i), :]
            out[r, at(i), :] = (z * zs * m).astype(bf16)
            slope[r, at(i), :] = (zs * (1.0 + z * (1.0 - zs)) * m).astype(bf16)
            branch[r, at(i), :] = b.astype(bf16)
            sig_out[r, at(i), :] = sig.astype(bf16)
        return 0

    loop(size // chunk, piece, 0)
    value = out[...].reshape(rows * size, part)
    new = dot(value, w_next[...]).reshape(rows, size, part)
    new_red = dot(value, red_next[...]).reshape(rows, size, acc_red.shape[2])

    @pl.when(step == 0)
    def _():
        acc[...] = new
        acc_red[...] = new_red

    @pl.when(step > 0)
    def _():
        acc[...] += new
        acc_red[...] += new_red

    @pl.when(step == steps - 1)
    def _():
        finish_first(acc, acc_red, mask, first, red, pay, low, high, rows, size)


def run_mid(layer, hidden, w_out, sums, inv, gain, bias, maps, gate, w_exp, mask, w_next, red_next):
    frames, rows, cols, channels = maps.shape
    size = frames * cols
    steps = channels // part
    devices, space = sums.shape[0], gate.shape[0]
    reduced = w_exp.shape[1]
    more, more_specs = first_outputs(rows, size, devices, space, reduced)
    wide = hbm_shape((rows, size, channels), bf16)
    slab = pl.BlockSpec((rows, size, part), lambda k: (0, 0, k))
    return pl.pallas_call(
        functools.partial(mid_kernel, rows, size, steps),
        grid=(steps,),
        in_specs=[
            whole(hidden),
            pl.BlockSpec((None, part, part), lambda k: (layer, 0, k)),
            pl.BlockSpec((devices, 8, 128), lambda k: (0, k, 0)),
            whole(inv),
            pl.BlockSpec((1, part), lambda k: (0, k)),
            pl.BlockSpec((1, part), lambda k: (0, k)),
            pl.BlockSpec((frames, rows, cols, part), lambda k: (0, 0, 0, k)),
            whole(gate),
            pl.BlockSpec((None, reduced, part), lambda k: (layer, 0, k)),
            whole(mask),
            pl.BlockSpec((None, part, part), lambda k: (layer + 1, k, 0)),
            pl.BlockSpec((None, part, reduced), lambda k: (layer + 1, k, 0)),
        ],
        out_specs=(slab,) * 4 + more_specs,
        out_shape=(wide,) * 4 + more,
        scratch_shapes=[pltpu.VMEM((rows, size, part), f32)] * 3
        + [pltpu.VMEM((rows, size, reduced), f32)],
        compiler_params=params(),
        cost_estimate=cost(2 * rows * size * channels * (part + part + 256), 20 * MB),
        name="mid",
    )(hidden, in_hbm(w_out), sums, inv, gain, bias, in_hbm(maps), gate, in_hbm(w_exp), mask,
      in_hbm(w_next), in_hbm(red_next))


def place(owner, owners, me):
    if me is None:
        return owner
    other = jnp.bitwise_xor(owner, me[0])
    return lax.rem(other, 2) * (owners // 2) + other // 2


def put_rows(ref, me, begin, per, value):
    done = 0
    while done < value.shape[0]:
        owner, offset = (begin + done) // per, (begin + done) % per
        length = min(value.shape[0] - done, per - offset)
        ref[place(owner, ref.shape[0], me), offset : offset + length, :] = value[done : done + length]
        done += length


def gate_grads(step, steps, rows, size, me, pre_grad, gate, w_exp, grad_exp, grad_gate, acc):
    left = flat_gate(gate, rows, size)
    right = pre_grad[...].reshape(rows * size, part)
    value = dot_inner(left, right).astype(bf16)
    owners, per = grad_exp.shape[:2]
    for i in range(steps):

        @pl.when(step == i)
        def _():
            put_rows(grad_exp, me, i * value.shape[0], per, value)

    new = dot_back(right, w_exp[...]).reshape(rows, size, acc.shape[2])

    @pl.when(step == 0)
    def _():
        acc[...] = new

    @pl.when(step > 0)
    def _():
        acc[...] += new

    @pl.when(step == steps - 1)
    def _():
        for g in range(grad_gate.shape[0]):
            for r in range(rows):
                lo = g * group * 8
                if lo < size:
                    grad_gate[g, r] = acc[r, lo : lo + group * 8, :].astype(bf16)
                else:
                    grad_gate[g, r] = jnp.zeros((group * 8, acc.shape[2]), bf16)


def last_kernel(rows, size, steps, hidden, w_out, sums, inv, gain, bias, x, gate, w_exp, mask,
                grad_out,
                out, branch, grad_branch, grad_in, grad_exp, grad_gate, pay,
                prod, pre, pre_grad, acc):
    step = pl.program_id(0)
    prod[...] = dot(hidden[...].reshape(rows * size, part), w_out[...]).reshape(rows, size, part)
    pre[...] = dot(flat_gate(gate, rows, size), w_exp[...]).reshape(rows, size, part)
    mean, inverse, scale, offset = norm_scale(pair_sum(sums), inv[0:1, 0:1], gain[...], bias[...])
    frames = chunk // 8

    def piece(i, carry):
        s, q = carry
        for r in range(rows):
            n = (prod[r, at(i), :] - mean) * inverse
            b = n * gain[...] + bias[...]
            sig = sigmoid(pre[r, at(i), :])
            z = x[r, at(i), :].astype(f32) + b * sig
            zs = sigmoid(z)
            m = mask[r, at(i), :]
            out[pl.ds(i * frames, frames), r] = (z * zs * m).reshape(frames, 8, part).astype(bf16)
            dz = grad_out[pl.ds(i * frames, frames), r].astype(f32).reshape(chunk, part)
            dz = dz * m * (zs * (1.0 + z * (1.0 - zs)))
            db = dz * sig
            s = s + fold(db)
            q = q + fold(db * n)
            branch[r, at(i), :] = b.astype(bf16)
            grad_branch[r, at(i), :] = db.astype(bf16)
            grad_in[r, at(i), :] = dz.astype(bf16)
            pre_grad[r, at(i), :] = (db * b * (1.0 - sig)).astype(bf16)
        return s, q

    zero = jnp.zeros((8, part), f32)
    s, q = loop(size // chunk, piece, (zero, zero))
    store_pair(pay, squash(s), squash(q))
    gate_grads(step, steps, rows, size, None, pre_grad, gate, w_exp, grad_exp, grad_gate, acc)


def expand_spec(owners, channels):
    rows = wide_rows(owners, channels)
    return pl.BlockSpec((owners, rows[2], part), lambda *_: (0, (rows[0] + rows[1]) // rows[2], 0))


def run_last(owners, layer, hidden, w_out, sums, inv, gain, bias, maps, gate, w_exp, mask, grad_out):
    frames, rows, cols, channels = grad_out.shape
    size = frames * cols
    steps = channels // part
    devices, space = sums.shape[0], gate.shape[0]
    reduced = w_exp.shape[1]
    wide = hbm_shape((rows, size, channels), bf16)
    slab = pl.BlockSpec((rows, size, part), lambda k: (0, 0, k))
    outside = pl.BlockSpec((frames, rows, cols, part), lambda k: (0, 0, 0, k))
    pays = pl.BlockSpec((devices, 8, 128), lambda k: (0, k, 0))
    row = pl.BlockSpec((1, part), lambda k: (0, k))
    return pl.pallas_call(
        functools.partial(last_kernel, rows, size, steps),
        grid=(steps,),
        in_specs=[
            whole(hidden), pl.BlockSpec((None, part, part), lambda k: (layer, 0, k)), pays, whole(inv),
            row, row, slab, whole(gate), pl.BlockSpec((None, reduced, part), lambda k: (layer, 0, k)),
            whole(mask), outside,
        ],
        out_specs=(outside, slab, slab, slab, expand_spec(owners, channels), full(gate.shape), pays),
        out_shape=(hbm_shape(grad_out.shape, bf16), wide, wide, wide,
                   hbm_shape((owners, sum(wide_rows(owners, channels)), part), bf16),
                   shape_of(gate.shape, bf16), shape_of(sums.shape, f32)),
        scratch_shapes=[pltpu.VMEM((rows, size, part), f32)] * 2
        + [pltpu.VMEM((rows, size, part), bf16), pltpu.VMEM((rows, size, reduced), f32)],
        compiler_params=params(),
        cost_estimate=cost(2 * rows * size * channels * (part + 512), 20 * MB),
        name="last",
    )(hidden, in_hbm(w_out), sums, inv, gain, bias, in_hbm(maps), gate, in_hbm(w_exp), mask,
      in_hbm(grad_out))


def third_back_kernel(rows, size, steps, fixed, me, buffer, grad_branch, branch, back_sums, sums, inv, gain, bias, mask,
                      hidden, w_out, second, sums_two, gain_two, bias_two,
                      grad_w, part_two, pay, low, high, third_grad, hidden_t, acc):
    step = pl.program_id(0)

    @pl.when(step == 0)
    def _():
        hidden_t[...] = hidden[...].reshape(rows * size, part).T

    inv_count = inv[0:1, 0:1]
    mean, inverse, scale, offset = norm_scale(pair_sum(sums), inv_count, gain[...], bias[...])
    sum_bias, sum_gain = pair_sum(back_sums)
    inv_gain = 1.0 / gain[...]
    slope = -scale * inv_count * sum_gain * inv_gain
    const = -scale * inv_count * sum_bias - slope * bias[...]

    def piece(i, _):
        for r in range(rows):
            db = grad_branch[r, at(i), :].astype(f32)
            b = branch[r, at(i), :].astype(f32)
            value = scale * db + mask[r, at(i), :] * (const + slope * b)
            third_grad[r, at(i), :] = value.astype(bf16)
        return 0

    loop(size // chunk, piece, 0)
    right = third_grad[...].reshape(rows * size, part)
    new = dot_back(right, w_out[...]).reshape(rows, size, part)

    @pl.when(step == 0)
    def _():
        acc[...] = new

    @pl.when(step > 0)
    def _():
        acc[...] += new

    put_rows(grad_w, None if fixed else me, 0, grad_w.shape[1], dot(hidden_t[...], right).astype(bf16))

    @pl.when(step == steps - 1)
    def _():
        finish_back(rows, size, acc, second, sums_two, inv, gain_two, bias_two, mask,
                    part_two, pay, low, high)


def finish_back(rows, size, acc, value_ref, sums, inv, gain, bias, mask, part_ref, pay, low, high):
    mean, inverse, scale, offset = norm_scale(pair_sum(sums), inv[0:1, 0:1], gain[...], bias[...])

    def piece(i, carry):
        s, q = carry
        for r in range(rows):
            n = (value_ref[r, at(i), :] - mean) * inverse
            grad = acc[r, at(i), :] * silu_slope(n * gain[...] + bias[...]) * mask[r, at(i), :]
            s = s + fold(grad)
            q = q + fold(grad * n)
            part_ref[r, at(i), :] = grad * scale
        return s, q

    zero = jnp.zeros((8, part), f32)
    s, q = loop(size // chunk, piece, (zero, zero))
    s, q = squash(s), squash(q)
    store_pair(pay, s, q)
    if low is not None:
        store_halo(low, high, lambda r, i: part_ref[r, at(i), :], mask, s * scale, rows, size)


def run_third_back(me, fixed, buffer, layer, grad_branch, branch, back_sums, sums, inv, gain, bias, mask,
                   hidden, w_out, second, sums_two, gain_two, bias_two):
    rows, size, channels = branch.shape
    steps = channels // part
    devices = sums.shape[0]
    owners = buffer.shape[0]
    slab = pl.BlockSpec((rows, size, part), lambda k: (0, 0, k))
    pays = pl.BlockSpec((devices, 8, 128), lambda k: (0, k, 0))
    row = pl.BlockSpec((1, part), lambda k: (0, k))
    return pl.pallas_call(
        functools.partial(third_back_kernel, rows, size, steps, fixed),
        grid=(steps,),
        in_specs=[smem, pl.BlockSpec(memory_space=pl.ANY), slab, slab, pays, pays, whole(inv), row, row, whole(mask), whole(hidden),
                  pl.BlockSpec((None, part, part), lambda k: (layer, 0, k)), whole(second), whole(sums_two),
                  whole(gain_two), whole(bias_two)],
        out_specs=(pl.BlockSpec((owners, part // owners, part), lambda k: (0, 9 + k, 0)),
                   full((rows, size, part)),
                   full((devices, 8, 128)), full((size + 16, part)), full((size + 16, part))),
        out_shape=(hbm_shape(buffer.shape, bf16), shape_of((rows, size, part), f32),
                   shape_of((devices, 8, 128), f32), shape_of((size + 16, part), bf16),
                   shape_of((size + 16, part), bf16)),
        scratch_shapes=[pltpu.VMEM((rows, size, part), bf16), pltpu.VMEM((part, rows * size), bf16),
                        pltpu.VMEM((rows, size, part), f32)],
        compiler_params=params(),
        cost_estimate=cost(4 * rows * size * channels * part, 12 * MB),
        input_output_aliases={1: 0},
        name="third_back",
    )(me, in_hbm(buffer), in_hbm(grad_branch), in_hbm(branch), back_sums, sums, inv, gain, bias, mask, hidden,
      in_hbm(w_out), second, sums_two, gain_two, bias_two)


def conv_back_kernel(rows, size, part_two, second, back_sums, sums_two, gain_two, bias_two, inv, mask,
                     w, grad_second, out, shifted):
    step = pl.program_id(0)

    @pl.when(step == 0)
    def _():
        inv_count = inv[0:1, 0:1]
        mean, inverse, scale, offset = norm_scale(
            pair_sum(sums_two), inv_count, gain_two[...], bias_two[...]
        )
        sum_bias, sum_gain = pair_sum(back_sums)
        slope = -scale * inv_count * sum_gain * inverse
        const = -scale * inv_count * sum_bias

        def own(i, _):
            for r in range(rows):
                centred = second[r, at(i), :] - mean
                value = part_two[r, at(i), :] + mask[r, at(i), :] * (const + slope * centred)
                grad_second[r, at(i), :] = value.astype(bf16)
                for j in range(3):
                    shifted[j, r, at(i), :] = shift_columns(value, 1 - j).astype(bf16)
            return 0

        loop(size // chunk, own, 0)

    def taps(lo, hi, source):
        new = None
        for j in range(3):
            left = shifted[j, source : source + hi - lo].reshape((hi - lo) * size, part)
            term = dot_back(left, w[j * part : (j + 1) * part, :])
            new = term if new is None else new + term
        return new.reshape(hi - lo, size, part)

    own_taps(rows, step, out, taps)


def run_conv_back(part_two, second, back_sums, sums_two, gain_two, bias_two, inv, mask, layer, w):
    rows, size = second.shape[:2]
    args = (part_two, second, back_sums, sums_two, gain_two, bias_two, inv, mask)
    shapes = (shape_of((rows, size, part), bf16), shape_of((rows, size, part), f32))
    return pl.pallas_call(
        functools.partial(conv_back_kernel, rows, size),
        grid=(3 if rows > 1 else 1,),
        in_specs=[whole(a) for a in args]
        + [pl.BlockSpec((None, 3 * part, part), lambda i: (layer, jnp.where(i == 0, 1, jnp.where(i == 1, 2, 0)), 0))],
        out_specs=tuple(full(s.shape) for s in shapes),
        out_shape=shapes,
        scratch_shapes=[pltpu.VMEM((3, rows, size, part), bf16)],
        compiler_params=params(),
        cost_estimate=cost(2 * rows * size * 6 * part * part, 8 * MB),
        name="conv_back",
    )(*args, in_hbm(w))


def conv_back_edge_kernel(rows, size, before, part_low, part_high, second_low, second_high, edge,
                          back_sums, sums_two, gain_two, bias_two, inv, mask, w,
                          first, sums_one, gain_one, bias_one, part_one, pay, shifted, acc):
    step = pl.program_id(0)
    inv_count = inv[0:1, 0:1]
    mean, inverse, scale, offset = norm_scale(
        pair_sum(sums_two), inv_count, gain_two[...], bias_two[...]
    )
    sum_bias, sum_gain = pair_sum(back_sums)
    slope = -scale * inv_count * sum_gain * inverse
    const = -scale * inv_count * sum_bias

    @pl.when(step == 0)
    def _():
        acc[...] = before[...]

    for which, ref, val, row, side in (
        (0, part_high, second_high, rows - 1, 1), (1, part_low, second_low, 0, 0)
    ):

        @pl.when(step == which)
        def _():
            middle = val[pl.ds(size, 16), :].astype(f32)[0:1] - mean
            base = ref[pl.ds(size, 16), :].astype(f32)[0:1] + const + slope * middle
            here = edge[side] > 0

            def piece(i, _):
                got = ref[at(i), :].astype(f32)
                value = got + base + slope * val[at(i), :].astype(f32)
                value = jnp.where((got > 0.5 * absent) & here, value, 0.0)
                for j in range(3):
                    shifted[j, at(i), :] = shift_columns(value, 1 - j).astype(bf16)
                return 0

            loop(size // chunk, piece, 0)
            new = None
            for j in range(3):
                term = dot_back(shifted[j], w[j * part : (j + 1) * part, :])
                new = term if new is None else new + term
            acc[row] += new

    @pl.when(step == 1)
    def _():
        finish_back(rows, size, acc, first, sums_one, inv, gain_one, bias_one, mask,
                    part_one, pay, None, None)


def run_conv_back_edge(before, part_low, part_high, second_low, second_high, edge, back_sums, sums_two,
                       gain_two, bias_two, inv, mask, layer, w, first, sums_one, gain_one, bias_one):
    rows, size = before.shape[:2]
    devices = sums_two.shape[0]
    args = (before, part_low, part_high, second_low, second_high, edge, back_sums, sums_two,
            gain_two, bias_two, inv, mask, w, first, sums_one, gain_one, bias_one)
    specs = [None if a is w else whole(a) for a in args]
    specs[5] = smem
    specs[12] = pl.BlockSpec((None, 3 * part, part), lambda i: (layer, 2 * i, 0))
    shapes = (shape_of((rows, size, part), f32), shape_of((devices, 8, 128), f32))
    return pl.pallas_call(
        functools.partial(conv_back_edge_kernel, rows, size),
        grid=(2,),
        in_specs=specs,
        out_specs=tuple(full(s.shape) for s in shapes),
        out_shape=shapes,
        scratch_shapes=[pltpu.VMEM((3, size, part), bf16), pltpu.VMEM((rows, size, part), f32)],
        compiler_params=params(),
        cost_estimate=cost(2 * size * 6 * part * part, 8 * MB),
        name="conv_back_edge",
    )(*[in_hbm(a) if a is w else a for a in args])


def conv_weight_kernel(rows, size, fixed, me, hidden, hidden_edge, grad_second, buffer, out, hidden_t, shifted):
    step = pl.program_id(0)
    owners, per = out.shape[:2]

    @pl.when(step == 0)
    def _():
        hidden_t[:, 0:size] = hidden_edge[0].T
        for r in range(rows):
            hidden_t[:, (r + 1) * size : (r + 2) * size] = hidden[r].T
        hidden_t[:, (rows + 1) * size : (rows + 2) * size] = hidden_edge[1].T

        def piece(i, _):
            for r in range(rows):
                value = grad_second[r, at(i), :].astype(f32)
                for j in range(3):
                    shifted[j, r, at(i), :] = shift_columns(value, 1 - j).astype(bf16)
            return 0

        loop(size // chunk, piece, 0)

    for i in range(3):

        @pl.when(step == i)
        def _():
            left = hidden_t[:, i * size : (i + rows) * size]
            for j in range(3):
                right = shifted[j].reshape(rows * size, part)
                value = dot(left, right).astype(bf16)
                put_rows(out, None if fixed else me, (3 * i + j) * part, per, value)


def run_conv_weight(me, fixed, hidden, hidden_edge, grad_second, buffer):
    rows, size = grad_second.shape[:2]
    owners = buffer.shape[0]
    return pl.pallas_call(
        functools.partial(conv_weight_kernel, rows, size, fixed),
        grid=(3,),
        in_specs=[smem, whole(hidden), whole(hidden_edge), whole(grad_second),
                  pl.BlockSpec(memory_space=pl.ANY)],
        out_specs=full((owners, 9 * part // owners, part)),
        out_shape=hbm_shape(buffer.shape, bf16),
        scratch_shapes=[pltpu.VMEM((part, (rows + 2) * size), bf16), pltpu.VMEM((3, rows, size, part), bf16)],
        input_output_aliases={4: 0},
        compiler_params=params(),
        cost_estimate=cost(2 * rows * size * 9 * part * part, 8 * MB),
        name="conv_weight",
    )(me, hidden, hidden_edge, grad_second, in_hbm(buffer))


def first_grad(rows, size, part_one, first, back_sums, sums_one, inv, gain, bias, mask, out):
    inv_count = inv[0:1, 0:1]
    mean, inverse, scale, offset = norm_scale(pair_sum(sums_one), inv_count, gain[...], bias[...])
    sum_bias, sum_gain = pair_sum(back_sums)
    slope = -scale * inv_count * sum_gain * inverse
    const = -scale * inv_count * sum_bias

    def own(i, _):
        for r in range(rows):
            centred = first[r, at(i), :] - mean
            value = part_one[r, at(i), :] + mask[r, at(i), :] * (const + slope * centred)
            out[r, at(i), :] = value.astype(bf16)
        return 0

    loop(size // chunk, own, 0)


def mask_gate(grad_rows, mask, out, rows, size):
    for r in range(rows):
        for g in range(size // (group * 8)):
            lo = g * group * 8
            value = grad_rows[g, r].astype(f32) * mask[r, lo : lo + group * 8, :]
            out[r, lo : lo + group * 8, :] = value.astype(bf16)


def between_kernel(rows, size, steps, part_one, first, back_sums, sums_one, inv, gain, bias, mask,
                   grad_rows, w_in, w_red, grad_above, slope, sig, branch, gain_three, bias_three,
                   gate, w_exp, me,
                   first_out, rows_out, grad_in, grad_branch, grad_exp, grad_gate, pay,
                   prod, pre_grad, acc):
    step = pl.program_id(0)

    @pl.when(step == 0)
    def _():
        first_grad(rows, size, part_one, first, back_sums, sums_one, inv, gain, bias, mask, first_out)
        mask_gate(grad_rows, mask, rows_out, rows, size)

    prod[...] = (
        dot_back(first_out[...].reshape(rows * size, part), w_in[...])
        + dot_back(rows_out[...].reshape(rows * size, rows_out.shape[2]), w_red[...])
    ).reshape(rows, size, part)
    inv_gain = 1.0 / gain_three[...]
    offset = bias_three[...] * inv_gain

    def piece(i, carry):
        s, q = carry
        for r in range(rows):
            dy = grad_above[r, at(i), :].astype(f32) + prod[r, at(i), :]
            dz = dy * slope[r, at(i), :].astype(f32)
            sg = sig[r, at(i), :].astype(f32)
            b = branch[r, at(i), :].astype(f32)
            db = dz * sg
            s = s + fold(db)
            q = q + fold(db * (b * inv_gain - offset))
            grad_branch[r, at(i), :] = db.astype(bf16)
            grad_in[r, at(i), :] = dz.astype(bf16)
            pre_grad[r, at(i), :] = (db * b * (1.0 - sg)).astype(bf16)
        return s, q

    zero = jnp.zeros((8, part), f32)
    s, q = loop(size // chunk, piece, (zero, zero))
    store_pair(pay, squash(s), squash(q))
    gate_grads(step, steps, rows, size, me, pre_grad, gate, w_exp, grad_exp, grad_gate, acc)


def run_between(me, owners, layer, part_one, first, back_sums, sums_one, inv, gain, bias, mask, grad_rows, w_in, w_red,
                grad_above, slope, sig, branch, gain_three, bias_three, gate, w_exp):
    rows, size, channels = branch.shape
    steps = channels // part
    devices = sums_one.shape[0]
    reduced = w_exp.shape[1]
    slab = pl.BlockSpec((rows, size, part), lambda k: (0, 0, k))
    pays = pl.BlockSpec((devices, 8, 128), lambda k: (0, k, 0))
    row = pl.BlockSpec((1, part), lambda k: (0, k))
    wide = hbm_shape(branch.shape, bf16)
    return pl.pallas_call(
        functools.partial(between_kernel, rows, size, steps),
        grid=(steps,),
        in_specs=[whole(part_one), whole(first), whole(back_sums), whole(sums_one), whole(inv),
                  whole(gain), whole(bias), whole(mask), whole(grad_rows),
                  pl.BlockSpec((None, part, part), lambda k: (layer, k, 0)),
                  pl.BlockSpec((None, part, reduced), lambda k: (layer, k, 0)),
                  slab, slab, slab, slab, row, row, whole(gate),
                  pl.BlockSpec((None, reduced, part), lambda k: (layer - 1, 0, k)), smem],
        out_specs=(full((rows, size, part)), full((rows, size, reduced)), slab, slab,
                   expand_spec(owners, channels), full(gate.shape), pays),
        out_shape=(shape_of((rows, size, part), bf16), shape_of((rows, size, reduced), bf16), wide, wide,
                   hbm_shape((owners, sum(wide_rows(owners, channels)), part), bf16),
                   shape_of(gate.shape, bf16), shape_of((devices, 8 * steps, 128), f32)),
        scratch_shapes=[pltpu.VMEM((rows, size, part), f32), pltpu.VMEM((rows, size, part), bf16),
                        pltpu.VMEM((rows, size, reduced), f32)],
        compiler_params=params(),
        cost_estimate=cost(2 * rows * size * channels * (part + 512), 20 * MB),
        name="between",
    )(part_one, first, back_sums, sums_one, inv, gain, bias, mask, grad_rows, in_hbm(w_in),
      in_hbm(w_red), in_hbm(grad_above), in_hbm(slope), in_hbm(sig), in_hbm(branch), gain_three,
      bias_three, gate, in_hbm(w_exp), me)


def first_back_kernel(rows, size, part_one, first, back_sums, sums_one, inv, gain, bias, mask, grad_rows,
                      first_out, rows_out):
    first_grad(rows, size, part_one, first, back_sums, sums_one, inv, gain, bias, mask, first_out)
    mask_gate(grad_rows, mask, rows_out, rows, size)


def run_first_back(part_one, first, back_sums, sums_one, inv, gain, bias, mask, grad_rows):
    rows, size = first.shape[:2]
    reduced = grad_rows.shape[3]
    args = (part_one, first, back_sums, sums_one, inv, gain, bias, mask, grad_rows)
    return pl.pallas_call(
        functools.partial(first_back_kernel, rows, size),
        grid=(1,),
        in_specs=[whole(a) for a in args],
        out_specs=(full((rows, size, part)), full((rows, size, reduced))),
        out_shape=(shape_of((rows, size, part), bf16), shape_of((rows, size, reduced), bf16)),
        compiler_params=params(),
        cost_estimate=cost(rows * size * part * 8, 5 * MB),
        name="first_back",
    )(*args)


def input_kernel(rows, size, first_out, rows_out, w_in, w_red, grad_above, mask, out, prod):
    prod[...] = (
        dot_back(first_out[...].reshape(rows * size, part), w_in[...])
        + dot_back(rows_out[...].reshape(rows * size, rows_out.shape[2]), w_red[...])
    ).reshape(rows, size, part)
    frames = chunk // 8

    def piece(i, _):
        for r in range(rows):
            value = grad_above[r, at(i), :].astype(f32) + prod[r, at(i), :] * mask[r, at(i), :]
            out[pl.ds(i * frames, frames), r] = value.reshape(frames, 8, part).astype(bf16)
        return 0

    loop(size // chunk, piece, 0)


def run_input(layer, first_out, rows_out, w_in, w_red, grad_above, mask, frames):
    rows, size, channels = grad_above.shape
    steps = channels // part
    reduced = w_red.shape[2]
    return pl.pallas_call(
        functools.partial(input_kernel, rows, size),
        grid=(steps,),
        in_specs=[whole(first_out), whole(rows_out),
                  pl.BlockSpec((None, part, part), lambda k: (layer, k, 0)),
                  pl.BlockSpec((None, part, reduced), lambda k: (layer, k, 0)),
                  pl.BlockSpec((rows, size, part), lambda k: (0, 0, k)), whole(mask)],
        out_specs=pl.BlockSpec((frames, rows, 8, part), lambda k: (0, 0, 0, k)),
        out_shape=hbm_shape((frames, rows, 8, channels), bf16),
        scratch_shapes=[pltpu.VMEM((rows, size, part), f32)],
        compiler_params=params(),
        cost_estimate=cost(2 * rows * size * channels * 640, 10 * MB),
        name="input",
    )(first_out, rows_out, in_hbm(w_in), in_hbm(w_red), in_hbm(grad_above), mask)


def weight_kernel(rows, size, steps, outside, fixed, me, x, first_out, rows_out, out):
    step = pl.program_id(0)
    for r in range(rows):
        value = x[:, r].reshape(size, part) if outside else x[r]
        turned = value.T
        new, new_red = dot(turned, first_out[r]), dot(turned, rows_out[r])
        total = new if r == 0 else total + new
        total_red = new_red if r == 0 else total_red + new_red
    owners = out.shape[0]
    here = owners // steps
    per = part // here
    quarter = per // 4
    for i in range(steps):

        @pl.when(step == i)
        def _():
            for d in range(here):
                where = place(i * here + d, owners, None if fixed else me)
                out[where, 0:per, :] = total[d * per : (d + 1) * per].astype(bf16)
                piece = total_red[d * per : (d + 1) * per]
                wide = [piece[j * quarter : (j + 1) * quarter] for j in range(4)]
                out[where, per : per + quarter, :] = jnp.concatenate(wide, axis=1).astype(bf16)


def run_weight(me, fixed, owners, x, first_out, rows_out):
    rows, size = first_out.shape[:2]
    channels = x.shape[-1]
    steps = channels // part
    per = channels // owners
    outside = x.ndim == 4
    if outside:
        x_spec = pl.BlockSpec((x.shape[0], rows, 8, part), lambda k: (0, 0, 0, k))
    else:
        x_spec = pl.BlockSpec((rows, size, part), lambda k: (0, 0, k))
    return pl.pallas_call(
        functools.partial(weight_kernel, rows, size, steps, outside, fixed),
        grid=(steps,),
        in_specs=[smem, x_spec, whole(first_out), whole(rows_out)],
        out_specs=full((owners, per + per // 4, part)),
        out_shape=hbm_shape((owners, per + per // 4, part), bf16),
        compiler_params=params(),
        cost_estimate=cost(2 * rows * size * channels * 640, 8 * MB),
        name="weight",
    )(me, in_hbm(x), first_out, rows_out)


def three_shifts(value, step, sign):
    height, size, channels = value.shape
    flat = value.reshape(height * size, channels)
    wide = jnp.concatenate(
        [shift_columns(flat, sign * (j - 1) * step).astype(bf16) for j in range(3)], axis=1
    ).reshape(height, size, 3 * channels)
    blank = jnp.zeros((1, size, 3 * channels), bf16)
    return jnp.concatenate([blank, wide, blank], axis=0)


def small_conv(taps, w):
    height, size = taps.shape[0] - 2, taps.shape[1]
    depth = taps.shape[2]
    total = None
    for i in range(3):
        new = dot(taps[i : i + height].reshape(height * size, depth), w[i * depth : (i + 1) * depth])
        total = new if total is None else total + new
    return total.reshape(height, size, -1)


def small_conv_back(taps, w):
    height, size = taps.shape[0] - 2, taps.shape[1]
    channels = taps.shape[2] // 3
    total = None
    for i in range(3):
        left = taps[2 - i : 2 - i + height].reshape(height * size, 3 * channels)
        for j in range(3):
            tap = (3 * i + j) * channels
            new = dot_back(left[:, j * channels : (j + 1) * channels], w[tap : tap + channels])
            total = new if total is None else total + new
    return total.reshape(height, size, channels)


def small_weight(taps, grad, out, me, which, factor):
    height, size = taps.shape[0] - 2, taps.shape[1]
    depth = taps.shape[2]
    right = grad.reshape(height * size, -1)
    for i in range(3):
        left = taps[i : i + height].reshape(height * size, depth)
        value = (dot_inner(left, right) * factor).astype(bf16)
        for j in range(3):
            block = 9 * which + 3 * i + j
            lane = block % 4 * 128
            put_rows(out.at[:, :, lane : lane + 128], me, block // 4 * 128, out.shape[1],
                     value[j * 128 : (j + 1) * 128])


def add_rows(value):
    height, size, channels = value.shape
    pairs = value.reshape(height // 2, 2, size, channels)
    return pairs[:, 0] + pairs[:, 1]


def add_columns(value, step):
    height, size, channels = value.shape
    flat = value.reshape(height * size, channels)
    count = height * size
    lower = columns(flat.shape) % (2 * step) < step
    moved = jnp.where(lower, pltpu.roll(flat, count - step, 0), pltpu.roll(flat, step, 0))
    return (flat + moved).reshape(height, size, channels)


def spread_rows(value, factor):
    height, size, channels = value.shape
    wide = jnp.broadcast_to(value[:, None], (height, factor, size, channels))
    return wide.reshape(height * factor, size, channels)


def take_frames(dest, source, index):
    height = dest.shape[0]
    for f in range(group):
        dest[:, f] = source[:, index[f]]


def gate_kernel(reduce_ref, index, w, out, coarse_two, coarse_four, plain, moved):
    height, size, channels = reduce_ref.shape
    plain[...] = reduce_ref[...].astype(f32).reshape(height, group, 8, channels)
    take_frames(moved, plain, index)
    diff = small_conv(three_shifts(moved[...].reshape(height, size, channels), 1, 1), w[0])
    diff = diff - plain[...].reshape(height, size, channels)
    sum_two = add_columns(add_rows(diff), 1)
    sum_four = add_columns(add_rows(sum_two), 2)
    two = (sum_two * 0.25).astype(bf16)
    four = (sum_four * 0.0625).astype(bf16)
    coarse_two[...] = two
    coarse_four[...] = four
    conv_two = small_conv(three_shifts(two.astype(f32), 2, 1), w[1])
    conv_four = small_conv(three_shifts(four.astype(f32), 4, 1), w[2])
    out[...] = (diff + spread_rows(conv_two, 2) + spread_rows(conv_four, 4)).astype(bf16)


def run_gate(layer, reduce_full, index, w):
    height, size, channels = reduce_full.shape
    shapes = (
        shape_of((height, size, channels), bf16),
        shape_of((height // 2, size, channels), bf16),
        shape_of((height // 4, size, channels), bf16),
    )
    return pl.pallas_call(
        gate_kernel,
        grid=(1,),
        in_specs=[whole(reduce_full), smem, pl.BlockSpec((None,) + w.shape[1:], lambda k: (layer, 0, 0, 0))],
        out_specs=tuple(full(s.shape) for s in shapes),
        out_shape=shapes,
        scratch_shapes=[pltpu.VMEM((height, group, 8, channels), f32)] * 2,
        compiler_params=params(),
        cost_estimate=cost(2 * height * size * 9 * channels * channels * 2, 2 * MB),
        name="gate",
    )(reduce_full, index, in_hbm(w))


def gate_back_kernel(fixed, me, buffer, grad, reduce_ref, index, w, coarse_two, coarse_four, out, grad_w,
                     plain, moved, total, back):
    height, size, channels = reduce_ref.shape
    me = None if fixed else me
    plain[...] = reduce_ref[...].astype(f32).reshape(height, group, 8, channels)
    take_frames(moved, plain, index)
    g = grad[...].astype(f32)
    sum_two = add_columns(add_rows(g), 1)
    sum_four = add_columns(add_rows(sum_two), 2)
    two = sum_two.astype(bf16)
    four = sum_four.astype(bf16)
    small_weight(three_shifts(coarse_two[...].astype(f32), 2, 1), two, grad_w, me, 1, 0.5)
    small_weight(three_shifts(coarse_four[...].astype(f32), 4, 1), four, grad_w, me, 2, 0.25)
    back_two = small_conv_back(three_shifts(two.astype(f32), 2, -1), w.at[1])
    back_four = small_conv_back(three_shifts(four.astype(f32), 4, -1), w.at[2])
    diff = g + spread_rows(back_two * 0.25, 2) + spread_rows(back_four * 0.0625, 4)
    low = diff.astype(bf16)
    small_weight(three_shifts(moved[...].reshape(height, size, channels), 1, 1), low, grad_w, me, 0, 1.0)
    back[...] = small_conv_back(three_shifts(low.astype(f32), 1, -1), w.at[0]).reshape(
        height, group, 8, channels
    )
    total[...] = -diff.reshape(height, group, 8, channels)
    for f in range(group):
        total[:, index[f]] += back[:, f]
    out[...] = total[...].reshape(height, size, channels).astype(bf16)


def run_gate_back(me, fixed, buffer, layer, grad, reduce_full, index, w, coarse_two, coarse_four):
    height, size, channels = reduce_full.shape
    owners, total = buffer.shape[:2]
    per = gate_conv_rows(owners)
    return pl.pallas_call(
        functools.partial(gate_back_kernel, fixed),
        grid=(1,),
        in_specs=[smem, pl.BlockSpec(memory_space=pl.ANY), whole(grad), whole(reduce_full), smem,
                  pl.BlockSpec((None,) + w.shape[1:], lambda k: (layer, 0, 0, 0)),
                  whole(coarse_two), whole(coarse_four)],
        out_specs=(full((height, size, channels)),
                   pl.BlockSpec((owners, per, part), lambda k: (0, (total - per) // per, 0))),
        out_shape=(shape_of((height, size, channels), bf16), hbm_shape(buffer.shape, bf16)),
        scratch_shapes=[pltpu.VMEM((height, group, 8, channels), f32)] * 4,
        compiler_params=params(),
        cost_estimate=cost(2 * height * size * 9 * channels * channels * 4, 3 * MB),
        input_output_aliases={1: 1},
        name="gate_back",
    )(me, in_hbm(buffer), grad, reduce_full, index, in_hbm(w), coarse_two, coarse_four)


def small_kernel(counts, owners, channels, places, first, second, convs, expand):
    wide, per = counts[2], counts[3]
    for layer, ref in ((0, first), (1, second)):
        for owner in range(owners):
            where = places[layer, owner]
            value = ref[where].astype(f32)
            done = 0
            while done < wide:
                row = owner * wide + done
                length = min(wide - done, 128 - row % 128)
                lane = row // 128 * part
                expand[layer, row % 128 : row % 128 + length, lane : lane + part] = value[done : done + length]
                done += length
            done = 0
            while done < per and owner * per + done < 7 * 128:
                row = owner * per + done
                length = min(per - done, 128 - row % 128)
                for j in range(4):
                    block = row // 128 * 4 + j
                    if block < 27:
                        top = block % 9 * 128 + row % 128
                        convs[layer, block // 9, top : top + length, :] = value[
                            wide + done : wide + done + length, j * 128 : (j + 1) * 128
                        ]
                done += length


def run_small(halves, places, counts, owners, channels):
    shapes = (shape_of((2, 3, 9 * 128, 128), f32), shape_of((2, 128, channels), f32))
    return pl.pallas_call(
        functools.partial(small_kernel, counts, owners, channels),
        grid=(1,),
        in_specs=[smem, whole(halves[0]), whole(halves[1])],
        out_specs=tuple(full(s.shape) for s in shapes),
        out_shape=shapes,
        compiler_params=params(),
        cost_estimate=cost(0, 8 * MB),
        name="small",
    )(places, *halves)


def large_kernel(counts, owners, channels, wide0, wide1, proj0, proj1, proj, conv, out, red):
    for layer, (wide, first) in enumerate(((wide0, proj0), (wide1, proj1))):
        rows = channels // owners
        proj[layer] = first[0:rows, :].astype(f32)
        quarter = rows // 4
        for j in range(4):
            red[layer, j * quarter : (j + 1) * quarter, :] = first[
                rows : rows + quarter, j * 128 : (j + 1) * 128
            ].astype(f32)
        conv[layer] = wide[0 : counts[0], :].astype(f32)
        per = part // owners
        for k in range(channels // part):
            at_row = counts[0] + k * per
            out[layer, :, k * part : (k + 1) * part] = wide[at_row : at_row + per, :].astype(f32)


def run_large(wide, proj, counts, owners, channels):
    rows = channels // owners
    shapes = (
        shape_of((2, rows, part), f32),
        shape_of((2, counts[0], part), f32),
        shape_of((2, part // owners, channels), f32),
        shape_of((2, rows, 128), f32),
    )
    args = (*wide, *proj)
    return pl.pallas_call(
        functools.partial(large_kernel, counts, owners, channels),
        grid=(1,),
        in_specs=[whole(a) for a in args],
        out_specs=tuple(full(s.shape) for s in shapes),
        out_shape=shapes,
        compiler_params=params(),
        cost_estimate=cost(0, 8 * MB),
        name="large",
    )(*args)


def exchange(block):
    return lax.all_to_all(block, both, 0, 0, tiled=True)


def to_frames(own):
    space, rows, size, channels = own.shape
    return lax.all_to_all(own, "space", 0, 0, tiled=True).reshape(space * rows, size, channels)


def to_rows(all_rows, rows):
    height, size, channels = all_rows.shape
    return lax.all_to_all(all_rows.reshape(height // rows, rows, size, channels), "space", 0, 0, tiled=True)


def neighbours(low, high):
    count = lax.axis_size("space")
    from_low = lax.ppermute(high, "space", [(i, i + 1) for i in range(count - 1)])
    from_high = lax.ppermute(low, "space", [(i + 1, i) for i in range(count - 1)])
    return from_low, from_high


def add(left, right):
    return (left.astype(f32) + right.astype(f32)).astype(bf16)


def swap(block, bit):
    count = lax.axis_size("dp")
    return lax.ppermute(block, "dp", [(i, i ^ bit) for i in range(count)])


def core_sum(grad):
    half = grad.shape[0] // 2
    return grad[:half], swap(grad[half:], 1)


def gather_owners(own):
    count = lax.axis_size("dp")
    bits = chip_bits()
    half = len(bits) // 2
    mine = lax.axis_index("dp")
    rows = own.shape[0] // 2
    sequences = (bits + [1], bits[half:] + bits[:half] + [1])
    got = [own[None, which * rows : (which + 1) * rows] for which in range(2)]
    for stage in range(len(sequences[0])):
        got = together(*got)
        new = [swap(g, sequence[stage]) for g, sequence in zip(got, sequences)]
        got = [jnp.concatenate(pair, axis=0) for pair in zip(got, new)]
    places = []
    for sequence in sequences:
        row = []
        for owner in range(count):
            other = jnp.bitwise_xor(mine, owner)
            row.append(sum(jnp.where(other & bit, 1 << i, 0) for i, bit in enumerate(sequence)))
        places.append(jnp.stack(row))
    return got, jnp.stack(places).astype(jnp.int32)


def chip_bits():
    count = lax.axis_size("dp")
    bits = []
    bit = 2
    while bit < count:
        bits.append(bit)
        bit *= 2
    return bits


def reduce_start(kept, got):
    bits = chip_bits()
    rows, cols = kept.shape[1:]
    half = len(bits) // 2
    state = []
    for which, sequence in enumerate((bits, bits[half:] + bits[:half])):
        span = slice(which * (rows // 2), (which + 1) * (rows // 2))
        shape = (2,) * len(bits) + (rows // 2, cols)
        state.append((kept[:, span].reshape(shape), got[:, span].reshape(shape), bits, sequence))
    return reduce_step(state)


def reduce_step(state):
    stays, goes = [], []
    for keep, new, left, sequence in state:
        where = len(left) - 1 - left.index(sequence[0])
        stay, go = [
            add(
                lax.index_in_dim(keep, side, where, keepdims=False),
                lax.index_in_dim(new, side, where, keepdims=False),
            )
            for side in (0, 1)
        ]
        stays.append(stay)
        goes.append(go)
    goes = together(*goes)
    return [
        (stay, swap(go, sequence[0]), [b for b in left if b != sequence[0]], sequence[1:])
        for stay, go, (_, _, left, sequence) in zip(stays, goes, state)
    ]


def reduce_finish(state):
    while state[0][3]:
        state = reduce_step(state)
    return jnp.concatenate([add(keep, new) for keep, new, _, _ in state], axis=0)


def space_scatter(value):
    count = lax.axis_size("space")
    rows, cols = value.shape
    parts = lax.all_to_all(value.reshape(count, rows // count, cols), "space", 0, 0, tiled=True)
    return jnp.sum(parts.astype(f32), axis=0).astype(bf16)


def space_gather(own):
    count = lax.axis_size("space")
    spread = jnp.broadcast_to(own[None], (count,) + own.shape)
    return lax.all_to_all(spread, "space", 0, 0, tiled=True).reshape(-1, own.shape[1])


def space_sum(value):
    return space_gather(space_scatter(value))


def together(*values):
    return lax.optimization_barrier(values)


def body(
    clip_maps,
    next_frame,
    valid_rows,
    proj_in,
    conv_mid,
    proj_out,
    gate_reduce,
    gate_convs,
    gate_expand,
    norm_gain,
    norm_bias,
    out_grad,
):
    frames, rows, cols, channels = clip_maps.shape
    size = frames * cols
    space, here = lax.axis_size("space"), lax.axis_index("space")
    devices = lax.axis_size("dp") * space
    valid = valid_rows.astype(f32)
    mask = jnp.broadcast_to(valid.T[:, :, None], (rows, frames, cols)).reshape(rows, size, 1)
    edge = jnp.stack([(here > 0).astype(jnp.int32), (here < space - 1).astype(jnp.int32)])
    padded = jnp.pad(next_frame, (0, space * group - frames))
    own_next = lax.dynamic_slice_in_dim(padded, here * group, group)
    base = lax.axis_index("dp") * frames + here * group
    index = jnp.clip(own_next - base, 0, group - 1)

    def vectors(layer):
        out = []
        for source in (norm_gain, norm_bias):
            row = source[layer][None]
            out.append((row[:, :part], row[:, part : 2 * part], row[:, 2 * part :]))
        return out

    gains, biases = zip(vectors(0), vectors(1))
    owners = lax.axis_size("dp")
    firsts = [run_first(clip_maps, 0, proj_in, gate_reduce, mask, devices, space), None]
    sums_one, sums_two, sums_three = [None, None], [None, None], [None, None]
    seconds, hidden_twos, gates, reduces = [None, None], [None, None], [None, None], [None, None]
    gate_kept, halos, hidden_ones = [None, None], [None, None], [None, None]
    firsts[0] = list(firsts[0])
    for layer in range(2):
        gain, bias = gains[layer], biases[layer]
        first, red, pay, low, high = firsts[layer]
        sums_one[layer] = exchange(pay)
        if layer == 0:
            inv = 1.0 / jnp.sum(sums_one[0][:, 8:9], axis=0).reshape(1, 128)
        halo = neighbours(low, high)
        reduces[layer] = to_frames(red)
        hidden_own, before = run_conv(
            first, sums_one[layer], inv, gain[0], bias[0], mask, layer, conv_mid
        )
        second, hidden_edge, pay, low, high = run_conv_edge(
            before, *halo, edge, sums_one[layer], inv, gain[0], bias[0], mask, layer, conv_mid
        )
        hidden_ones[layer] = hidden_own, hidden_edge
        seconds[layer] = second
        sums_two[layer] = exchange(pay)
        gate_full, *gate_kept[layer] = run_gate(layer, reduces[layer], index, gate_convs)
        sums_two[layer], gate_full = together(sums_two[layer], gate_full)
        gates[layer] = to_rows(gate_full, rows)
        hidden_twos[layer], pay = run_third(
            second, sums_two[layer], inv, gain[1], bias[1], mask, layer, proj_out
        )
        pay, gates[layer], low, high = together(pay, gates[layer], low, high)
        sums_three[layer] = exchange(pay)
        halos[layer] = neighbours(low, high)
        if layer == 0:
            mid, branch_zero, sig_zero, slope_zero, *firsts[1] = run_mid(
                0, hidden_twos[0], proj_out, sums_three[0], inv, gain[2], bias[2], clip_maps,
                gates[0], gate_expand, mask, proj_in, gate_reduce,
            )
            firsts[1][2], *halos[0] = together(firsts[1][2], *halos[0])
    out_maps, branch_one, grad_branch, grad_in, buffer, grad_gate, pay = run_last(
        owners, 1, hidden_twos[1], proj_out, sums_three[1], inv, gains[1][2], biases[1][2], mid,
        gates[1], gate_expand, mask, out_grad,
    )
    pay, *halos[1] = together(pay, *halos[1])
    branches = [branch_zero, branch_one]
    me = lax.axis_index("dp").astype(jnp.int32)[None]
    results = [None, None]
    vectors_of = [None, None]

    def scatter(grad):
        return lax.psum_scatter(grad, "dp", scatter_dimension=0, tiled=False)

    for layer in (1, 0):
        fixed = layer == 1
        gain, bias = gains[layer], biases[layer]
        first, second = firsts[layer][0], seconds[layer]
        back_three = exchange(pay)
        grad_full = to_frames(grad_gate)
        if layer == 0:
            grad_proj = run_weight(me, True, owners, mid, first_out, rows_out)
            back_three, grad_proj = together(back_three, grad_proj)
            results[1] = results[1] + (scatter(grad_proj),)
        buffer, part_two, pay, low, high = run_third_back(
            me, fixed, buffer, layer, grad_branch, branches[layer], back_three, sums_three[layer], inv,
            gain[2], bias[2], mask, hidden_twos[layer], proj_out, second, sums_two[layer],
            gain[1], bias[1],
        )
        back_two = exchange(pay)
        halo = neighbours(low, high)
        rows_full, buffer = run_gate_back(
            me, fixed, buffer, layer, grad_full, reduces[layer], index, gate_convs, *gate_kept[layer]
        )
        back_two, rows_full = together(back_two, rows_full)
        grad_second, before = run_conv_back(
            part_two, second, back_two, sums_two[layer], gain[1], bias[1], inv, mask, layer, conv_mid
        )
        grad_rows = to_rows(rows_full, rows)
        if layer == 0:
            before, scattered = together(before, results[1][0])
            results[1] = (scattered,) + results[1][1:]
        part_one, pay = run_conv_back_edge(
            before, *halo, *halos[layer], edge, back_two, sums_two[layer], gain[1], bias[1], inv, mask,
            layer, conv_mid, first, sums_one[layer], gain[0], bias[0],
        )
        pay, grad_second, grad_rows = together(pay, grad_second, grad_rows)
        back_one = exchange(pay)
        buffer = run_conv_weight(me, fixed, *hidden_ones[layer], grad_second, buffer)
        if layer == 0:
            back_one, buffer, scattered = together(back_one, buffer, results[1][1])
            results[1] = (results[1][0], scattered)
        else:
            back_one, buffer = together(back_one, buffer)
        common = (part_one, first, back_one, sums_one[layer], inv, gain[0], bias[0], mask, grad_rows)
        if layer == 1:
            results[1] = (scatter(buffer),)
            first_out, rows_out, grad_in, grad_branch, buffer, grad_gate, pay = run_between(
                me, owners, 1, *common, proj_in, gate_reduce, grad_in, slope_zero, sig_zero,
                branch_zero, gains[0][2], biases[0][2], gates[0], gate_expand,
            )
        else:
            wide_sum = core_sum(buffer)
            first_out, rows_out = run_first_back(*common)
            grad_proj = run_weight(me, False, owners, clip_maps, first_out, rows_out)
            earlier = space_scatter(jnp.concatenate(results[1], axis=0))
            wide_state = reduce_start(*wide_sum)
            grad_proj, earlier, *arrived = together(
                grad_proj, earlier, *[half[1] for half in wide_state]
            )
            earlier = space_gather(earlier)
            wide_state = [(half[0], new) + half[2:] for half, new in zip(wide_state, arrived)]
            results[0] = reduce_finish(wide_state), reduce_finish(reduce_start(*core_sum(grad_proj)))
            grad_maps = run_input(0, first_out, rows_out, proj_in, gate_reduce, grad_in, mask, frames)
        vecs = [jnp.sum(back, axis=0) for back in (back_one, back_two, back_three)]

        def pick(which):
            return jnp.concatenate(
                [v.reshape(-1, 2, 4, 128)[:, which].reshape(-1) for v in vecs]
            )

        vectors_of[layer] = pick(1), pick(0)

    counts = wide_rows(owners, channels)
    ends = [sum(counts[: i + 1]) for i in range(4)]
    wide, proj = results[0]
    wide, earlier = together(wide, earlier)
    later = earlier[: wide.shape[0]], earlier[wide.shape[0] :]
    small = space_sum(wide[ends[1] :])
    small, wide, proj, grad_maps = together(small, wide, proj, grad_maps)
    summed = space_sum(jnp.concatenate([wide[: ends[1]], proj], axis=0))
    wide, proj = summed[: ends[1]], summed[ends[1] :]
    halves, places = gather_owners(jnp.concatenate([small, later[0][ends[1] :]], axis=0))
    convs, expand = run_small(halves, places, counts, owners, channels)
    large = run_large([wide, later[0]], [proj, later[1]], counts, owners, channels)
    little = [jnp.stack(pair) for pair in zip(*vectors_of)]
    return (out_maps, grad_maps, *large, convs, expand, *little)


def solution(mesh):
    maps = P("dp", "space", None, None)
    in_specs = (maps, P("dp"), P("dp", "space")) + (P(),) * 8 + (maps,)
    out_specs = (maps, maps) + (P(None, "dp", None),) * 4 + (P(),) * 4
    return jax.shard_map(body, mesh=mesh, in_specs=in_specs, out_specs=out_specs, check_vma=False)
```

```python
import functools

import jax
import jax.numpy as jnp
from jax import lax
from jax.experimental import pallas as pl
from jax.experimental.pallas import tpu as pltpu
from jax.sharding import PartitionSpec as P

norm_eps = 1e-05
both = ("dp", "space")
f32 = jnp.float32
bf16 = jnp.bfloat16
group = 16
part = 512
chunk = 16
absent = -1e30
MB = 1024 * 1024


def dot(left, right):
    return jnp.dot(left, right, preferred_element_type=f32)


def dot_back(left, right):
    return lax.dot_general(left, right, (((1,), (1,)), ((), ())), preferred_element_type=f32)


def dot_inner(left, right):
    return lax.dot_general(left, right, (((0,), (0,)), ((), ())), preferred_element_type=f32)


def sigmoid(value):
    return 0.5 * jnp.tanh(0.5 * value) + 0.5


def silu(value):
    return value * sigmoid(value)


def silu_slope(value):
    sig = sigmoid(value)
    return sig * (1.0 + value * (1.0 - sig))


def lanes(rows):
    return jnp.concatenate([rows[i : i + 1] for i in range(rows.shape[0])], axis=1)


def unlanes(vector):
    return jnp.concatenate(
        [vector[:, 128 * i : 128 * (i + 1)] for i in range(vector.shape[1] // 128)], axis=0
    )


def pair_sum(ref):
    total = jnp.sum(ref[...], axis=0)
    return lanes(total[0:4]), lanes(total[4:8])


def norm_scale(sums, inv_count, gain, bias):
    mean = sums[0] * inv_count
    variance = sums[1] * inv_count - mean * mean
    inverse = lax.rsqrt(variance + norm_eps)
    scale = inverse * gain
    return mean, inverse, scale, bias - mean * scale


def store_pair(ref, first, second):
    rows = jnp.concatenate([unlanes(first), unlanes(second)], axis=0)
    ref[:, 0:8, :] = jnp.broadcast_to(rows[None], (ref.shape[0], 8, 128))


def fold(value):
    return jnp.sum(value.reshape(-1, 8, value.shape[-1]), axis=0)


def squash(value):
    return jnp.sum(value, axis=0, keepdims=True)


def loop(count, body, init):
    return lax.fori_loop(0, count, body, init, unroll=True)


def at(index):
    return pl.ds(pl.multiple_of(index * chunk, chunk), chunk)


def columns(shape):
    return lax.broadcasted_iota(jnp.int32, shape, 0) % 8


def shift_columns(value, step):
    if step == 0:
        return value
    size = value.shape[0]
    col = columns(value.shape)
    moved = pltpu.roll(value, (-step) % size, 0)
    keep = (col + step >= 0) & (col + step < 8)
    return jnp.where(keep, moved, 0.0)


def params():
    return pltpu.CompilerParams(vmem_limit_bytes=60 * MB, dimension_semantics=("arbitrary",))


def whole(array):
    zeros = (0,) * array.ndim
    return pl.BlockSpec(array.shape, lambda *_: zeros)


def full(shape):
    zeros = (0,) * len(shape)
    return pl.BlockSpec(shape, lambda *_: zeros)


def gate_conv_rows(owners):
    return -(-7 * 128 // (owners * 16)) * 16


def wide_rows(owners, channels):
    return 9 * part // owners, channels // owners, channels // 4 // owners, gate_conv_rows(owners)


def shape_of(shape, kind):
    return jax.ShapeDtypeStruct(shape, kind)


def in_hbm(array):
    return pltpu.with_memory_space_constraint(array, pltpu.HBM)


def hbm_shape(shape, kind):
    return pltpu.HBM(shape, kind)


def cost(flops, moved, special=0):
    return pl.CostEstimate(flops=flops // 4, bytes_accessed=moved // 4, transcendentals=special)


def store_halo(low_ref, high_ref, value_of, mask_ref, sums, rows, size):
    mean = (sums * (1.0 / (rows * size))).astype(bf16)
    centre = mean.astype(f32)
    for ref, row in ((low_ref, 0), (high_ref, rows - 1)):

        def piece(i, _, ref=ref, row=row):
            value = value_of(row, i) - centre
            ref[at(i), :] = jnp.where(mask_ref[row, at(i), :] > 0.0, value, absent).astype(bf16)
            return 0

        loop(size // chunk, piece, 0)
        ref[pl.ds(size, 16), :] = jnp.broadcast_to(mean.astype(f32), (16, mean.shape[1])).astype(
            bf16
        )


def store_reduce(ref, acc, mask_ref, rows, size):
    space = ref.shape[0]
    for g in range(space):
        for r in range(rows):
            if g * group * 8 < size:
                lo = g * group * 8
                value = acc[r, lo : lo + group * 8, :].astype(bf16).astype(f32)
                ref[g, r] = (value * mask_ref[r, lo : lo + group * 8, :]).astype(bf16)
            else:
                ref[g, r] = jnp.zeros((group * 8, ref.shape[3]), bf16)


def finish_first(acc, acc_red, mask_ref, first, red, pay, low, high, rows, size):
    def piece(i, carry):
        s, q = carry
        for r in range(rows):
            value = acc[r, at(i), :] * mask_ref[r, at(i), :]
            first[r, at(i), :] = value
            s = s + fold(value)
            q = q + fold(value * value)
        return s, q

    zero = jnp.zeros((8, part), f32)
    s, q = loop(size // chunk, piece, (zero, zero))
    s, q = squash(s), squash(q)
    store_pair(pay, s, q)
    if pay.shape[1] > 8:
        total = mask_ref[0]
        for r in range(1, rows):
            total = total + mask_ref[r]
        total = jnp.broadcast_to(jnp.sum(total, axis=0, keepdims=True), (1, 128))
        pay[:, 8:9, :] = jnp.broadcast_to(total[None], (pay.shape[0], 1, 128))
    store_halo(low, high, lambda r, i: first[r, at(i), :], mask_ref, s, rows, size)
    store_reduce(red, acc_red, mask_ref, rows, size)


def first_kernel(rows, size, steps, x, w, w_red, mask, first, red, pay, low, high, acc, acc_red):
    step = pl.program_id(0)
    for r in range(rows):
        value = x[:, r].reshape(size, part)
        new, new_red = dot(value, w[...]), dot(value, w_red[...])

        @pl.when(step == 0)
        def _():
            acc[r] = new
            acc_red[r] = new_red

        @pl.when(step > 0)
        def _():
            acc[r] += new
            acc_red[r] += new_red

    @pl.when(step == steps - 1)
    def _():
        finish_first(acc, acc_red, mask, first, red, pay, low, high, rows, size)


def first_outputs(rows, size, devices, space, reduced, pay_rows=8):
    shapes = (
        shape_of((rows, size, part), f32),
        shape_of((space, rows, group * 8, reduced), bf16),
        shape_of((devices, pay_rows, 128), f32),
        shape_of((size + 16, part), bf16),
        shape_of((size + 16, part), bf16),
    )
    return shapes, tuple(full(s.shape) for s in shapes)


def run_first(maps, layer, w, w_red, mask, devices, space):
    frames, rows, cols, channels = maps.shape
    size = frames * cols
    steps = channels // part
    reduced = w_red.shape[2]
    shapes, specs = first_outputs(rows, size, devices, space, reduced, 9)
    return pl.pallas_call(
        functools.partial(first_kernel, rows, size, steps),
        grid=(steps,),
        in_specs=[
            pl.BlockSpec((frames, rows, cols, part), lambda k: (0, 0, 0, k)),
            pl.BlockSpec((None, part, part), lambda k: (layer, k, 0)),
            pl.BlockSpec((None, part, reduced), lambda k: (layer, k, 0)),
            whole(mask),
        ],
        out_specs=specs,
        out_shape=shapes,
        scratch_shapes=[pltpu.VMEM((rows, size, part), f32), pltpu.VMEM((rows, size, reduced), f32)],
        compiler_params=params(),
        cost_estimate=cost(2 * rows * size * channels * 640, 8 * MB),
        name="first",
    )(in_hbm(maps), in_hbm(w), in_hbm(w_red), mask)


def conv_kernel(rows, size, first, sums, inv, gain, bias, mask, w, hidden, out, shifted):
    step = pl.program_id(0)

    @pl.when(step == 0)
    def _():
        mean, inverse, scale, offset = norm_scale(
            pair_sum(sums), inv[0:1, 0:1], gain[...], bias[...]
        )

        def own(i, _):
            for r in range(rows):
                value = silu(first[r, at(i), :] * scale + offset) * mask[r, at(i), :]
                hidden[r, at(i), :] = value.astype(bf16)
                for j in range(3):
                    shifted[j, r, at(i), :] = shift_columns(value, j - 1).astype(bf16)
            return 0

        loop(size // chunk, own, 0)

    def taps(lo, hi, source):
        new = None
        for j in range(3):
            left = shifted[j, source : source + hi - lo].reshape((hi - lo) * size, part)
            term = dot(left, w[j * part : (j + 1) * part, :])
            new = term if new is None else new + term
        return new.reshape(hi - lo, size, part)

    own_taps(rows, step, out, taps)


def own_taps(rows, step, out, taps):
    @pl.when(step == 0)
    def _():
        out[...] = taps(0, rows, 0)

    if rows > 1:

        @pl.when(step == 1)
        def _():
            out[1:rows] += taps(1, rows, 0)

        @pl.when(step == 2)
        def _():
            out[0 : rows - 1] += taps(0, rows - 1, 1)


smem = pl.BlockSpec(memory_space=pltpu.SMEM)


def tap_order(step):
    return lax.rem(step + 1, 3)


def run_conv(first, sums, inv, gain, bias, mask, layer, w):
    rows, size = first.shape[:2]
    shapes = (shape_of((rows, size, part), bf16), shape_of((rows, size, part), f32))
    return pl.pallas_call(
        functools.partial(conv_kernel, rows, size),
        grid=(3 if rows > 1 else 1,),
        in_specs=[whole(first), whole(sums), whole(inv), whole(gain), whole(bias), whole(mask),
                  pl.BlockSpec((None, 3 * part, part), lambda i: (layer, jnp.where(i == 0, 1, jnp.where(i == 1, 0, 2)), 0))],
        out_specs=tuple(full(s.shape) for s in shapes),
        out_shape=shapes,
        scratch_shapes=[pltpu.VMEM((3, rows, size, part), bf16)],
        compiler_params=params(),
        cost_estimate=cost(2 * rows * size * 6 * part * part, 8 * MB),
        name="conv",
    )(first, sums, inv, gain, bias, mask, in_hbm(w))


def conv_edge_kernel(rows, size, before, low, high, edge, sums, inv, gain, bias, mask, w,
                     second, hidden, pay, send_low, send_high, shifted):
    step = pl.program_id(0)
    mean, inverse, scale, offset = norm_scale(pair_sum(sums), inv[0:1, 0:1], gain[...], bias[...])

    @pl.when(step == 0)
    def _():
        second[...] = before[...]

    for which, ref, row in ((0, low, 0), (1, high, rows - 1)):

        @pl.when(step == which)
        def _():
            centre = ref[pl.ds(size, 16), :].astype(f32)[0:1]
            here = edge[which] > 0

            def piece(i, _):
                got = ref[at(i), :].astype(f32)
                value = silu((got + centre) * scale + offset)
                value = jnp.where((got > 0.5 * absent) & here, value, 0.0)
                hidden[which, at(i), :] = value.astype(bf16)
                for j in range(3):
                    shifted[j, at(i), :] = shift_columns(value, j - 1).astype(bf16)
                return 0

            loop(size // chunk, piece, 0)
            new = None
            for j in range(3):
                term = dot(shifted[j], w[j * part : (j + 1) * part, :])
                new = term if new is None else new + term
            second[row] += new

    @pl.when(step == 1)
    def _():
        def piece(i, carry):
            s, q = carry
            for r in range(rows):
                value = second[r, at(i), :]
                masked = value * mask[r, at(i), :]
                s = s + fold(masked)
                q = q + fold(masked * value)
            return s, q

        zero = jnp.zeros((8, part), f32)
        s, q = loop(size // chunk, piece, (zero, zero))
        s, q = squash(s), squash(q)
        store_pair(pay, s, q)
        store_halo(send_low, send_high, lambda r, i: second[r, at(i), :], mask, s, rows, size)


def run_conv_edge(before, low, high, edge, sums, inv, gain, bias, mask, layer, w):
    rows, size = before.shape[:2]
    devices = sums.shape[0]
    shapes = (
        shape_of((rows, size, part), f32),
        shape_of((2, size, part), bf16),
        shape_of((devices, 8, 128), f32),
        shape_of((size + 16, part), bf16),
        shape_of((size + 16, part), bf16),
    )
    return pl.pallas_call(
        functools.partial(conv_edge_kernel, rows, size),
        grid=(2,),
        in_specs=[whole(before), whole(low), whole(high), smem, whole(sums), whole(inv), whole(gain),
                  whole(bias), whole(mask),
                  pl.BlockSpec((None, 3 * part, part), lambda i: (layer, 2 * i, 0))],
        out_specs=tuple(full(s.shape) for s in shapes),
        out_shape=shapes,
        scratch_shapes=[pltpu.VMEM((3, size, part), bf16)],
        compiler_params=params(),
        cost_estimate=cost(2 * size * 6 * part * part, 8 * MB),
        name="conv_edge",
    )(before, low, high, edge, sums, inv, gain, bias, mask, in_hbm(w))


def third_kernel(rows, size, second, sums, inv, gain, bias, mask, w, hidden, pay, prod):
    @pl.when(pl.program_id(0) == 0)
    def _():
        mean, inverse, scale, offset = norm_scale(
            pair_sum(sums), inv[0:1, 0:1], gain[...], bias[...]
        )

        def own(i, _):
            for r in range(rows):
                value = silu(second[r, at(i), :] * scale + offset) * mask[r, at(i), :]
                hidden[r, at(i), :] = value.astype(bf16)
            return 0

        loop(size // chunk, own, 0)

    prod[...] = dot(hidden[...].reshape(rows * size, part), w[...])

    def piece(i, carry):
        value = prod[at(i), :]
        return carry[0] + fold(value), carry[1] + fold(value * value)

    zero = jnp.zeros((8, part), f32)
    s, q = loop(rows * size // chunk, piece, (zero, zero))
    store_pair(pay, squash(s), squash(q))


def run_third(second, sums, inv, gain, bias, mask, layer, w):
    rows, size = second.shape[:2]
    devices = sums.shape[0]
    channels = w.shape[2]
    steps = channels // part
    return pl.pallas_call(
        functools.partial(third_kernel, rows, size),
        grid=(steps,),
        in_specs=[whole(second), whole(sums), whole(inv), whole(gain), whole(bias), whole(mask),
                  pl.BlockSpec((None, part, part), lambda k: (layer, 0, k))],
        out_specs=(full((rows, size, part)), pl.BlockSpec((devices, 8, 128), lambda k: (0, k, 0))),
        out_shape=(shape_of((rows, size, part), bf16), shape_of((devices, 8 * steps, 128), f32)),
        scratch_shapes=[pltpu.VMEM((rows * size, part), f32)],
        compiler_params=params(),
        cost_estimate=cost(2 * rows * size * channels * part, 5 * MB),
        name="third",
    )(second, sums, inv, gain, bias, mask, in_hbm(w))


def flat_gate(gate, rows, size):
    pieces = []
    for r in range(rows):
        for g in range(size // (group * 8)):
            pieces.append(gate[g, r])
    return jnp.concatenate(pieces, axis=0)


def mid_kernel(rows, size, steps, hidden, w_out, sums, inv, gain, bias, x, gate, w_exp, mask,
               w_next, red_next,
               out, branch, sig_out, slope, first, red, pay, low, high,
               prod, pre, acc, acc_red):
    step = pl.program_id(0)
    prod[...] = dot(hidden[...].reshape(rows * size, part), w_out[...]).reshape(rows, size, part)
    pre[...] = dot(flat_gate(gate, rows, size), w_exp[...]).reshape(rows, size, part)
    mean, inverse, scale, offset = norm_scale(pair_sum(sums), inv[0:1, 0:1], gain[...], bias[...])
    frames = chunk // 8

    def piece(i, _):
        for r in range(rows):
            b = prod[r, at(i), :] * scale + offset
            sig = sigmoid(pre[r, at(i), :])
            z = x[pl.ds(i * frames, frames), r].astype(f32).reshape(chunk, part) + b * sig
            zs = sigmoid(z)
            m = mask[r, at(i), :]
            zm = zs * m
            y = z * zm
            out[r, at(i), :] = y.astype(bf16)
            slope[r, at(i), :] = (zm + y * (1.0 - zs)).astype(bf16)
            branch[r, at(i), :] = b.astype(bf16)
            sig_out[r, at(i), :] = sig.astype(bf16)
        return 0

    loop(size // chunk, piece, 0)
    value = out[...].reshape(rows * size, part)
    new = dot(value, w_next[...]).reshape(rows, size, part)
    new_red = dot(value, red_next[...]).reshape(rows, size, acc_red.shape[2])

    @pl.when(step == 0)
    def _():
        acc[...] = new
        acc_red[...] = new_red

    @pl.when(step > 0)
    def _():
        acc[...] += new
        acc_red[...] += new_red

    @pl.when(step == steps - 1)
    def _():
        finish_first(acc, acc_red, mask, first, red, pay, low, high, rows, size)


def run_mid(layer, hidden, w_out, sums, inv, gain, bias, maps, gate, w_exp, mask, w_next, red_next):
    frames, rows, cols, channels = maps.shape
    size = frames * cols
    steps = channels // part
    devices, space = sums.shape[0], gate.shape[0]
    reduced = w_exp.shape[1]
    more, more_specs = first_outputs(rows, size, devices, space, reduced)
    wide = hbm_shape((rows, size, channels), bf16)
    slab = pl.BlockSpec((rows, size, part), lambda k: (0, 0, k))
    return pl.pallas_call(
        functools.partial(mid_kernel, rows, size, steps),
        grid=(steps,),
        in_specs=[
            whole(hidden),
            pl.BlockSpec((None, part, part), lambda k: (layer, 0, k)),
            pl.BlockSpec((devices, 8, 128), lambda k: (0, k, 0)),
            whole(inv),
            pl.BlockSpec((1, part), lambda k: (0, k)),
            pl.BlockSpec((1, part), lambda k: (0, k)),
            pl.BlockSpec((frames, rows, cols, part), lambda k: (0, 0, 0, k)),
            whole(gate),
            pl.BlockSpec((None, reduced, part), lambda k: (layer, 0, k)),
            whole(mask),
            pl.BlockSpec((None, part, part), lambda k: (layer + 1, k, 0)),
            pl.BlockSpec((None, part, reduced), lambda k: (layer + 1, k, 0)),
        ],
        out_specs=(slab,) * 4 + more_specs,
        out_shape=(wide,) * 4 + more,
        scratch_shapes=[pltpu.VMEM((rows, size, part), f32)] * 3
        + [pltpu.VMEM((rows, size, reduced), f32)],
        compiler_params=params(),
        cost_estimate=cost(2 * rows * size * channels * (part + part + 256), 20 * MB),
        name="mid",
    )(hidden, in_hbm(w_out), sums, inv, gain, bias, in_hbm(maps), gate, in_hbm(w_exp), mask,
      in_hbm(w_next), in_hbm(red_next))


def place(owner, owners, me):
    if me is None:
        return owner
    other = jnp.bitwise_xor(owner, me[0])
    return lax.rem(other, 2) * (owners // 2) + other // 2


def put_rows(ref, me, begin, per, value):
    done = 0
    while done < value.shape[0]:
        owner, offset = (begin + done) // per, (begin + done) % per
        length = min(value.shape[0] - done, per - offset)
        ref[place(owner, ref.shape[0], me), offset : offset + length, :] = value[done : done + length]
        done += length


def gate_grads(step, steps, rows, size, me, pre_grad, gate, w_exp, grad_exp, grad_gate, acc):
    left = flat_gate(gate, rows, size)
    right = pre_grad[...].reshape(rows * size, part)
    value = dot_inner(left, right).astype(bf16)
    owners, per = grad_exp.shape[:2]
    for i in range(steps):

        @pl.when(step == i)
        def _():
            put_rows(grad_exp, me, i * value.shape[0], per, value)

    new = dot_back(right, w_exp[...]).reshape(rows, size, acc.shape[2])

    @pl.when(step == 0)
    def _():
        acc[...] = new

    @pl.when(step > 0)
    def _():
        acc[...] += new

    @pl.when(step == steps - 1)
    def _():
        for g in range(grad_gate.shape[0]):
            for r in range(rows):
                lo = g * group * 8
                if lo < size:
                    grad_gate[g, r] = acc[r, lo : lo + group * 8, :].astype(bf16)
                else:
                    grad_gate[g, r] = jnp.zeros((group * 8, acc.shape[2]), bf16)


def last_kernel(rows, size, steps, hidden, w_out, sums, inv, gain, bias, x, gate, w_exp, mask,
                grad_out,
                out, branch, grad_branch, grad_in, grad_exp, grad_gate, pay,
                prod, pre, pre_grad, acc):
    step = pl.program_id(0)
    prod[...] = dot(hidden[...].reshape(rows * size, part), w_out[...]).reshape(rows, size, part)
    pre[...] = dot(flat_gate(gate, rows, size), w_exp[...]).reshape(rows, size, part)
    mean, inverse, scale, offset = norm_scale(pair_sum(sums), inv[0:1, 0:1], gain[...], bias[...])
    frames = chunk // 8

    def piece(i, carry):
        s, q = carry
        for r in range(rows):
            n = (prod[r, at(i), :] - mean) * inverse
            b = n * gain[...] + bias[...]
            sig = sigmoid(pre[r, at(i), :])
            z = x[r, at(i), :].astype(f32) + b * sig
            zs = sigmoid(z)
            m = mask[r, at(i), :]
            zm = zs * m
            y = z * zm
            out[pl.ds(i * frames, frames), r] = y.reshape(frames, 8, part).astype(bf16)
            dz = grad_out[pl.ds(i * frames, frames), r].astype(f32).reshape(chunk, part)
            dz = dz * (zm + y * (1.0 - zs))
            db = dz * sig
            s = s + fold(db)
            q = q + fold(db * n)
            branch[r, at(i), :] = b.astype(bf16)
            grad_branch[r, at(i), :] = db.astype(bf16)
            grad_in[r, at(i), :] = dz.astype(bf16)
            pre_grad[r, at(i), :] = (db * b * (1.0 - sig)).astype(bf16)
        return s, q

    zero = jnp.zeros((8, part), f32)
    s, q = loop(size // chunk, piece, (zero, zero))
    store_pair(pay, squash(s), squash(q))
    gate_grads(step, steps, rows, size, None, pre_grad, gate, w_exp, grad_exp, grad_gate, acc)


def expand_spec(owners, channels):
    rows = wide_rows(owners, channels)
    return pl.BlockSpec((owners, rows[2], part), lambda *_: (0, (rows[0] + rows[1]) // rows[2], 0))


def run_last(owners, layer, hidden, w_out, sums, inv, gain, bias, maps, gate, w_exp, mask, grad_out):
    frames, rows, cols, channels = grad_out.shape
    size = frames * cols
    steps = channels // part
    devices, space = sums.shape[0], gate.shape[0]
    reduced = w_exp.shape[1]
    wide = hbm_shape((rows, size, channels), bf16)
    slab = pl.BlockSpec((rows, size, part), lambda k: (0, 0, k))
    outside = pl.BlockSpec((frames, rows, cols, part), lambda k: (0, 0, 0, k))
    pays = pl.BlockSpec((devices, 8, 128), lambda k: (0, k, 0))
    row = pl.BlockSpec((1, part), lambda k: (0, k))
    return pl.pallas_call(
        functools.partial(last_kernel, rows, size, steps),
        grid=(steps,),
        in_specs=[
            whole(hidden), pl.BlockSpec((None, part, part), lambda k: (layer, 0, k)), pays, whole(inv),
            row, row, slab, whole(gate), pl.BlockSpec((None, reduced, part), lambda k: (layer, 0, k)),
            whole(mask), outside,
        ],
        out_specs=(outside, slab, slab, slab, expand_spec(owners, channels), full(gate.shape), pays),
        out_shape=(hbm_shape(grad_out.shape, bf16), wide, wide, wide,
                   hbm_shape((owners, sum(wide_rows(owners, channels)), part), bf16),
                   shape_of(gate.shape, bf16), shape_of(sums.shape, f32)),
        scratch_shapes=[pltpu.VMEM((rows, size, part), f32)] * 2
        + [pltpu.VMEM((rows, size, part), bf16), pltpu.VMEM((rows, size, reduced), f32)],
        compiler_params=params(),
        cost_estimate=cost(2 * rows * size * channels * (part + 512), 20 * MB),
        name="last",
    )(hidden, in_hbm(w_out), sums, inv, gain, bias, in_hbm(maps), gate, in_hbm(w_exp), mask,
      in_hbm(grad_out))


def third_back_kernel(rows, size, steps, fixed, me, buffer, grad_branch, branch, back_sums, sums, inv, gain, bias, mask,
                      hidden, w_out, second, sums_two, gain_two, bias_two,
                      grad_w, part_two, pay, low, high, third_grad, hidden_t, acc):
    step = pl.program_id(0)

    @pl.when(step == 0)
    def _():
        hidden_t[...] = hidden[...].reshape(rows * size, part).T

    inv_count = inv[0:1, 0:1]
    mean, inverse, scale, offset = norm_scale(pair_sum(sums), inv_count, gain[...], bias[...])
    sum_bias, sum_gain = pair_sum(back_sums)
    inv_gain = 1.0 / gain[...]
    slope = -scale * inv_count * sum_gain * inv_gain
    const = -scale * inv_count * sum_bias - slope * bias[...]

    def piece(i, _):
        for r in range(rows):
            db = grad_branch[r, at(i), :].astype(f32)
            b = branch[r, at(i), :].astype(f32)
            value = scale * db + mask[r, at(i), :] * (const + slope * b)
            third_grad[r, at(i), :] = value.astype(bf16)
        return 0

    loop(size // chunk, piece, 0)
    right = third_grad[...].reshape(rows * size, part)
    new = dot_back(right, w_out[...]).reshape(rows, size, part)

    @pl.when(step == 0)
    def _():
        acc[...] = new

    @pl.when(step > 0)
    def _():
        acc[...] += new

    put_rows(grad_w, None if fixed else me, 0, grad_w.shape[1], dot(hidden_t[...], right).astype(bf16))

    @pl.when(step == steps - 1)
    def _():
        finish_back(rows, size, acc, second, sums_two, inv, gain_two, bias_two, mask,
                    part_two, pay, low, high)


def finish_back(rows, size, acc, value_ref, sums, inv, gain, bias, mask, part_ref, pay, low, high):
    mean, inverse, scale, offset = norm_scale(pair_sum(sums), inv[0:1, 0:1], gain[...], bias[...])

    def piece(i, carry):
        s, q = carry
        for r in range(rows):
            n = (value_ref[r, at(i), :] - mean) * inverse
            grad = acc[r, at(i), :] * silu_slope(n * gain[...] + bias[...]) * mask[r, at(i), :]
            s = s + fold(grad)
            q = q + fold(grad * n)
            part_ref[r, at(i), :] = grad * scale
        return s, q

    zero = jnp.zeros((8, part), f32)
    s, q = loop(size // chunk, piece, (zero, zero))
    s, q = squash(s), squash(q)
    store_pair(pay, s, q)
    if low is not None:
        store_halo(low, high, lambda r, i: part_ref[r, at(i), :], mask, s * scale, rows, size)


def run_third_back(me, fixed, buffer, layer, grad_branch, branch, back_sums, sums, inv, gain, bias, mask,
                   hidden, w_out, second, sums_two, gain_two, bias_two):
    rows, size, channels = branch.shape
    steps = channels // part
    devices = sums.shape[0]
    owners = buffer.shape[0]
    slab = pl.BlockSpec((rows, size, part), lambda k: (0, 0, k))
    pays = pl.BlockSpec((devices, 8, 128), lambda k: (0, k, 0))
    row = pl.BlockSpec((1, part), lambda k: (0, k))
    return pl.pallas_call(
        functools.partial(third_back_kernel, rows, size, steps, fixed),
        grid=(steps,),
        in_specs=[smem, pl.BlockSpec(memory_space=pl.ANY), slab, slab, pays, pays, whole(inv), row, row, whole(mask), whole(hidden),
                  pl.BlockSpec((None, part, part), lambda k: (layer, 0, k)), whole(second), whole(sums_two),
                  whole(gain_two), whole(bias_two)],
        out_specs=(pl.BlockSpec((owners, part // owners, part), lambda k: (0, 9 + k, 0)),
                   full((rows, size, part)),
                   full((devices, 8, 128)), full((size + 16, part)), full((size + 16, part))),
        out_shape=(hbm_shape(buffer.shape, bf16), shape_of((rows, size, part), f32),
                   shape_of((devices, 8, 128), f32), shape_of((size + 16, part), bf16),
                   shape_of((size + 16, part), bf16)),
        scratch_shapes=[pltpu.VMEM((rows, size, part), bf16), pltpu.VMEM((part, rows * size), bf16),
                        pltpu.VMEM((rows, size, part), f32)],
        compiler_params=params(),
        cost_estimate=cost(4 * rows * size * channels * part, 12 * MB),
        input_output_aliases={1: 0},
        name="third_back",
    )(me, in_hbm(buffer), in_hbm(grad_branch), in_hbm(branch), back_sums, sums, inv, gain, bias, mask, hidden,
      in_hbm(w_out), second, sums_two, gain_two, bias_two)


def conv_back_kernel(rows, size, part_two, second, back_sums, sums_two, gain_two, bias_two, inv, mask,
                     w, grad_second, out, shifted):
    step = pl.program_id(0)

    @pl.when(step == 0)
    def _():
        inv_count = inv[0:1, 0:1]
        mean, inverse, scale, offset = norm_scale(
            pair_sum(sums_two), inv_count, gain_two[...], bias_two[...]
        )
        sum_bias, sum_gain = pair_sum(back_sums)
        slope = -scale * inv_count * sum_gain * inverse
        const = -scale * inv_count * sum_bias

        def own(i, _):
            for r in range(rows):
                centred = second[r, at(i), :] - mean
                value = part_two[r, at(i), :] + mask[r, at(i), :] * (const + slope * centred)
                grad_second[r, at(i), :] = value.astype(bf16)
                for j in range(3):
                    shifted[j, r, at(i), :] = shift_columns(value, 1 - j).astype(bf16)
            return 0

        loop(size // chunk, own, 0)

    def taps(lo, hi, source):
        new = None
        for j in range(3):
            left = shifted[j, source : source + hi - lo].reshape((hi - lo) * size, part)
            term = dot_back(left, w[j * part : (j + 1) * part, :])
            new = term if new is None else new + term
        return new.reshape(hi - lo, size, part)

    own_taps(rows, step, out, taps)


def run_conv_back(part_two, second, back_sums, sums_two, gain_two, bias_two, inv, mask, layer, w):
    rows, size = second.shape[:2]
    args = (part_two, second, back_sums, sums_two, gain_two, bias_two, inv, mask)
    shapes = (shape_of((rows, size, part), bf16), shape_of((rows, size, part), f32))
    return pl.pallas_call(
        functools.partial(conv_back_kernel, rows, size),
        grid=(3 if rows > 1 else 1,),
        in_specs=[whole(a) for a in args]
        + [pl.BlockSpec((None, 3 * part, part), lambda i: (layer, jnp.where(i == 0, 1, jnp.where(i == 1, 2, 0)), 0))],
        out_specs=tuple(full(s.shape) for s in shapes),
        out_shape=shapes,
        scratch_shapes=[pltpu.VMEM((3, rows, size, part), bf16)],
        compiler_params=params(),
        cost_estimate=cost(2 * rows * size * 6 * part * part, 8 * MB),
        name="conv_back",
    )(*args, in_hbm(w))


def conv_back_edge_kernel(rows, size, before, part_low, part_high, second_low, second_high, edge,
                          back_sums, sums_two, gain_two, bias_two, inv, mask, w,
                          first, sums_one, gain_one, bias_one, part_one, pay, shifted, acc):
    step = pl.program_id(0)
    inv_count = inv[0:1, 0:1]
    mean, inverse, scale, offset = norm_scale(
        pair_sum(sums_two), inv_count, gain_two[...], bias_two[...]
    )
    sum_bias, sum_gain = pair_sum(back_sums)
    slope = -scale * inv_count * sum_gain * inverse
    const = -scale * inv_count * sum_bias

    @pl.when(step == 0)
    def _():
        acc[...] = before[...]

    for which, ref, val, row, side in (
        (0, part_high, second_high, rows - 1, 1), (1, part_low, second_low, 0, 0)
    ):

        @pl.when(step == which)
        def _():
            middle = val[pl.ds(size, 16), :].astype(f32)[0:1] - mean
            base = ref[pl.ds(size, 16), :].astype(f32)[0:1] + const + slope * middle
            here = edge[side] > 0

            def piece(i, _):
                got = ref[at(i), :].astype(f32)
                value = got + base + slope * val[at(i), :].astype(f32)
                value = jnp.where((got > 0.5 * absent) & here, value, 0.0)
                for j in range(3):
                    shifted[j, at(i), :] = shift_columns(value, 1 - j).astype(bf16)
                return 0

            loop(size // chunk, piece, 0)
            new = None
            for j in range(3):
                term = dot_back(shifted[j], w[j * part : (j + 1) * part, :])
                new = term if new is None else new + term
            acc[row] += new

    @pl.when(step == 1)
    def _():
        finish_back(rows, size, acc, first, sums_one, inv, gain_one, bias_one, mask,
                    part_one, pay, None, None)


def run_conv_back_edge(before, part_low, part_high, second_low, second_high, edge, back_sums, sums_two,
                       gain_two, bias_two, inv, mask, layer, w, first, sums_one, gain_one, bias_one):
    rows, size = before.shape[:2]
    devices = sums_two.shape[0]
    args = (before, part_low, part_high, second_low, second_high, edge, back_sums, sums_two,
            gain_two, bias_two, inv, mask, w, first, sums_one, gain_one, bias_one)
    specs = [None if a is w else whole(a) for a in args]
    specs[5] = smem
    specs[12] = pl.BlockSpec((None, 3 * part, part), lambda i: (layer, 2 * i, 0))
    shapes = (shape_of((rows, size, part), f32), shape_of((devices, 8, 128), f32))
    return pl.pallas_call(
        functools.partial(conv_back_edge_kernel, rows, size),
        grid=(2,),
        in_specs=specs,
        out_specs=tuple(full(s.shape) for s in shapes),
        out_shape=shapes,
        scratch_shapes=[pltpu.VMEM((3, size, part), bf16), pltpu.VMEM((rows, size, part), f32)],
        compiler_params=params(),
        cost_estimate=cost(2 * size * 6 * part * part, 8 * MB),
        name="conv_back_edge",
    )(*[in_hbm(a) if a is w else a for a in args])


def conv_weight_kernel(rows, size, fixed, me, hidden, hidden_edge, grad_second, buffer, out, hidden_t, shifted):
    step = pl.program_id(0)
    owners, per = out.shape[:2]

    @pl.when(step == 0)
    def _():
        hidden_t[:, 0:size] = hidden_edge[0].T
        for r in range(rows):
            hidden_t[:, (r + 1) * size : (r + 2) * size] = hidden[r].T
        hidden_t[:, (rows + 1) * size : (rows + 2) * size] = hidden_edge[1].T

        def piece(i, _):
            for r in range(rows):
                value = grad_second[r, at(i), :].astype(f32)
                for j in range(3):
                    shifted[j, r, at(i), :] = shift_columns(value, 1 - j).astype(bf16)
            return 0

        loop(size // chunk, piece, 0)

    for i in range(3):

        @pl.when(step == i)
        def _():
            left = hidden_t[:, i * size : (i + rows) * size]
            for j in range(3):
                right = shifted[j].reshape(rows * size, part)
                value = dot(left, right).astype(bf16)
                put_rows(out, None if fixed else me, (3 * i + j) * part, per, value)


def run_conv_weight(me, fixed, hidden, hidden_edge, grad_second, buffer):
    rows, size = grad_second.shape[:2]
    owners = buffer.shape[0]
    return pl.pallas_call(
        functools.partial(conv_weight_kernel, rows, size, fixed),
        grid=(3,),
        in_specs=[smem, whole(hidden), whole(hidden_edge), whole(grad_second),
                  pl.BlockSpec(memory_space=pl.ANY)],
        out_specs=full((owners, 9 * part // owners, part)),
        out_shape=hbm_shape(buffer.shape, bf16),
        scratch_shapes=[pltpu.VMEM((part, (rows + 2) * size), bf16), pltpu.VMEM((3, rows, size, part), bf16)],
        input_output_aliases={4: 0},
        compiler_params=params(),
        cost_estimate=cost(2 * rows * size * 9 * part * part, 8 * MB),
        name="conv_weight",
    )(me, hidden, hidden_edge, grad_second, in_hbm(buffer))


def first_grad(rows, size, part_one, first, back_sums, sums_one, inv, gain, bias, mask, out):
    inv_count = inv[0:1, 0:1]
    mean, inverse, scale, offset = norm_scale(pair_sum(sums_one), inv_count, gain[...], bias[...])
    sum_bias, sum_gain = pair_sum(back_sums)
    slope = -scale * inv_count * sum_gain * inverse
    const = -scale * inv_count * sum_bias

    def own(i, _):
        for r in range(rows):
            centred = first[r, at(i), :] - mean
            value = part_one[r, at(i), :] + mask[r, at(i), :] * (const + slope * centred)
            out[r, at(i), :] = value.astype(bf16)
        return 0

    loop(size // chunk, own, 0)


def mask_gate(grad_rows, mask, out, rows, size):
    for r in range(rows):
        for g in range(size // (group * 8)):
            lo = g * group * 8
            value = grad_rows[g, r].astype(f32) * mask[r, lo : lo + group * 8, :]
            out[r, lo : lo + group * 8, :] = value.astype(bf16)


def between_kernel(rows, size, steps, part_one, first, back_sums, sums_one, inv, gain, bias, mask,
                   grad_rows, w_in, w_red, grad_above, slope, sig, branch, gain_three, bias_three,
                   gate, w_exp, me,
                   first_out, rows_out, grad_in, grad_branch, grad_exp, grad_gate, pay,
                   prod, pre_grad, acc):
    step = pl.program_id(0)

    @pl.when(step == 0)
    def _():
        first_grad(rows, size, part_one, first, back_sums, sums_one, inv, gain, bias, mask, first_out)
        mask_gate(grad_rows, mask, rows_out, rows, size)

    prod[...] = (
        dot_back(first_out[...].reshape(rows * size, part), w_in[...])
        + dot_back(rows_out[...].reshape(rows * size, rows_out.shape[2]), w_red[...])
    ).reshape(rows, size, part)
    inv_gain = 1.0 / gain_three[...]
    offset = bias_three[...] * inv_gain

    def piece(i, carry):
        s, q = carry
        for r in range(rows):
            dy = grad_above[r, at(i), :].astype(f32) + prod[r, at(i), :]
            dz = dy * slope[r, at(i), :].astype(f32)
            sg = sig[r, at(i), :].astype(f32)
            b = branch[r, at(i), :].astype(f32)
            db = dz * sg
            s = s + fold(db)
            q = q + fold(db * (b * inv_gain - offset))
            grad_branch[r, at(i), :] = db.astype(bf16)
            grad_in[r, at(i), :] = dz.astype(bf16)
            pre_grad[r, at(i), :] = (db * b * (1.0 - sg)).astype(bf16)
        return s, q

    zero = jnp.zeros((8, part), f32)
    s, q = loop(size // chunk, piece, (zero, zero))
    store_pair(pay, squash(s), squash(q))
    gate_grads(step, steps, rows, size, me, pre_grad, gate, w_exp, grad_exp, grad_gate, acc)


def run_between(me, owners, layer, part_one, first, back_sums, sums_one, inv, gain, bias, mask, grad_rows, w_in, w_red,
                grad_above, slope, sig, branch, gain_three, bias_three, gate, w_exp):
    rows, size, channels = branch.shape
    steps = channels // part
    devices = sums_one.shape[0]
    reduced = w_exp.shape[1]
    slab = pl.BlockSpec((rows, size, part), lambda k: (0, 0, k))
    pays = pl.BlockSpec((devices, 8, 128), lambda k: (0, k, 0))
    row = pl.BlockSpec((1, part), lambda k: (0, k))
    wide = hbm_shape(branch.shape, bf16)
    return pl.pallas_call(
        functools.partial(between_kernel, rows, size, steps),
        grid=(steps,),
        in_specs=[whole(part_one), whole(first), whole(back_sums), whole(sums_one), whole(inv),
                  whole(gain), whole(bias), whole(mask), whole(grad_rows),
                  pl.BlockSpec((None, part, part), lambda k: (layer, k, 0)),
                  pl.BlockSpec((None, part, reduced), lambda k: (layer, k, 0)),
                  slab, slab, slab, slab, row, row, whole(gate),
                  pl.BlockSpec((None, reduced, part), lambda k: (layer - 1, 0, k)), smem],
        out_specs=(full((rows, size, part)), full((rows, size, reduced)), slab, slab,
                   expand_spec(owners, channels), full(gate.shape), pays),
        out_shape=(shape_of((rows, size, part), bf16), shape_of((rows, size, reduced), bf16), wide, wide,
                   hbm_shape((owners, sum(wide_rows(owners, channels)), part), bf16),
                   shape_of(gate.shape, bf16), shape_of((devices, 8 * steps, 128), f32)),
        scratch_shapes=[pltpu.VMEM((rows, size, part), f32), pltpu.VMEM((rows, size, part), bf16),
                        pltpu.VMEM((rows, size, reduced), f32)],
        compiler_params=params(),
        cost_estimate=cost(2 * rows * size * channels * (part + 512), 20 * MB),
        name="between",
    )(part_one, first, back_sums, sums_one, inv, gain, bias, mask, grad_rows, in_hbm(w_in),
      in_hbm(w_red), in_hbm(grad_above), in_hbm(slope), in_hbm(sig), in_hbm(branch), gain_three,
      bias_three, gate, in_hbm(w_exp), me)


def first_back_kernel(rows, size, part_one, first, back_sums, sums_one, inv, gain, bias, mask, grad_rows,
                      first_out, rows_out):
    first_grad(rows, size, part_one, first, back_sums, sums_one, inv, gain, bias, mask, first_out)
    mask_gate(grad_rows, mask, rows_out, rows, size)


def run_first_back(part_one, first, back_sums, sums_one, inv, gain, bias, mask, grad_rows):
    rows, size = first.shape[:2]
    reduced = grad_rows.shape[3]
    args = (part_one, first, back_sums, sums_one, inv, gain, bias, mask, grad_rows)
    return pl.pallas_call(
        functools.partial(first_back_kernel, rows, size),
        grid=(1,),
        in_specs=[whole(a) for a in args],
        out_specs=(full((rows, size, part)), full((rows, size, reduced))),
        out_shape=(shape_of((rows, size, part), bf16), shape_of((rows, size, reduced), bf16)),
        compiler_params=params(),
        cost_estimate=cost(rows * size * part * 8, 5 * MB),
        name="first_back",
    )(*args)


def input_kernel(rows, size, first_out, rows_out, w_in, w_red, grad_above, mask, out, prod):
    prod[...] = (
        dot_back(first_out[...].reshape(rows * size, part), w_in[...])
        + dot_back(rows_out[...].reshape(rows * size, rows_out.shape[2]), w_red[...])
    ).reshape(rows, size, part)
    frames = chunk // 8

    def piece(i, _):
        for r in range(rows):
            value = grad_above[r, at(i), :].astype(f32) + prod[r, at(i), :] * mask[r, at(i), :]
            out[pl.ds(i * frames, frames), r] = value.reshape(frames, 8, part).astype(bf16)
        return 0

    loop(size // chunk, piece, 0)


def run_input(layer, first_out, rows_out, w_in, w_red, grad_above, mask, frames):
    rows, size, channels = grad_above.shape
    steps = channels // part
    reduced = w_red.shape[2]
    return pl.pallas_call(
        functools.partial(input_kernel, rows, size),
        grid=(steps,),
        in_specs=[whole(first_out), whole(rows_out),
                  pl.BlockSpec((None, part, part), lambda k: (layer, k, 0)),
                  pl.BlockSpec((None, part, reduced), lambda k: (layer, k, 0)),
                  pl.BlockSpec((rows, size, part), lambda k: (0, 0, k)), whole(mask)],
        out_specs=pl.BlockSpec((frames, rows, 8, part), lambda k: (0, 0, 0, k)),
        out_shape=hbm_shape((frames, rows, 8, channels), bf16),
        scratch_shapes=[pltpu.VMEM((rows, size, part), f32)],
        compiler_params=params(),
        cost_estimate=cost(2 * rows * size * channels * 640, 10 * MB),
        name="input",
    )(first_out, rows_out, in_hbm(w_in), in_hbm(w_red), in_hbm(grad_above), mask)


def weight_kernel(rows, size, steps, outside, fixed, me, x, first_out, rows_out, out):
    step = pl.program_id(0)
    for r in range(rows):
        value = x[:, r].reshape(size, part) if outside else x[r]
        turned = value.T
        new, new_red = dot(turned, first_out[r]), dot(turned, rows_out[r])
        total = new if r == 0 else total + new
        total_red = new_red if r == 0 else total_red + new_red
    owners = out.shape[0]
    here = owners // steps
    per = part // here
    quarter = per // 4
    for i in range(steps):

        @pl.when(step == i)
        def _():
            for d in range(here):
                where = place(i * here + d, owners, None if fixed else me)
                out[where, 0:per, :] = total[d * per : (d + 1) * per].astype(bf16)
                piece = total_red[d * per : (d + 1) * per]
                wide = [piece[j * quarter : (j + 1) * quarter] for j in range(4)]
                out[where, per : per + quarter, :] = jnp.concatenate(wide, axis=1).astype(bf16)


def run_weight(me, fixed, owners, x, first_out, rows_out):
    rows, size = first_out.shape[:2]
    channels = x.shape[-1]
    steps = channels // part
    per = channels // owners
    outside = x.ndim == 4
    if outside:
        x_spec = pl.BlockSpec((x.shape[0], rows, 8, part), lambda k: (0, 0, 0, k))
    else:
        x_spec = pl.BlockSpec((rows, size, part), lambda k: (0, 0, k))
    return pl.pallas_call(
        functools.partial(weight_kernel, rows, size, steps, outside, fixed),
        grid=(steps,),
        in_specs=[smem, x_spec, whole(first_out), whole(rows_out)],
        out_specs=full((owners, per + per // 4, part)),
        out_shape=hbm_shape((owners, per + per // 4, part), bf16),
        compiler_params=params(),
        cost_estimate=cost(2 * rows * size * channels * 640, 8 * MB),
        name="weight",
    )(me, in_hbm(x), first_out, rows_out)


def three_shifts(value, step, sign):
    height, size, channels = value.shape
    flat = value.reshape(height * size, channels)
    wide = jnp.concatenate(
        [shift_columns(flat, sign * (j - 1) * step).astype(bf16) for j in range(3)], axis=1
    ).reshape(height, size, 3 * channels)
    blank = jnp.zeros((1, size, 3 * channels), bf16)
    return jnp.concatenate([blank, wide, blank], axis=0)


def small_conv(taps, w):
    height, size = taps.shape[0] - 2, taps.shape[1]
    depth = taps.shape[2]
    total = None
    for i in range(3):
        new = dot(taps[i : i + height].reshape(height * size, depth), w[i * depth : (i + 1) * depth])
        total = new if total is None else total + new
    return total.reshape(height, size, -1)


def small_conv_back(taps, w):
    height, size = taps.shape[0] - 2, taps.shape[1]
    channels = taps.shape[2] // 3
    total = None
    for i in range(3):
        left = taps[2 - i : 2 - i + height].reshape(height * size, 3 * channels)
        for j in range(3):
            tap = (3 * i + j) * channels
            new = dot_back(left[:, j * channels : (j + 1) * channels], w[tap : tap + channels])
            total = new if total is None else total + new
    return total.reshape(height, size, channels)


def small_weight(taps, grad, out, me, which, factor):
    height, size = taps.shape[0] - 2, taps.shape[1]
    depth = taps.shape[2]
    right = grad.reshape(height * size, -1)
    for i in range(3):
        left = taps[i : i + height].reshape(height * size, depth)
        value = (dot_inner(left, right) * factor).astype(bf16)
        for j in range(3):
            block = 9 * which + 3 * i + j
            lane = block % 4 * 128
            put_rows(out.at[:, :, lane : lane + 128], me, block // 4 * 128, out.shape[1],
                     value[j * 128 : (j + 1) * 128])


def add_rows(value):
    height, size, channels = value.shape
    pairs = value.reshape(height // 2, 2, size, channels)
    return pairs[:, 0] + pairs[:, 1]


def add_columns(value, step):
    height, size, channels = value.shape
    flat = value.reshape(height * size, channels)
    count = height * size
    lower = columns(flat.shape) % (2 * step) < step
    moved = jnp.where(lower, pltpu.roll(flat, count - step, 0), pltpu.roll(flat, step, 0))
    return (flat + moved).reshape(height, size, channels)


def spread_rows(value, factor):
    height, size, channels = value.shape
    wide = jnp.broadcast_to(value[:, None], (height, factor, size, channels))
    return wide.reshape(height * factor, size, channels)


def take_frames(dest, source, index):
    height = dest.shape[0]
    for f in range(group):
        dest[:, f] = source[:, index[f]]


def gate_kernel(reduce_ref, index, w, out, coarse_two, coarse_four, plain, moved):
    height, size, channels = reduce_ref.shape
    plain[...] = reduce_ref[...].astype(f32).reshape(height, group, 8, channels)
    take_frames(moved, plain, index)
    diff = small_conv(three_shifts(moved[...].reshape(height, size, channels), 1, 1), w[0])
    diff = diff - plain[...].reshape(height, size, channels)
    sum_two = add_columns(add_rows(diff), 1)
    sum_four = add_columns(add_rows(sum_two), 2)
    two = (sum_two * 0.25).astype(bf16)
    four = (sum_four * 0.0625).astype(bf16)
    coarse_two[...] = two
    coarse_four[...] = four
    conv_two = small_conv(three_shifts(two.astype(f32), 2, 1), w[1])
    conv_four = small_conv(three_shifts(four.astype(f32), 4, 1), w[2])
    out[...] = (diff + spread_rows(conv_two, 2) + spread_rows(conv_four, 4)).astype(bf16)


def run_gate(layer, reduce_full, index, w):
    height, size, channels = reduce_full.shape
    shapes = (
        shape_of((height, size, channels), bf16),
        shape_of((height // 2, size, channels), bf16),
        shape_of((height // 4, size, channels), bf16),
    )
    return pl.pallas_call(
        gate_kernel,
        grid=(1,),
        in_specs=[whole(reduce_full), smem, pl.BlockSpec((None,) + w.shape[1:], lambda k: (layer, 0, 0, 0))],
        out_specs=tuple(full(s.shape) for s in shapes),
        out_shape=shapes,
        scratch_shapes=[pltpu.VMEM((height, group, 8, channels), f32)] * 2,
        compiler_params=params(),
        cost_estimate=cost(2 * height * size * 9 * channels * channels * 2, 2 * MB),
        name="gate",
    )(reduce_full, index, in_hbm(w))


def gate_back_kernel(fixed, me, buffer, grad, reduce_ref, index, w, coarse_two, coarse_four, out, grad_w,
                     plain, moved, total, back):
    height, size, channels = reduce_ref.shape
    me = None if fixed else me
    plain[...] = reduce_ref[...].astype(f32).reshape(height, group, 8, channels)
    take_frames(moved, plain, index)
    g = grad[...].astype(f32)
    sum_two = add_columns(add_rows(g), 1)
    sum_four = add_columns(add_rows(sum_two), 2)
    two = sum_two.astype(bf16)
    four = sum_four.astype(bf16)
    small_weight(three_shifts(coarse_two[...].astype(f32), 2, 1), two, grad_w, me, 1, 0.5)
    small_weight(three_shifts(coarse_four[...].astype(f32), 4, 1), four, grad_w, me, 2, 0.25)
    back_two = small_conv_back(three_shifts(two.astype(f32), 2, -1), w.at[1])
    back_four = small_conv_back(three_shifts(four.astype(f32), 4, -1), w.at[2])
    diff = g + spread_rows(back_two * 0.25, 2) + spread_rows(back_four * 0.0625, 4)
    low = diff.astype(bf16)
    small_weight(three_shifts(moved[...].reshape(height, size, channels), 1, 1), low, grad_w, me, 0, 1.0)
    back[...] = small_conv_back(three_shifts(low.astype(f32), 1, -1), w.at[0]).reshape(
        height, group, 8, channels
    )
    total[...] = -diff.reshape(height, group, 8, channels)
    for f in range(group):
        total[:, index[f]] += back[:, f]
    out[...] = total[...].reshape(height, size, channels).astype(bf16)


def run_gate_back(me, fixed, buffer, layer, grad, reduce_full, index, w, coarse_two, coarse_four):
    height, size, channels = reduce_full.shape
    owners, total = buffer.shape[:2]
    per = gate_conv_rows(owners)
    return pl.pallas_call(
        functools.partial(gate_back_kernel, fixed),
        grid=(1,),
        in_specs=[smem, pl.BlockSpec(memory_space=pl.ANY), whole(grad), whole(reduce_full), smem,
                  pl.BlockSpec((None,) + w.shape[1:], lambda k: (layer, 0, 0, 0)),
                  whole(coarse_two), whole(coarse_four)],
        out_specs=(full((height, size, channels)),
                   pl.BlockSpec((owners, per, part), lambda k: (0, (total - per) // per, 0))),
        out_shape=(shape_of((height, size, channels), bf16), hbm_shape(buffer.shape, bf16)),
        scratch_shapes=[pltpu.VMEM((height, group, 8, channels), f32)] * 4,
        compiler_params=params(),
        cost_estimate=cost(2 * height * size * 9 * channels * channels * 4, 3 * MB),
        input_output_aliases={1: 1},
        name="gate_back",
    )(me, in_hbm(buffer), grad, reduce_full, index, in_hbm(w), coarse_two, coarse_four)


def small_kernel(counts, owners, channels, places, first, second, convs, expand):
    wide, per = counts[2], counts[3]
    for layer, ref in ((0, first), (1, second)):
        for owner in range(owners):
            where = places[layer, owner]
            value = ref[where].astype(f32)
            done = 0
            while done < wide:
                row = owner * wide + done
                length = min(wide - done, 128 - row % 128)
                lane = row // 128 * part
                expand[layer, row % 128 : row % 128 + length, lane : lane + part] = value[done : done + length]
                done += length
            done = 0
            while done < per and owner * per + done < 7 * 128:
                row = owner * per + done
                length = min(per - done, 128 - row % 128)
                for j in range(4):
                    block = row // 128 * 4 + j
                    if block < 27:
                        top = block % 9 * 128 + row % 128
                        convs[layer, block // 9, top : top + length, :] = value[
                            wide + done : wide + done + length, j * 128 : (j + 1) * 128
                        ]
                done += length


def run_small(halves, places, counts, owners, channels):
    shapes = (shape_of((2, 3, 9 * 128, 128), f32), shape_of((2, 128, channels), f32))
    return pl.pallas_call(
        functools.partial(small_kernel, counts, owners, channels),
        grid=(1,),
        in_specs=[smem, whole(halves[0]), whole(halves[1])],
        out_specs=tuple(full(s.shape) for s in shapes),
        out_shape=shapes,
        compiler_params=params(),
        cost_estimate=cost(0, 8 * MB),
        name="small",
    )(places, *halves)


def large_kernel(counts, owners, channels, wide0, wide1, proj0, proj1, proj, conv, out, red):
    for layer, (wide, first) in enumerate(((wide0, proj0), (wide1, proj1))):
        rows = channels // owners
        proj[layer] = first[0:rows, :].astype(f32)
        quarter = rows // 4
        for j in range(4):
            red[layer, j * quarter : (j + 1) * quarter, :] = first[
                rows : rows + quarter, j * 128 : (j + 1) * 128
            ].astype(f32)
        conv[layer] = wide[0 : counts[0], :].astype(f32)
        per = part // owners
        for k in range(channels // part):
            at_row = counts[0] + k * per
            out[layer, :, k * part : (k + 1) * part] = wide[at_row : at_row + per, :].astype(f32)


def run_large(wide, proj, counts, owners, channels):
    rows = channels // owners
    shapes = (
        shape_of((2, rows, part), f32),
        shape_of((2, counts[0], part), f32),
        shape_of((2, part // owners, channels), f32),
        shape_of((2, rows, 128), f32),
    )
    args = (*wide, *proj)
    return pl.pallas_call(
        functools.partial(large_kernel, counts, owners, channels),
        grid=(1,),
        in_specs=[whole(a) for a in args],
        out_specs=tuple(full(s.shape) for s in shapes),
        out_shape=shapes,
        compiler_params=params(),
        cost_estimate=cost(0, 8 * MB),
        name="large",
    )(*args)


def exchange(block):
    return lax.all_to_all(block, both, 0, 0, tiled=True)


def to_frames(own):
    space, rows, size, channels = own.shape
    return lax.all_to_all(own, "space", 0, 0, tiled=True).reshape(space * rows, size, channels)


def to_rows(all_rows, rows):
    height, size, channels = all_rows.shape
    return lax.all_to_all(all_rows.reshape(height // rows, rows, size, channels), "space", 0, 0, tiled=True)


def neighbours(low, high):
    count = lax.axis_size("space")
    from_low = lax.ppermute(high, "space", [(i, i + 1) for i in range(count - 1)])
    from_high = lax.ppermute(low, "space", [(i + 1, i) for i in range(count - 1)])
    return from_low, from_high


def add(left, right):
    return (left.astype(f32) + right.astype(f32)).astype(bf16)


def swap(block, bit):
    count = lax.axis_size("dp")
    return lax.ppermute(block, "dp", [(i, i ^ bit) for i in range(count)])


def core_sum(grad):
    half = grad.shape[0] // 2
    return grad[:half], swap(grad[half:], 1)


def gather_owners(own):
    count = lax.axis_size("dp")
    bits = chip_bits()
    half = len(bits) // 2
    mine = lax.axis_index("dp")
    rows = own.shape[0] // 2
    sequences = (bits + [1], bits[half:] + bits[:half] + [1])
    got = [own[None, which * rows : (which + 1) * rows] for which in range(2)]
    for stage in range(len(sequences[0])):
        got = together(*got)
        new = [swap(g, sequence[stage]) for g, sequence in zip(got, sequences)]
        got = [jnp.concatenate(pair, axis=0) for pair in zip(got, new)]
    places = []
    for sequence in sequences:
        row = []
        for owner in range(count):
            other = jnp.bitwise_xor(mine, owner)
            row.append(sum(jnp.where(other & bit, 1 << i, 0) for i, bit in enumerate(sequence)))
        places.append(jnp.stack(row))
    return got, jnp.stack(places).astype(jnp.int32)


def chip_bits():
    count = lax.axis_size("dp")
    bits = []
    bit = 2
    while bit < count:
        bits.append(bit)
        bit *= 2
    return bits


def reduce_start(kept, got):
    bits = chip_bits()
    rows, cols = kept.shape[1:]
    half = len(bits) // 2
    state = []
    for which, sequence in enumerate((bits, bits[half:] + bits[:half])):
        span = slice(which * (rows // 2), (which + 1) * (rows // 2))
        shape = (2,) * len(bits) + (rows // 2, cols)
        state.append((kept[:, span].reshape(shape), got[:, span].reshape(shape), bits, sequence))
    return reduce_step(state)


def reduce_step(state):
    stays, goes = [], []
    for keep, new, left, sequence in state:
        where = len(left) - 1 - left.index(sequence[0])
        stay, go = [
            add(
                lax.index_in_dim(keep, side, where, keepdims=False),
                lax.index_in_dim(new, side, where, keepdims=False),
            )
            for side in (0, 1)
        ]
        stays.append(stay)
        goes.append(go)
    goes = together(*goes)
    return [
        (stay, swap(go, sequence[0]), [b for b in left if b != sequence[0]], sequence[1:])
        for stay, go, (_, _, left, sequence) in zip(stays, goes, state)
    ]


def reduce_finish(state):
    while state[0][3]:
        state = reduce_step(state)
    return jnp.concatenate([add(keep, new) for keep, new, _, _ in state], axis=0)


def space_scatter(value):
    count = lax.axis_size("space")
    rows, cols = value.shape
    parts = lax.all_to_all(value.reshape(count, rows // count, cols), "space", 0, 0, tiled=True)
    return jnp.sum(parts.astype(f32), axis=0).astype(bf16)


def space_gather(own):
    count = lax.axis_size("space")
    spread = jnp.broadcast_to(own[None], (count,) + own.shape)
    return lax.all_to_all(spread, "space", 0, 0, tiled=True).reshape(-1, own.shape[1])


def space_sum(value):
    return space_gather(space_scatter(value))


def together(*values):
    return lax.optimization_barrier(values)


def body(
    clip_maps,
    next_frame,
    valid_rows,
    proj_in,
    conv_mid,
    proj_out,
    gate_reduce,
    gate_convs,
    gate_expand,
    norm_gain,
    norm_bias,
    out_grad,
):
    frames, rows, cols, channels = clip_maps.shape
    size = frames * cols
    space, here = lax.axis_size("space"), lax.axis_index("space")
    devices = lax.axis_size("dp") * space
    valid = valid_rows.astype(f32)
    mask = jnp.broadcast_to(valid.T[:, :, None], (rows, frames, cols)).reshape(rows, size, 1)
    edge = jnp.stack([(here > 0).astype(jnp.int32), (here < space - 1).astype(jnp.int32)])
    padded = jnp.pad(next_frame, (0, space * group - frames))
    own_next = lax.dynamic_slice_in_dim(padded, here * group, group)
    base = lax.axis_index("dp") * frames + here * group
    index = jnp.clip(own_next - base, 0, group - 1)

    def vectors(layer):
        out = []
        for source in (norm_gain, norm_bias):
            row = source[layer][None]
            out.append((row[:, :part], row[:, part : 2 * part], row[:, 2 * part :]))
        return out

    gains, biases = zip(vectors(0), vectors(1))
    owners = lax.axis_size("dp")
    firsts = [run_first(clip_maps, 0, proj_in, gate_reduce, mask, devices, space), None]
    sums_one, sums_two, sums_three = [None, None], [None, None], [None, None]
    seconds, hidden_twos, gates, reduces = [None, None], [None, None], [None, None], [None, None]
    gate_kept, halos, hidden_ones = [None, None], [None, None], [None, None]
    firsts[0] = list(firsts[0])
    for layer in range(2):
        gain, bias = gains[layer], biases[layer]
        first, red, pay, low, high = firsts[layer]
        sums_one[layer] = exchange(pay)
        if layer == 0:
            inv = 1.0 / jnp.sum(sums_one[0][:, 8:9], axis=0).reshape(1, 128)
        halo = neighbours(low, high)
        reduces[layer] = to_frames(red)
        hidden_own, before = run_conv(
            first, sums_one[layer], inv, gain[0], bias[0], mask, layer, conv_mid
        )
        second, hidden_edge, pay, low, high = run_conv_edge(
            before, *halo, edge, sums_one[layer], inv, gain[0], bias[0], mask, layer, conv_mid
        )
        hidden_ones[layer] = hidden_own, hidden_edge
        seconds[layer] = second
        sums_two[layer] = exchange(pay)
        gate_full, *gate_kept[layer] = run_gate(layer, reduces[layer], index, gate_convs)
        sums_two[layer], gate_full = together(sums_two[layer], gate_full)
        gates[layer] = to_rows(gate_full, rows)
        hidden_twos[layer], pay = run_third(
            second, sums_two[layer], inv, gain[1], bias[1], mask, layer, proj_out
        )
        pay, gates[layer], low, high = together(pay, gates[layer], low, high)
        sums_three[layer] = exchange(pay)
        halos[layer] = neighbours(low, high)
        if layer == 0:
            mid, branch_zero, sig_zero, slope_zero, *firsts[1] = run_mid(
                0, hidden_twos[0], proj_out, sums_three[0], inv, gain[2], bias[2], clip_maps,
                gates[0], gate_expand, mask, proj_in, gate_reduce,
            )
            firsts[1][2], *halos[0] = together(firsts[1][2], *halos[0])
    out_maps, branch_one, grad_branch, grad_in, buffer, grad_gate, pay = run_last(
        owners, 1, hidden_twos[1], proj_out, sums_three[1], inv, gains[1][2], biases[1][2], mid,
        gates[1], gate_expand, mask, out_grad,
    )
    pay, *halos[1] = together(pay, *halos[1])
    branches = [branch_zero, branch_one]
    me = lax.axis_index("dp").astype(jnp.int32)[None]
    results = [None, None]
    vectors_of = [None, None]

    def scatter(grad):
        return lax.psum_scatter(grad, "dp", scatter_dimension=0, tiled=False)

    for layer in (1, 0):
        fixed = layer == 1
        gain, bias = gains[layer], biases[layer]
        first, second = firsts[layer][0], seconds[layer]
        back_three = exchange(pay)
        grad_full = to_frames(grad_gate)
        if layer == 0:
            grad_proj = run_weight(me, True, owners, mid, first_out, rows_out)
            back_three, grad_proj = together(back_three, grad_proj)
            results[1] = results[1] + (scatter(grad_proj),)
        buffer, part_two, pay, low, high = run_third_back(
            me, fixed, buffer, layer, grad_branch, branches[layer], back_three, sums_three[layer], inv,
            gain[2], bias[2], mask, hidden_twos[layer], proj_out, second, sums_two[layer],
            gain[1], bias[1],
        )
        back_two = exchange(pay)
        halo = neighbours(low, high)
        rows_full, buffer = run_gate_back(
            me, fixed, buffer, layer, grad_full, reduces[layer], index, gate_convs, *gate_kept[layer]
        )
        back_two, rows_full = together(back_two, rows_full)
        grad_second, before = run_conv_back(
            part_two, second, back_two, sums_two[layer], gain[1], bias[1], inv, mask, layer, conv_mid
        )
        grad_rows = to_rows(rows_full, rows)
        if layer == 0:
            before, scattered = together(before, results[1][0])
            results[1] = (scattered,) + results[1][1:]
        part_one, pay = run_conv_back_edge(
            before, *halo, *halos[layer], edge, back_two, sums_two[layer], gain[1], bias[1], inv, mask,
            layer, conv_mid, first, sums_one[layer], gain[0], bias[0],
        )
        pay, grad_second, grad_rows = together(pay, grad_second, grad_rows)
        back_one = exchange(pay)
        buffer = run_conv_weight(me, fixed, *hidden_ones[layer], grad_second, buffer)
        if layer == 0:
            back_one, buffer, scattered = together(back_one, buffer, results[1][1])
            results[1] = (results[1][0], scattered)
        else:
            back_one, buffer = together(back_one, buffer)
        common = (part_one, first, back_one, sums_one[layer], inv, gain[0], bias[0], mask, grad_rows)
        if layer == 1:
            results[1] = (scatter(buffer),)
            first_out, rows_out, grad_in, grad_branch, buffer, grad_gate, pay = run_between(
                me, owners, 1, *common, proj_in, gate_reduce, grad_in, slope_zero, sig_zero,
                branch_zero, gains[0][2], biases[0][2], gates[0], gate_expand,
            )
        else:
            wide_sum = core_sum(buffer)
            first_out, rows_out = run_first_back(*common)
            grad_proj = run_weight(me, False, owners, clip_maps, first_out, rows_out)
            earlier = space_scatter(jnp.concatenate(results[1], axis=0))
            wide_state = reduce_start(*wide_sum)
            grad_proj, earlier, *arrived = together(
                grad_proj, earlier, *[half[1] for half in wide_state]
            )
            earlier = space_gather(earlier)
            wide_state = [(half[0], new) + half[2:] for half, new in zip(wide_state, arrived)]
            results[0] = reduce_finish(wide_state), reduce_finish(reduce_start(*core_sum(grad_proj)))
            grad_maps = run_input(0, first_out, rows_out, proj_in, gate_reduce, grad_in, mask, frames)
        vecs = [jnp.sum(back, axis=0) for back in (back_one, back_two, back_three)]

        def pick(which):
            return jnp.concatenate(
                [v.reshape(-1, 2, 4, 128)[:, which].reshape(-1) for v in vecs]
            )

        vectors_of[layer] = pick(1), pick(0)

    counts = wide_rows(owners, channels)
    ends = [sum(counts[: i + 1]) for i in range(4)]
    wide, proj = results[0]
    wide, earlier = together(wide, earlier)
    later = earlier[: wide.shape[0]], earlier[wide.shape[0] :]
    small = space_sum(wide[ends[1] :])
    small, wide, proj, grad_maps = together(small, wide, proj, grad_maps)
    summed = space_sum(jnp.concatenate([wide[: ends[1]], proj], axis=0))
    wide, proj = summed[: ends[1]], summed[ends[1] :]
    halves, places = gather_owners(jnp.concatenate([small, later[0][ends[1] :]], axis=0))
    convs, expand = run_small(halves, places, counts, owners, channels)
    large = run_large([wide, later[0]], [proj, later[1]], counts, owners, channels)
    little = [jnp.stack(pair) for pair in zip(*vectors_of)]
    return (out_maps, grad_maps, *large, convs, expand, *little)


def solution(mesh):
    maps = P("dp", "space", None, None)
    in_specs = (maps, P("dp"), P("dp", "space")) + (P(),) * 8 + (maps,)
    out_specs = (maps, maps) + (P(None, "dp", None),) * 4 + (P(),) * 4
    return jax.shard_map(body, mesh=mesh, in_specs=in_specs, out_specs=out_specs, check_vma=False)
```
